32 devices in a mesh: section: 2 (over core), dp: 16 (over z, y, x).
Axes of the slice: x: 2, y: 2, z: 4, core: 2. Of those that a mesh axis runs over, the one named last changes fastest.
Arguments:
- node_input: bfloat16 [2, 2048, 128], P(None, 'dp'), may hold values from -6 to 6
- edge_input: bfloat16 [2, 16, 10240], P(None, None, 'dp'), may hold values from -6 to 6
- edge_source: int32 [2, 10240], P(None, 'dp'), may hold values from 0 to 127, as said below
- edge_target: int32 [2, 10240], P(None, 'dp'), may hold values from 0 to 127, as said below
- edge_valid: int32 [2, 10240], P(None, 'dp'), may hold values 0 or 1
- node_labeled: int32 [2, 2048], P(None, 'dp'), may hold values from 0 to 1, as said below
- edge_w1: bfloat16 [16, 128], replicated, may hold values from -1.5 to 1.5
- edge_b1: bfloat16 [128], replicated, may hold values from -3 to 3
- edge_w2: bfloat16 [128, 16384], replicated, may hold values from -0.046875 to 0.046875
- edge_b2: bfloat16 [16384], replicated, may hold values from -0.29882812 to 0.29882812
- gru_wi: bfloat16 [128, 384], replicated, may hold values from -0.5 to 0.5
- gru_bi: bfloat16 [384], replicated, may hold values from -3 to 3
- gru_wh: bfloat16 [128, 384], replicated, may hold values from -0.5 to 0.5
- gru_bh: bfloat16 [384], replicated, may hold values from -3 to 3
- state_cot: float32 [2, 2048, 128], P(None, 'dp'), may hold values from -6 to 6
Outputs:
- states: float32 [2, 2, 2048, 128], P('section', None, 'dp')
- state_grads: float32 [2, 2, 2048, 128], P('section', None, 'dp')
- grad_edge_w1: float32 [16, 128], replicated
- grad_edge_b1: float32 [128], replicated
- grad_edge_w2: float32 [128, 16384], replicated
- grad_edge_b2: float32 [16384], replicated
- grad_gru_wi: float32 [128, 384], replicated
- grad_gru_bi: float32 [384], replicated
- grad_gru_wh: float32 [128, 384], replicated
- grad_gru_bh: float32 [384], replicated
The draws below stay inside these ranges and needn't reach their ends.
Inputs may be any that keep to these rules, and one draw needn't show every extreme that they name: `edge_source`: an edge's source and destination lie in the same aligned group of 16 node slots; slot k * (80) onward of a device's edges belong to group k. `edge_target`: same groups as edge_source. `node_labeled`: node 0 of every device's micro-batch is labeled.
All inputs are finite; a program needn't handle non-finite values. No bound on the sum of `edge_valid` on one device may be relied on, other than what follows from the above.
Results may differ from the reference program's by a relative error of at most 0.009.
The reference program's roundings to bfloat16 on the way count: a program that leaves them out, or rounds other values in their place, can miss the bound.
Values may be sent and summed in bfloat16 or wider, within the bound.
A program may use at most 128 MiB of HBM per device.

```python
import jax
import jax.numpy as jnp
from jax import lax

H = 128
EDGE_IN = 16
EDGE_HID = 128
MOL_NODES = 16
EDGE_BLOCK = 128
MICRO = 2
NODE_MB = 128
EDGE_MB = 640
NODES = 2048
EDGES = 10240
N_DP = 16


def edge_ends(key):
    cols = jnp.arange(MICRO * EDGES, dtype=jnp.int32).reshape(MICRO, EDGES) % EDGE_MB
    groups = NODE_MB // MOL_NODES
    base = cols // (EDGE_MB // groups) * MOL_NODES
    first = base + jax.random.randint(jax.random.fold_in(key, 11), (MICRO, EDGES), 0, MOL_NODES)
    second = base + jax.random.randint(jax.random.fold_in(key, 12), (MICRO, EDGES), 0, MOL_NODES)
    return (first.astype(jnp.int32), second.astype(jnp.int32))


def draw_edge_source(key, part):
    ends = edge_ends(key)
    return ends[0]


def draw_edge_target(key, part):
    ends = edge_ends(key)
    return ends[1]


def draw_node_labeled(key, part):
    key = jax.random.fold_in(key, 3)
    index = jnp.arange(MICRO * NODES, dtype=jnp.int32).reshape(MICRO, NODES) % NODES
    limit = 250 + 500 * index // NODES
    rolls = jax.random.randint(key, (MICRO, NODES), 0, 1000)
    labeled = (rolls < limit) | (index % NODE_MB == 0)
    return labeled.astype(jnp.int32)


def place_ends(values, key, low, top_value):
    longest = values.shape.index(max(values.shape))
    spots = []
    for shift in (0, 1):
        where = [jax.random.randint(jax.random.fold_in(key, axis), (), 0, length) for axis, length in enumerate(values.shape)]
        where[longest] = (where[longest] + shift) % values.shape[longest]
        spots.append(tuple(where))
    return values.at[spots[0]].set(low).at[spots[1]].set(top_value)


def level_of(stream_key, extent, shards, smallest, high):
    factor_of = 1.0
    for position, shards_of in shards:
        draws = jax.random.uniform(jax.random.fold_in(jax.random.fold_in(stream_key, 6), position), (shards_of,), jnp.float32, smallest / len(shards), high / len(shards))
        factor_of = factor_of * jnp.repeat(jnp.exp(draws), extent[position] // shards_of).reshape((-1,) + (1,) * (len(extent) - 1 - position))
    return factor_of


def normal_values(own_key, shape, spread, most, shards=(), held_as=jnp.bfloat16):
    result = jax.random.normal(own_key, shape, jnp.float32) * spread
    if len(shards) > 0:
        result = level_of(own_key, shape, shards, -0.22, 0.18) * result
    return jnp.clip(result, min=-most, max=most).astype(held_as)


def setup_inputs(seed: int = 0) -> dict:
    key_of = jax.random.split(jax.random.key(seed), 16)
    return {
        "node_input": normal_values(key_of[0], (MICRO, NODES, H), 1.0, 6.0, ((1, 16),)),
        "edge_input": normal_values(key_of[1], (MICRO, EDGE_IN, EDGES), 1.0, 6.0, ((2, 16),)),
        "edge_source": draw_edge_source(jax.random.fold_in(key_of[15], 71), 0),
        "edge_target": draw_edge_target(jax.random.fold_in(key_of[15], 71), 0),
        "edge_valid": place_ends((jax.random.randint(key_of[4], (MICRO, EDGES), 0, 6) < 5).astype(jnp.int32), jax.random.fold_in(key_of[4], 1), 0, 1),
        "node_labeled": draw_node_labeled(jax.random.fold_in(key_of[15], 71), 0),
        "edge_w1": normal_values(key_of[6], (EDGE_IN, EDGE_HID), EDGE_IN ** -0.5, 1.5),
        "edge_b1": normal_values(key_of[7], (EDGE_HID,), 0.5, 3.0),
        "edge_w2": normal_values(key_of[8], (EDGE_HID, H * H), (EDGE_HID * H) ** -0.5, 0.046875),
        "edge_b2": normal_values(key_of[9], (H * H,), 0.05, 0.29882812),
        "gru_wi": normal_values(key_of[10], (H, 3 * H), H ** -0.5, 0.5),
        "gru_bi": normal_values(key_of[11], (3 * H,), 0.5, 3.0),
        "gru_wh": normal_values(key_of[12], (H, 3 * H), H ** -0.5, 0.5),
        "gru_bh": normal_values(key_of[13], (3 * H,), 0.5, 3.0),
        "state_cot": normal_values(key_of[14], (MICRO, NODES, H), 1.0, 6.0, ((1, 16),), jnp.float32),
    }


@jax.custom_vjp
def low(v):
    return lax.optimization_barrier(v.astype(jnp.bfloat16)).astype(jnp.float32)

@jax.custom_vjp
def low_back(v):
    return v

def low_keep(v):
    return (low(v), None)

def low_pass(kept, grad):
    return (grad,)

def back_keep(v):
    return (v, None)

def back_low(kept, grad):
    return (low(grad),)
low.defvjp(low_keep, low_pass)
low_back.defvjp(back_keep, back_low)
HI = lax.Precision.HIGHEST

def edge_block(params, state, feats, source, target, valid):
    w1, b1, w2, b2 = (params[0], params[1], params[2], params[3])
    zpre = low_back(jnp.dot(feats.T, w1, precision=HI) + b1)
    z_low = low(jax.nn.silu(zpre))
    amat = low_back(low(jnp.dot(z_low, w2, precision=HI) + b2)).reshape(EDGE_BLOCK, H, H)
    node_ids = jnp.arange(NODE_MB, dtype=jnp.int32)
    pick = (source[:, None] == node_ids[None, :]).astype(jnp.float32)
    h_source = jnp.dot(pick, state, precision=HI)
    message = jnp.einsum('eij,ej->ei', amat, h_source, precision=HI)
    put = ((target[:, None] == node_ids[None, :]) & (valid[:, None] > 0)).astype(jnp.float32)
    return jnp.dot(put.T, message, precision=HI)

def message_step(params, state, feats, source, target, valid):
    count = EDGE_MB // EDGE_BLOCK
    feat_blocks = feats.reshape(EDGE_IN, count, EDGE_BLOCK).transpose(1, 0, 2)
    blocked = jax.checkpoint(edge_block)

    def add(total, pieces):
        return (total + blocked(params, state, pieces[0], pieces[1], pieces[2], pieces[3]), None)
    summed, _ = lax.scan(add, jnp.zeros((NODE_MB, H), jnp.float32), (feat_blocks, source.reshape(count, EDGE_BLOCK), target.reshape(count, EDGE_BLOCK), valid.reshape(count, EDGE_BLOCK)))
    gathered = low_back(low(summed))
    wi, bi, wh, bh = (params[4], params[5], params[6], params[7])
    gate_in = low_back(jnp.dot(gathered, wi, precision=HI) + bi)
    gate_state = low_back(jnp.dot(state, wh, precision=HI) + bh)
    reset = jax.nn.sigmoid(gate_in[:, :H] + gate_state[:, :H])
    update = jax.nn.sigmoid(gate_in[:, H:2 * H] + gate_state[:, H:2 * H])
    candidate = jnp.tanh(gate_in[:, 2 * H:] + reset * gate_state[:, 2 * H:])
    return (1.0 - update) * candidate + update * state

def forward(params, node_in, probe, feats, source, target, valid, coeff):

    def piece(loss, items):
        x_piece, p_piece, f_piece, s_piece, t_piece, v_piece, c_piece = items
        first = message_step(params, x_piece, f_piece, s_piece, t_piece, v_piece)
        kept = low(first)
        second_in = low_back(kept + p_piece)
        second = message_step(params, second_in, f_piece, s_piece, t_piece, v_piece)
        return (loss + jnp.sum(c_piece * second), (kept, second))
    loss, outs = lax.scan(piece, jnp.float32(0.0), (node_in, probe, feats, source, target, valid, coeff))
    return (loss, outs[0], outs[1])

def reference(node_input, edge_input, edge_source, edge_target, edge_valid, node_labeled, edge_w1, edge_b1, edge_w2, edge_b2, gru_wi, gru_bi, gru_wh, gru_bh, state_cot):
    pieces = MICRO * N_DP
    node_in = node_input.astype(jnp.float32).reshape(pieces, NODE_MB, H)
    feats = edge_input.astype(jnp.float32).reshape(MICRO, EDGE_IN, N_DP, EDGE_MB).transpose(0, 2, 1, 3).reshape(pieces, EDGE_IN, EDGE_MB)
    source = edge_source.reshape(pieces, EDGE_MB)
    target = edge_target.reshape(pieces, EDGE_MB)
    valid = edge_valid.reshape(pieces, EDGE_MB)
    labels = node_labeled.astype(jnp.float32)
    coeff = (state_cot * labels[:, :, None]).reshape(pieces, NODE_MB, H)
    params = tuple((w.astype(jnp.float32) for w in (edge_w1, edge_b1, edge_w2, edge_b2, gru_wi, gru_bi, gru_wh, gru_bh)))
    probe = jnp.zeros((pieces, NODE_MB, H), jnp.float32)

    def run(p, x, q):
        return forward(p, x, q, feats, source, target, valid, coeff)
    (loss, first, second), pullback = jax.vjp(run, params, node_in, probe)
    grads, node_grad, probe_grad = pullback((jnp.float32(1.0), jnp.zeros_like(first), jnp.zeros_like(second)))
    count = jnp.sum(labels)
    states = jnp.stack([first.reshape(MICRO, NODES, H), second.reshape(MICRO, NODES, H)])
    state_grads = jnp.stack([node_grad.reshape(MICRO, NODES, H), probe_grad.reshape(MICRO, NODES, H)])
    scaled = [g / count for g in grads]
    return (states, state_grads, scaled[0], scaled[1], scaled[2], scaled[3], scaled[4], scaled[5], scaled[6], scaled[7])
```

```python
import functools

import jax
import jax.numpy as jnp
from jax import lax
from jax.experimental import pallas as pl
from jax.experimental.pallas import tpu as pltpu
from jax.sharding import PartitionSpec as P

BF, F32 = jnp.bfloat16, jnp.float32
VMEM = pltpu.VMEM
LANE = 128
ROUND = 16
SMALL_ROWS = 1024


def dot(a, b, ca=1, cb=0):
    return lax.dot_general(a, b, (((ca,), (cb,)), ((), ())), preferred_element_type=F32)


def split(x, parts):
    out = []
    for _ in range(parts - 1):
        piece = x.astype(BF)
        out.append(piece)
        x = x - piece.astype(F32)
    out.append(x.astype(BF))
    return out


def loop(count, body):
    def step(i, carry):
        body(i)
        return carry

    lax.fori_loop(0, count, step, 0)


def aligned(i, size):
    return pl.ds(pl.multiple_of(i * size, size), size)


def edge_tables(ends, nodes):
    ids = lax.broadcasted_iota(jnp.int32, (nodes, ends.shape[1]), 0).astype(F32)
    pick = (ids == ends[0:1]).astype(F32).astype(BF)
    put = (ids == ends[1:2]).astype(F32).astype(BF)
    return pick, put


def pack_ends(src_ref, tgt_ref, valid_ref, lab_ref, s):
    row = pl.ds(s, 1)
    src = src_ref[row, :].astype(F32)
    tgt = jnp.where(valid_ref[row, :] > 0, tgt_ref[row, :], -1).astype(F32)
    lab = lab_ref[row, :].astype(F32)
    edges, nodes = src.shape[1], lab.shape[1]
    lab = jnp.concatenate([lab, jnp.zeros((1, edges - nodes), F32)], axis=1)
    return jnp.concatenate([src, tgt, lab, jnp.zeros((13, edges), F32)], axis=0)


def edge_hidden(feats, w1, b1):
    bias = jnp.broadcast_to(b1.astype(F32), (LANE, LANE)).T[:, 0:1]
    return dot(w1, feats, 0, 0) + bias


def gru_forward(m, h, wi, bi, wh, bh):
    w = h.shape[1]
    gi = dot(m, wi) + bi.astype(F32)
    gh = dot(h, wh) + bh.astype(F32)
    r = jax.nn.sigmoid(gi[:, :w] + gh[:, :w])
    u = jax.nn.sigmoid(gi[:, w : 2 * w] + gh[:, w : 2 * w])
    n = jnp.tanh(gi[:, 2 * w :] + r * gh[:, 2 * w :])
    fresh = (1.0 - u) * n + u * h.astype(F32)
    return fresh, gh[:, 2 * w :], r, u, n


def gru_backward(g, h, gates, wi, wh):
    _, ghn, r, u, n = gates
    dn = g * (1.0 - u)
    du = g * (h.astype(F32) - n)
    dnpre = dn * (1.0 - n * n)
    dupre = du * u * (1.0 - u)
    drpre = dnpre * ghn * r * (1.0 - r)
    dgi = jnp.concatenate([drpre, dupre, dnpre], axis=1).astype(BF)
    dgh = jnp.concatenate([drpre, dupre, dnpre * r], axis=1).astype(BF)
    dm = dot(dgi, wi, 1, 1).astype(BF)
    dh = g * u + dot(dgh, wh, 1, 1)
    return dgi, dgh, dm, dh


def local_kernel(
    x_ref, f_ref, src_ref, tgt_ref, val_ref, lab_ref, w1_ref, b1_ref, w2_hbm, b2_ref,
    wi_ref, bi_ref, wh_ref, bh_ref, cot_ref,
    fi_out, h1_out, dt2_out, dt1_out, h2_out, d1_out, d0_out, sm_out, w1_out,
    w2, amat, acc, zaug, zpre_s, hs, hsl, dms, dml, xbuf, dzacc, picks, puts, sem,
):
    s = lax.axis_index("section")
    w2_copy = pltpu.make_async_copy(w2_hbm, w2, sem)
    w2_copy.start()
    edges = f_ref.shape[2]
    nodes = x_ref.shape[1]
    feats = f_ref[s]
    ends = pack_ends(src_ref, tgt_ref, val_ref, lab_ref, s)
    fi_out[0:16] = feats
    fi_out[16:32] = ends.astype(BF)
    pick, put = edge_tables(ends, nodes)
    picks[...] = pick
    puts[...] = put
    zpre = edge_hidden(feats, w1_ref[...], b1_ref[...])
    zpre_s[...] = zpre
    zaug[0:LANE] = jax.nn.silu(zpre).astype(BF)
    zaug[LANE : 2 * LANE] = jnp.ones((LANE, edges), BF)
    h0 = x_ref[s]

    def sources(t, h):
        got = dot(h, picks[...], 0, 0)
        hs[t] = got
        hsl[:, t * edges : (t + 1) * edges] = got.astype(BF)

    sources(0, h0)
    lane = lax.broadcasted_iota(jnp.int32, (LANE, LANE), 1)
    b2t = b2_ref[...].T
    w2_copy.wait()
    tiles = [(e, min(256, edges - e)) for e in range(0, edges, 256)]

    def keep(i, e, w, p):
        p = p.reshape(16, 8, w).sum(0)
        for o in range(0, w, LANE):
            acc[(e + o) // LANE, aligned(i, 8), :] = p[:, o : o + LANE]

    def first(ib):
        lhs = []
        for v in range(ROUND):
            i = ib * ROUND + v
            bias = jnp.where(lane == i, b2t, jnp.zeros_like(b2t))
            lhs.append(jnp.concatenate([w2[:, aligned(i, LANE)].T, bias], axis=1))
        lhs = jnp.concatenate(lhs, axis=0)
        for e, w in tiles:
            a = dot(lhs, zaug[:, e : e + w]).astype(BF)
            amat[aligned(ib, ROUND * LANE), e : e + w] = a
            for v in range(ROUND):
                p = a[v * LANE : (v + 1) * LANE].astype(F32) * hs[0, :, e : e + w]
                keep(ib * ROUND + v, e, w, p)

    loop(LANE // ROUND, first)

    def again(ib):
        for e, w in tiles:
            for v in range(8):
                a = amat[aligned(ib * 8 + v, LANE), e : e + w]
                p = a.astype(F32) * hs[1, :, e : e + w]
                keep(ib * 8 + v, e, w, p)

    def gathered():
        msg = []
        for e in range(edges // LANE):
            part = acc[e, pl.ds(0, LANE, stride=8), :]
            for q in range(1, 8):
                part = part + acc[e, pl.ds(q, LANE, stride=8), :]
            msg.append(part)
        msg = jnp.concatenate(msg, axis=1)
        total = jnp.zeros((nodes, LANE), F32)
        for piece in split(msg, 3):
            total = total + dot(puts[...], piece, 1, 1)
        return total.astype(BF)

    weights = (wi_ref[...], bi_ref[...], wh_ref[...], bh_ref[...])
    m1 = gathered()
    gates1 = gru_forward(m1, h0, *weights)
    h1 = gates1[0].astype(BF)
    h1_out[...] = h1
    sources(1, h1)
    loop(LANE // 8, again)
    m2 = gathered()
    gates2 = gru_forward(m2, h1, *weights)
    h2_out[...] = gates2[0]
    label = jnp.broadcast_to(ends[2:3, :nodes], (LANE, nodes)).T
    g2 = cot_ref[s] * label
    dgi2, dgh2, dm2, dh2 = gru_backward(g2, h1, gates2, weights[0], weights[2])
    dt2 = dm2.T
    dt2_out[...] = dt2

    def spread(t, dt):
        got = dot(dt, puts[...])
        dms[t] = got
        dml[:, t * edges : (t + 1) * edges] = got.astype(BF)

    def to_sources(t):
        outs = []
        for e in range(0, edges, LANE):

            def body(ib, total):
                d = dms[t, aligned(ib, 8), e : e + LANE]
                for v in range(8):
                    a = amat[aligned(ib * 8 + v, LANE), e : e + LANE].astype(F32)
                    total = total + a * d[v : v + 1]
                return total

            outs.append(lax.fori_loop(0, LANE // 8, body, jnp.zeros((LANE, LANE), F32)))
        back = jnp.concatenate(outs, axis=1)
        total = jnp.zeros((nodes, LANE), F32)
        for piece in split(back, 3):
            total = total + dot(picks[...], piece, 1, 1)
        return total

    spread(1, dt2)
    d1 = (dh2 + to_sources(1)).astype(BF)
    d1_out[...] = d1.astype(F32)
    dgi1, dgh1, dm1, dh1 = gru_backward(d1.astype(F32), h0, gates1, weights[0], weights[2])
    dt1 = dm1.T
    dt1_out[...] = dt1
    spread(0, dt1)
    d0_out[...] = dh1 + to_sources(0)

    gwi = dot(m1, dgi1, 0, 0) + dot(m2, dgi2, 0, 0)
    gwh = dot(h0, dgh1, 0, 0) + dot(h1, dgh2, 0, 0)
    for q in range(3):
        sm_out[q * LANE : (q + 1) * LANE] = gwi[:, q * LANE : (q + 1) * LANE]
        sm_out[(3 + q) * LANE : (4 + q) * LANE] = gwh[:, q * LANE : (q + 1) * LANE]
    sm_out[6 * LANE : 7 * LANE] = dot(dml[...], hsl[...], 1, 1)
    gbi = dgi1.astype(F32).sum(0, keepdims=True) + dgi2.astype(F32).sum(0, keepdims=True)
    gbh = dgh1.astype(F32).sum(0, keepdims=True) + dgh2.astype(F32).sum(0, keepdims=True)
    rows = [x[:, q * LANE : (q + 1) * LANE] for x in (gbi, gbh) for q in range(3)]
    rows.append(jnp.zeros((SMALL_ROWS - 7 * LANE - 6, LANE), F32))
    sm_out[7 * LANE :] = jnp.concatenate(rows, axis=0)

    dzacc[...] = jnp.zeros_like(dzacc)

    def back_hidden(ib):
        for t in range(2):
            h = hsl[:, t * edges : (t + 1) * edges].astype(F32)
            d = dms[t, aligned(ib, ROUND), :]
            for v in range(ROUND):
                xbuf[v * LANE : (v + 1) * LANE, t * edges : (t + 1) * edges] = (
                    h * d[v : v + 1]
                ).astype(BF)
        dzacc[...] += dot(w2[:, aligned(ib, ROUND * LANE)], xbuf[...])

    loop(LANE // ROUND, back_hidden)
    zp = zpre_s[...]
    sig = jax.nn.sigmoid(zp)
    slope = sig * (1.0 + zp * (1.0 - sig))
    lhs = jnp.concatenate(
        [feats, jnp.ones((1, edges), BF), jnp.zeros((15, edges), BF)], axis=0
    )
    total = jnp.zeros((32, LANE), F32)
    for t in range(2):
        dzpre = (dzacc[:, t * edges : (t + 1) * edges] * slope).astype(BF)
        total = total + dot(lhs, dzpre, 1, 1)
    w1_out[...] = total


def shard_kernel(fi_ref, h0_ref, h1_ref, dt1_ref, dt2_ref, w1_ref, b1_ref, out_ref, qst, tmp):
    s, c = lax.axis_index("section"), lax.axis_index("dp")
    blocks, _, edges = fi_ref.shape
    nodes = h0_ref.shape[1]
    per = LANE // blocks
    first_k = (c * 2 + s) * per
    rows = lax.broadcasted_iota(jnp.int32, (8, LANE), 0) + first_k
    sel = (rows == lax.broadcasted_iota(jnp.int32, (8, LANE), 1)).astype(F32)
    w1t = dot(sel.astype(BF), w1_ref[...], 1, 1).astype(BF)
    b1 = jnp.sum(sel * b1_ref[...].astype(F32), axis=1, keepdims=True)
    quarter = nodes // 4
    qn = lax.broadcasted_iota(jnp.int32, (quarter, 256), 0).astype(F32)

    def build(blk):
        z = jax.nn.silu(dot(w1t, fi_ref[blk, 0:16]) + b1).astype(BF).astype(F32)
        ends = fi_ref[blk, 16:32].astype(F32)
        for q in range(4):
            lo = q * LANE
            zq = z[:, lo : lo + 256]
            hit_t = (qn + float(q * quarter)) == ends[1:2, lo : lo + 256]
            hit_s = (qn + float(q * quarter)) == ends[0:1, lo : lo + 256]
            lhs = [jnp.where(hit_t, zq[k : k + 1], 0.0).astype(BF) for k in range(per)]
            lhs = jnp.concatenate(lhs, axis=0)
            pairs = dot(lhs, hit_s.astype(F32).astype(BF), 1, 1)
            pairs = jnp.concatenate(split(pairs, 2), axis=1)
            row = aligned(q, quarter)
            h = jnp.concatenate([h0_ref[blk, row, :], h1_ref[blk, row, :]], axis=1)
            got = dot(pairs, jnp.concatenate([h, h], axis=0)).astype(BF)
            for t in range(2):
                for k in range(per):
                    qst[t, pl.ds(pl.multiple_of(blk * nodes + q * quarter, quarter), quarter), k * LANE : (k + 1) * LANE] = got[k * quarter : (k + 1) * quarter, t * LANE : (t + 1) * LANE]

    loop(blocks, build)
    total = jnp.zeros((LANE, per * LANE), F32)
    for t, ref in ((0, dt1_ref), (1, dt2_ref)):
        lhs = jnp.concatenate([ref[blk] for blk in range(blocks)], axis=1)
        total = total + dot(lhs, qst[t])
    count = jnp.zeros((1, 1), F32)
    for blk in range(blocks):
        count = count + jnp.sum(fi_ref[blk, 16:32].astype(F32)[2:3, :nodes], axis=1, keepdims=True)
    total = total / count
    for k in range(per):
        tmp[pl.ds(k, LANE, stride=per), :] = total[:, k * LANE : (k + 1) * LANE]
    out_ref[...] = tmp[...].astype(BF)


def final_kernel(a_ref, b_ref, out_ref):
    per = a_ref.shape[1] // LANE
    a = a_ref[0].astype(F32)
    b = b_ref[0].astype(F32)
    for i in range(LANE):
        out_ref[:, i * LANE : (i + 1) * LANE] = jnp.concatenate(
            [a[i * per : (i + 1) * per], b[i * per : (i + 1) * per]], axis=0
        )


def shards(
    node_input, edge_input, edge_source, edge_target, edge_valid, node_labeled,
    edge_w1, edge_b1, edge_w2, edge_b2, gru_wi, gru_bi, gru_wh, gru_bh, state_cot,
):
    micro, nodes, width = node_input.shape
    edges = edge_input.shape[2]
    parts = lax.axis_size("dp")
    blocks = 2 * parts
    per = width // blocks
    vm = pl.BlockSpec(memory_space=VMEM)
    limit = pltpu.CompilerParams(vmem_limit_bytes=60 * 2**20)
    sds = jax.ShapeDtypeStruct
    b1 = edge_b1.reshape(1, -1)
    fi, h1, dt2, dt1, h2, d1, d0, small, gw1 = pl.pallas_call(
        local_kernel,
        out_shape=(
            sds((32, edges), BF), sds((nodes, width), BF), sds((width, nodes), BF),
            sds((width, nodes), BF), sds((nodes, width), F32), sds((nodes, width), F32),
            sds((nodes, width), F32), sds((SMALL_ROWS, width), F32), sds((32, width), F32),
        ),
        in_specs=[vm] * 8 + [pl.BlockSpec(memory_space=pl.ANY)] + [vm] * 6,
        out_specs=[vm] * 9,
        scratch_shapes=[
            VMEM((width, width * width), BF), VMEM((width * width, edges), BF),
            VMEM((edges // LANE, 8 * width, LANE), F32), VMEM((2 * width, edges), BF),
            VMEM((width, edges), F32), VMEM((2, width, edges), F32),
            VMEM((width, 2 * edges), BF), VMEM((2, width, edges), F32),
            VMEM((width, 2 * edges), BF), VMEM((ROUND * width, 2 * edges), BF),
            VMEM((width, 2 * edges), F32), VMEM((nodes, edges), BF), VMEM((nodes, edges), BF),
            pltpu.SemaphoreType.DMA,
        ],
        compiler_params=limit,
    )(
        node_input, edge_input, edge_source, edge_target, edge_valid, node_labeled,
        edge_w1, b1, edge_w2, edge_b2.reshape(width, width),
        gru_wi, gru_bi.reshape(1, -1), gru_wh, gru_bh.reshape(1, -1), state_cot,
    )
    every = ("section", "dp")
    fi_all = lax.all_gather(fi, every)
    h1_all = lax.all_gather(h1, every)
    dt2_all = lax.all_gather(dt2, every)
    dt1_all = lax.all_gather(dt1, every)
    h0_all = lax.all_gather(node_input, "dp", axis=1).reshape(blocks, nodes, width)
    shard = pl.pallas_call(
        shard_kernel,
        out_shape=sds((width * per, width), BF),
        in_specs=[vm] * 7,
        out_specs=vm,
        scratch_shapes=[
            VMEM((2, blocks * nodes, per * width), BF), VMEM((width * per, width), F32)
        ],
        compiler_params=limit,
    )(fi_all, h0_all, h1_all, dt1_all, dt2_all, edge_w1, b1)
    full = lax.all_gather(shard, every)
    grad_w2 = pl.pallas_call(
        final_kernel,
        grid=(parts,),
        out_shape=sds((width, width * width), F32),
        in_specs=[
            pl.BlockSpec((1, width * per, width), lambda c: (c, 0, 0)),
            pl.BlockSpec((1, width * per, width), lambda c: (c + parts, 0, 0)),
        ],
        out_specs=pl.BlockSpec((2 * per, width * width), lambda c: (c, 0)),
    )(full, full)
    count = jnp.sum(fi_all[:, 18, :nodes].astype(F32))
    small, gw1 = lax.psum((small, gw1), every)
    small, gw1 = small / count, gw1 / count
    h1f = h1.astype(F32)
    mine = jnp.where(lax.axis_index("section") == 0, h1f, h2)
    other = jnp.where(lax.axis_index("section") == 0, h2, h1f)
    minex = jnp.where(lax.axis_index("section") == 0, d0, d1)
    otherx = jnp.where(lax.axis_index("section") == 0, d1, d0)
    got, gotx = lax.ppermute((other, otherx), "section", [(0, 1), (1, 0)])

    def order(a, b):
        return jnp.where(lax.axis_index("section") == 0, jnp.stack([a, b]), jnp.stack([b, a]))

    def third(rows):
        return rows.reshape(3, width, width).transpose(1, 0, 2).reshape(width, 3 * width)

    return (
        order(mine, got)[None],
        order(minex, gotx)[None],
        gw1[:16],
        gw1[16],
        grad_w2,
        small[6 * width : 7 * width].reshape(-1),
        third(small[: 3 * width]),
        small[7 * width : 7 * width + 3].reshape(-1),
        third(small[3 * width : 6 * width]),
        small[7 * width + 3 : 7 * width + 6].reshape(-1),
    )


EDGE_BLOCK = 128


def passed_along(value, axis, steps):
    count = lax.axis_size(axis)
    leading, last = (max(0, -steps), min(count, count - steps))
    return lax.ppermute(value, axis, [(source, source + steps) for source in range(leading, last)])


def split_blocks(feats, source, target, valid, block):
    count = feats.shape[1] // block
    return (
        feats.reshape(feats.shape[0], count, block).transpose(1, 0, 2),
        source.reshape(count, block),
        target.reshape(count, block),
        valid.reshape(count, block),
    )


def block_front(feats_b, source_b, weights, state_low):
    width = state_low.shape[1]
    zpre = jnp.dot(feats_b.T, weights[0], preferred_element_type=jnp.float32) + weights[1].astype(
        jnp.float32
    )
    z_low = jax.nn.silu(zpre).astype(jnp.bfloat16)
    amat = (
        jnp.dot(z_low, weights[2], preferred_element_type=jnp.float32)
        + weights[3].astype(jnp.float32)
    ).astype(jnp.bfloat16)
    amat = amat.reshape(-1, width, width)
    node_ids = lax.iota(jnp.int32, state_low.shape[0])
    pick = (source_b[:, None] == node_ids[None, :]).astype(jnp.bfloat16)
    h_source = jnp.dot(pick, state_low, preferred_element_type=jnp.float32).astype(jnp.bfloat16)
    return (zpre, z_low, amat, h_source)


def target_table(target_b, valid_b, nodes):
    node_ids = lax.iota(jnp.int32, nodes)
    return ((target_b[:, None] == node_ids[None, :]) & (valid_b[:, None] > 0)).astype(jnp.bfloat16)


def forward_messages(state_low, blocks, weights):
    nodes, width = state_low.shape

    def add(total, pieces):
        feats_b, source_b, target_b, valid_b = pieces
        _, _, amat, h_source = block_front(feats_b, source_b, weights, state_low)
        message = jnp.einsum("eij,ej->ei", amat, h_source, preferred_element_type=jnp.float32)
        message = message * (valid_b > 0).astype(jnp.float32)[:, None]
        return (total + jax.ops.segment_sum(message, target_b, num_segments=nodes), None)

    summed, _ = lax.scan(add, jnp.zeros((nodes, width), jnp.float32), blocks)
    return summed


def gru_gates(gathered_low, state_low, weights):
    width = state_low.shape[1]
    gate_in = jnp.dot(gathered_low, weights[4], preferred_element_type=jnp.float32) + weights[
        5
    ].astype(jnp.float32)
    gate_state = jnp.dot(state_low, weights[6], preferred_element_type=jnp.float32) + weights[
        7
    ].astype(jnp.float32)
    reset = jax.nn.sigmoid(gate_in[:, :width] + gate_state[:, :width])
    update = jax.nn.sigmoid(gate_in[:, width : 2 * width] + gate_state[:, width : 2 * width])
    candidate = jnp.tanh(gate_in[:, 2 * width :] + reset * gate_state[:, 2 * width :])
    fresh = (1.0 - update) * candidate + update * state_low.astype(jnp.float32)
    return (fresh, gate_state, reset, update, candidate)


def backward_step(upstream, state_low, gathered_low, blocks, weights):
    nodes, width = state_low.shape
    fresh, gate_state, reset, update, candidate = gru_gates(gathered_low, state_low, weights)
    state = state_low.astype(jnp.float32)
    d_cand = upstream * (1.0 - update)
    d_update = upstream * (state - candidate)
    d_state = upstream * update
    d_npre = d_cand * (1.0 - candidate * candidate)
    d_upre = d_update * update * (1.0 - update)
    d_rpre = d_npre * gate_state[:, 2 * width :] * reset * (1.0 - reset)
    d_in = jnp.concatenate([d_rpre, d_upre, d_npre], axis=1).astype(jnp.bfloat16)
    d_hid = jnp.concatenate([d_rpre, d_upre, d_npre * reset], axis=1).astype(jnp.bfloat16)
    grad_wi = jnp.dot(gathered_low.T, d_in, preferred_element_type=jnp.float32)
    grad_bi = jnp.sum(d_in.astype(jnp.float32), axis=0)
    grad_wh = jnp.dot(state_low.T, d_hid, preferred_element_type=jnp.float32)
    grad_bh = jnp.sum(d_hid.astype(jnp.float32), axis=0)
    d_state = d_state + jnp.dot(d_hid, weights[6].T, preferred_element_type=jnp.float32)
    d_gathered = jnp.dot(d_in, weights[4].T, preferred_element_type=jnp.float32).astype(
        jnp.bfloat16
    )

    def back_block(carry, pieces):
        d_src, grad_w1, grad_b1, grad_w2, grad_b2 = carry
        feats_b, source_b, target_b, valid_b = pieces
        zpre, z_low, amat, h_source = block_front(feats_b, source_b, weights, state_low)
        put = target_table(target_b, valid_b, nodes)
        d_msg = jnp.dot(put, d_gathered, preferred_element_type=jnp.float32).astype(jnp.bfloat16)
        d_amat = d_msg.astype(jnp.float32)[:, :, None] * h_source.astype(jnp.float32)[:, None, :]
        d_amat = d_amat.reshape(d_amat.shape[0], width * width).astype(jnp.bfloat16)
        grad_w2 = grad_w2 + jnp.dot(z_low.T, d_amat, preferred_element_type=jnp.float32)
        grad_b2 = grad_b2 + jnp.sum(d_amat.astype(jnp.float32), axis=0)
        d_z = jnp.dot(d_amat, weights[2].T, preferred_element_type=jnp.float32)
        sig = jax.nn.sigmoid(zpre)
        d_zpre = (d_z * sig * (1.0 + zpre * (1.0 - sig))).astype(jnp.bfloat16)
        grad_w1 = grad_w1 + jnp.dot(feats_b, d_zpre, preferred_element_type=jnp.float32)
        grad_b1 = grad_b1 + jnp.sum(d_zpre.astype(jnp.float32), axis=0)
        d_source = jnp.einsum("eij,ei->ej", amat, d_msg, preferred_element_type=jnp.float32)
        d_src = d_src + jax.ops.segment_sum(d_source, source_b, num_segments=nodes)
        return ((d_src, grad_w1, grad_b1, grad_w2, grad_b2), None)

    start = (
        jnp.zeros((nodes, width), jnp.float32),
        jnp.zeros(weights[0].shape, jnp.float32),
        jnp.zeros(weights[1].shape, jnp.float32),
        jnp.zeros(weights[2].shape, jnp.float32),
        jnp.zeros(weights[3].shape, jnp.float32),
    )
    ends, _ = lax.scan(back_block, start, blocks)
    d_total = d_state + ends[0]
    return (d_total, (ends[1], ends[2], ends[3], ends[4], grad_wi, grad_bi, grad_wh, grad_bh))


def plain_shards(
    node_input,
    edge_input,
    edge_source,
    edge_target,
    edge_valid,
    node_labeled,
    edge_w1,
    edge_b1,
    edge_w2,
    edge_b2,
    gru_wi,
    gru_bi,
    gru_wh,
    gru_bh,
    state_cot,
):
    weights = (edge_w1, edge_b1, edge_w2, edge_b2, gru_wi, gru_bi, gru_wh, gru_bh)
    micro, nodes, width = node_input.shape
    block = min(EDGE_BLOCK, edge_input.shape[2])
    section_id = lax.axis_index("section")
    first = section_id == 0
    count_local = jnp.sum(node_labeled.astype(jnp.float32))

    def batch_blocks(index):
        feats = lax.dynamic_index_in_dim(edge_input, index, 0, keepdims=False)
        source = lax.dynamic_index_in_dim(edge_source, index, 0, keepdims=False)
        target = lax.dynamic_index_in_dim(edge_target, index, 0, keepdims=False)
        valid = lax.dynamic_index_in_dim(edge_valid, index, 0, keepdims=False)
        return split_blocks(feats, source, target, valid, block)

    received = jnp.zeros((nodes, width), jnp.bfloat16)
    saved = []
    states_out = jnp.zeros((micro, nodes, width), jnp.float32)
    for tick in range(micro + 1):
        batch = tick - section_id
        live = (batch >= 0) & (batch < micro)
        index = jnp.clip(batch, 0, micro - 1)
        state_low = jnp.where(first, node_input[min(tick, micro - 1)], received)
        blocks = batch_blocks(index)
        gathered_low = forward_messages(state_low, blocks, weights).astype(jnp.bfloat16)
        fresh = gru_gates(gathered_low, state_low, weights)[0]
        saved.append((state_low, gathered_low))
        sending = fresh.astype(jnp.bfloat16)
        value = jnp.where(first, sending.astype(jnp.float32), fresh)
        states_out = jnp.where(
            live, lax.dynamic_update_index_in_dim(states_out, value, index, 0), states_out
        )
        if tick < micro:
            received = passed_along(sending, "section", 1)
    grad_received = jnp.zeros((nodes, width), jnp.bfloat16)
    grads_out = jnp.zeros((micro, nodes, width), jnp.float32)
    totals = tuple((jnp.zeros(w.shape, jnp.float32) for w in weights))
    for tick in range(micro + 1):
        batch = micro - tick - section_id
        live = (batch >= 0) & (batch < micro)
        index = jnp.clip(batch, 0, micro - 1)
        state_low, gathered_low = saved[micro - tick]
        labels = lax.dynamic_index_in_dim(node_labeled, index, 0, keepdims=False).astype(
            jnp.float32
        )
        top = lax.dynamic_index_in_dim(state_cot, index, 0, keepdims=False) * labels[:, None]
        upstream = jnp.where(first, grad_received.astype(jnp.float32), top)
        d_total, terms = backward_step(
            upstream, state_low, gathered_low, batch_blocks(index), weights
        )
        totals = tuple((acc + jnp.where(live, term, 0.0) for acc, term in zip(totals, terms)))
        sending = d_total.astype(jnp.bfloat16)
        value = jnp.where(first, d_total, sending.astype(jnp.float32))
        grads_out = jnp.where(
            live, lax.dynamic_update_index_in_dim(grads_out, value, index, 0), grads_out
        )
        if tick < micro:
            grad_received = passed_along(sending, "section", -1)
    count_total = lax.psum(count_local, "dp")
    summed = lax.psum(
        (totals[0], totals[1], totals[2], totals[3], totals[4], totals[5], totals[6], totals[7]),
        ("section", "dp"),
    )
    scaled = [g / count_total for g in summed]
    return (
        states_out[None],
        grads_out[None],
        scaled[0],
        scaled[1],
        scaled[2],
        scaled[3],
        scaled[4],
        scaled[5],
        scaled[6],
        scaled[7],
    )


def solution(mesh):
    placed = (
        P(None, "dp", None), P(None, None, "dp"), P(None, "dp"), P(None, "dp"), P(None, "dp"),
        P(None, "dp"), P(), P(), P(), P(), P(), P(), P(), P(), P(None, "dp", None),
    )
    fits = LANE % (2 * mesh.shape["dp"]) == 0
    return jax.shard_map(
        shards if fits else plain_shards,
        mesh=mesh,
        in_specs=placed,
        out_specs=(P("section", None, "dp", None), P("section", None, "dp", None)) + (P(),) * 8,
        check_vma=False,
    )
```

```python
import functools

import jax
import jax.numpy as jnp
from jax import lax
from jax.experimental import pallas as pl
from jax.experimental.pallas import tpu as pltpu
from jax.sharding import PartitionSpec as P

BF, F32 = jnp.bfloat16, jnp.float32
VMEM = pltpu.VMEM
LANE = 128
ROUND = 16
SMALL_ROWS = 1024
PLANE = 4
SEMS = 128


def dot(a, b, ca=1, cb=0):
    return lax.dot_general(a, b, (((ca,), (cb,)), ((), ())), preferred_element_type=F32)


def split(x, parts):
    out = []
    for _ in range(parts - 1):
        piece = x.astype(BF)
        out.append(piece)
        x = x - piece.astype(F32)
    out.append(x.astype(BF))
    return out


def loop(count, body):
    def step(i, carry):
        body(i)
        return carry

    lax.fori_loop(0, count, step, 0)


def aligned(i, size):
    return pl.ds(pl.multiple_of(i * size, size), size)


def edge_tables(ends, nodes):
    ids = lax.broadcasted_iota(jnp.int32, (nodes, ends.shape[1]), 0).astype(F32)
    pick = (ids == ends[0:1]).astype(F32).astype(BF)
    put = (ids == ends[1:2]).astype(F32).astype(BF)
    return pick, put


def pack_ends(src_ref, tgt_ref, valid_ref, lab_ref, s):
    row = pl.ds(s, 1)
    src = src_ref[row, :].astype(F32)
    tgt = jnp.where(valid_ref[row, :] > 0, tgt_ref[row, :], -1).astype(F32)
    lab = lab_ref[row, :].astype(F32)
    edges, nodes = src.shape[1], lab.shape[1]
    lab = jnp.concatenate([lab, jnp.zeros((1, edges - nodes), F32)], axis=1)
    return jnp.concatenate([src, tgt, lab, jnp.zeros((13, edges), F32)], axis=0)


def edge_hidden(feats, w1, b1):
    bias = jnp.broadcast_to(b1.astype(F32), (LANE, LANE)).T[:, 0:1]
    return dot(w1, feats, 0, 0) + bias


def gru_forward(m, h, wi, bi, wh, bh):
    w = h.shape[1]
    gi = dot(m, wi) + bi.astype(F32)
    gh = dot(h, wh) + bh.astype(F32)
    r = jax.nn.sigmoid(gi[:, :w] + gh[:, :w])
    u = jax.nn.sigmoid(gi[:, w : 2 * w] + gh[:, w : 2 * w])
    n = jnp.tanh(gi[:, 2 * w :] + r * gh[:, 2 * w :])
    fresh = (1.0 - u) * n + u * h.astype(F32)
    return fresh, gh[:, 2 * w :], r, u, n


def gru_backward(g, h, gates, wi, wh):
    _, ghn, r, u, n = gates
    dn = g * (1.0 - u)
    du = g * (h.astype(F32) - n)
    dnpre = dn * (1.0 - n * n)
    dupre = du * u * (1.0 - u)
    drpre = dnpre * ghn * r * (1.0 - r)
    dgi = jnp.concatenate([drpre, dupre, dnpre], axis=1).astype(BF)
    dgh = jnp.concatenate([drpre, dupre, dnpre * r], axis=1).astype(BF)
    dm = dot(dgi, wi, 1, 1).astype(BF)
    dh = g * u + dot(dgh, wh, 1, 1)
    return dgi, dgh, dm, dh


class Net:
    def __init__(self, send_sems, recv_sems):
        self.send_sems, self.recv_sems = send_sems, recv_sems
        self.slots, self.sent = {}, []

    def slot(self, key):
        return self.slots.setdefault(key, len(self.slots))

    def send(self, key, src, dst, peer):
        copy = pltpu.make_async_remote_copy(
            src_ref=src,
            dst_ref=dst,
            send_sem=self.send_sems.at[len(self.sent)],
            recv_sem=self.recv_sems.at[self.slot(key)],
            device_id=peer,
            device_id_type=pl.DeviceIdType.MESH,
        )
        copy.start()
        self.sent.append(copy)

    def wait(self, key, region, peer):
        pltpu.make_async_remote_copy(
            src_ref=region,
            dst_ref=region,
            send_sem=self.send_sems.at[0],
            recv_sem=self.recv_sems.at[self.slot(key)],
            device_id=peer,
            device_id_type=pl.DeviceIdType.MESH,
        ).wait_recv()

    def drain(self):
        for copy in self.sent:
            copy.wait_send()


class Place:
    def __init__(self, parts):
        self.parts, self.plane = parts, PLANE
        self.lines = parts // PLANE
        self.s, self.c = lax.axis_index("section"), lax.axis_index("dp")
        self.sibling = {"section": 1 - self.s}

    def flip(self, mask):
        at, bit = self.c, 1
        while bit <= mask:
            if mask & bit:
                at = at + bit * (1 - 2 * lax.rem(lax.div(self.c, bit), 2))
            bit *= 2
        return at

    def peer(self, mask):
        return {"dp": self.flip(mask)}

    def block(self, mask):
        return self.s * self.parts + self.flip(mask)

    def level(self, line):
        own = lax.div(self.flip(line * self.plane), self.plane) * self.plane
        return self.s * self.parts + own


class Gather:
    def __init__(self, net, place, name, buf):
        self.net, self.place, self.name, self.buf = net, place, name, buf

    def send(self, key, mask, peer):
        ref = self.buf.at[self.place.block(mask)]
        self.net.send((self.name,) + key, ref, ref, peer)

    def recv(self, key, mask, peer):
        self.net.wait((self.name,) + key, self.buf.at[self.place.block(mask)], peer)

    def begin(self):
        p = self.place
        for line in range(1, p.lines):
            self.send((line, 0), 0, p.peer(line * p.plane))
        for q in range(1, p.plane):
            self.send((0, q), 0, p.peer(q))

    def along(self):
        p = self.place
        for line in range(1, p.lines):
            mask = line * p.plane
            self.recv((line, 0), mask, p.peer(mask))
            for q in range(1, p.plane):
                self.send((line, q), mask, p.peer(q))

    def across(self):
        p = self.place
        for line in range(p.lines):
            for q in range(1, p.plane):
                self.recv((line, q), line * p.plane + q, p.peer(q))
            ref = self.buf.at[pl.ds(p.level(line), p.plane)]
            self.net.send((self.name, "sib", line), ref, ref, p.sibling)

    def finish(self):
        p = self.place
        for line in range(p.lines):
            first = p.level(line) + (1 - 2 * p.s) * p.parts
            self.net.wait((self.name, "sib", line), self.buf.at[pl.ds(first, p.plane)], p.sibling)


def main_kernel(
    x_ref, f_ref, src_ref, tgt_ref, val_ref, lab_ref, w1_ref, b1_ref, w2_hbm, b2_ref,
    wi_ref, bi_ref, wh_ref, bh_ref, cot_ref,
    full_out, states_out, grads_out, w1_out,
    w2, amat, acc, zaug, zpre_s, hs, hsl, dms, dml, xbuf, dzacc, picks, puts,
    ins, hid, dts, qst, tmp, mine, small, small_in, small_lo, small_line, small_plane,
    w1_io, swap, w2_sems, own_sem, send_sems, recv_sems,
):
    edges, nodes = f_ref.shape[2], x_ref.shape[1]
    tiles5 = edges // LANE
    parts = full_out.shape[0] // 2
    blocks = 2 * parts
    per = LANE // blocks
    place = Place(parts)
    net = Net(send_sems, recv_sems)
    s, c = place.s, place.c
    me = place.block(0)
    rounds = LANE // ROUND

    barrier = pltpu.get_barrier_semaphore()
    peers = [place.peer(q) for q in range(1, PLANE)]
    peers += [place.peer(line * PLANE) for line in range(1, place.lines)] + [place.sibling]
    for peer in peers:
        pl.semaphore_signal(
            barrier, inc=1, device_id=peer, device_id_type=pl.DeviceIdType.MESH
        )

    def w2_copy(ib):
        part = aligned(ib, ROUND * LANE)
        return pltpu.make_async_copy(w2_hbm.at[:, part], w2.at[:, part], w2_sems.at[ib])

    for ib in range(rounds):
        w2_copy(ib).start()

    feats = f_ref[s]
    ends = pack_ends(src_ref, tgt_ref, val_ref, lab_ref, s)
    h0 = x_ref[s]
    table = jnp.concatenate([feats, ends.astype(BF)], axis=0)
    for e in range(tiles5):
        ins[me, e * 32 : (e + 1) * 32, :] = table[:, e * LANE : (e + 1) * LANE]
    ins[me, tiles5 * 32 : tiles5 * 32 + nodes, :] = h0
    pick, put = edge_tables(ends, nodes)
    picks[...] = pick
    puts[...] = put
    zpre = edge_hidden(feats, w1_ref[...], b1_ref[...])
    zpre_s[...] = zpre
    zaug[0:LANE] = jax.nn.silu(zpre).astype(BF)
    zaug[LANE : 2 * LANE] = jnp.ones((LANE, edges), BF)

    def sources(t, h):
        got = dot(h, picks[...], 0, 0)
        hs[t] = got
        hsl[:, t * edges : (t + 1) * edges] = got.astype(BF)

    sources(0, h0)
    lane = lax.broadcasted_iota(jnp.int32, (LANE, LANE), 1)
    b2t = b2_ref[...].T
    tiles = [(e, min(256, edges - e)) for e in range(0, edges, 256)]

    pl.semaphore_wait(barrier, len(peers))
    gather_in = Gather(net, place, "in", ins)
    gather_h1 = Gather(net, place, "h1", hid)
    gather_d2 = Gather(net, place, "d2", dts.at[1])
    gather_d1 = Gather(net, place, "d1", dts.at[0])
    gather_in.begin()

    def keep(i, e, w, p):
        p = p.reshape(16, 8, w).sum(0)
        for o in range(0, w, LANE):
            acc[(e + o) // LANE, aligned(i, 8), :] = p[:, o : o + LANE]

    def first(ib):
        w2_copy(ib).wait()
        lhs = []
        for v in range(ROUND):
            i = ib * ROUND + v
            bias = jnp.where(lane == i, b2t, jnp.zeros_like(b2t))
            lhs.append(jnp.concatenate([w2[:, aligned(i, LANE)].T, bias], axis=1))
        lhs = jnp.concatenate(lhs, axis=0)
        for e, w in tiles:
            a = dot(lhs, zaug[:, e : e + w]).astype(BF)
            amat[aligned(ib, ROUND * LANE), e : e + w] = a
            for v in range(ROUND):
                p = a[v * LANE : (v + 1) * LANE].astype(F32) * hs[0, :, e : e + w]
                keep(ib * ROUND + v, e, w, p)

    loop(rounds, first)
    gather_in.along()

    def again(ib):
        for e, w in tiles:
            for v in range(8):
                a = amat[aligned(ib * 8 + v, LANE), e : e + w]
                keep(ib * 8 + v, e, w, a.astype(F32) * hs[1, :, e : e + w])

    def gathered():
        msg = []
        for e in range(tiles5):
            part = acc[e, pl.ds(0, LANE, stride=8), :]
            for q in range(1, 8):
                part = part + acc[e, pl.ds(q, LANE, stride=8), :]
            msg.append(part)
        msg = jnp.concatenate(msg, axis=1)
        total = jnp.zeros((nodes, LANE), F32)
        for piece in split(msg, 3):
            total = total + dot(puts[...], piece, 1, 1)
        return total.astype(BF)

    weights = (wi_ref[...], bi_ref[...], wh_ref[...], bh_ref[...])
    m1 = gathered()
    gates1 = gru_forward(m1, h0, *weights)
    h1 = gates1[0].astype(BF)
    hid[me] = h1
    gather_h1.begin()
    sources(1, h1)
    loop(LANE // 8, again)
    gather_in.across()
    gather_h1.along()
    m2 = gathered()
    gates2 = gru_forward(m2, h1, *weights)
    h2 = gates2[0]
    label = jnp.broadcast_to(ends[2:3, :nodes], (LANE, nodes)).T
    g2 = cot_ref[s] * label
    dgi2, dgh2, dm2, dh2 = gru_backward(g2, h1, gates2, weights[0], weights[2])
    dt2 = dm2.T
    dts[1, me] = dt2
    gather_d2.begin()

    def spread(t, dt):
        got = dot(dt, puts[...])
        dms[t] = got
        dml[:, t * edges : (t + 1) * edges] = got.astype(BF)

    def to_source_tile(t, e):
        def body(ib, total):
            d = dms[t, aligned(ib, 8), e * LANE : (e + 1) * LANE]
            for v in range(8):
                a = amat[aligned(ib * 8 + v, LANE), e * LANE : (e + 1) * LANE].astype(F32)
                total = total + a * d[v : v + 1]
            return total

        return lax.fori_loop(0, LANE // 8, body, jnp.zeros((LANE, LANE), F32))

    def to_nodes(outs):
        back = jnp.concatenate(outs, axis=1)
        total = jnp.zeros((nodes, LANE), F32)
        for piece in split(back, 3):
            total = total + dot(picks[...], piece, 1, 1)
        return total

    spread(1, dt2)
    back2 = [to_source_tile(1, e) for e in range(tiles5)]
    gather_d2.along()
    gather_h1.across()
    d1 = (dh2 + to_nodes(back2)).astype(BF)
    dgi1, dgh1, dm1, dh1 = gru_backward(d1.astype(F32), h0, gates1, weights[0], weights[2])
    dt1 = dm1.T
    dts[0, me] = dt1
    gather_d1.begin()

    half = SMALL_ROWS // 2
    plane_rows = half // place.lines
    own_rows = plane_rows // PLANE
    gwi = dot(m1, dgi1, 0, 0) + dot(m2, dgi2, 0, 0)
    gwh = dot(h0, dgh1, 0, 0) + dot(h1, dgh2, 0, 0)
    for q in range(3):
        small[q * LANE : (q + 1) * LANE] = gwi[:, q * LANE : (q + 1) * LANE]
        small[(3 + q) * LANE : (4 + q) * LANE] = gwh[:, q * LANE : (q + 1) * LANE]
    spread(0, dt1)
    small[6 * LANE : 7 * LANE] = dot(dml[...], hsl[...], 1, 1)
    gbi = dgi1.astype(F32).sum(0, keepdims=True) + dgi2.astype(F32).sum(0, keepdims=True)
    gbh = dgh1.astype(F32).sum(0, keepdims=True) + dgh2.astype(F32).sum(0, keepdims=True)
    rows = [x[:, q * LANE : (q + 1) * LANE] for x in (gbi, gbh) for q in range(3)]
    rows.append(jnp.zeros((SMALL_ROWS - 7 * LANE - 6, LANE), F32))
    small[7 * LANE :] = jnp.concatenate(rows, axis=0)
    net.send(("small", "sib"), small.at[aligned(1 - s, half)], small_in, place.sibling)

    back1 = [to_source_tile(0, e) for e in range(3)]
    gather_d1.along()
    gather_d2.across()
    net.wait(("small", "sib"), small_in, place.sibling)
    small_lo[...] = (small[aligned(s, half), :] + small_in[...]).astype(BF)
    z = lax.div(c, PLANE)
    for line in range(1, place.lines):
        to = lax.div(place.flip(line * PLANE), PLANE)
        net.send(
            ("small", "line", line),
            small_lo.at[aligned(to, plane_rows)],
            small_line.at[line],
            place.peer(line * PLANE),
        )
    back1 += [to_source_tile(0, e) for e in range(3, tiles5)]
    d0 = dh1 + to_nodes(back1)
    gather_in.finish()
    gather_h1.finish()

    zero = s == 0
    swap[0, 0] = jnp.where(zero, h2, h1.astype(F32))
    swap[0, 1] = jnp.where(zero, d1.astype(F32), d0)
    net.send(("swap",), swap.at[0], swap.at[1], place.sibling)

    first_k = (c * 2 + s) * per
    ks = lax.broadcasted_iota(jnp.int32, (8, LANE), 0) + first_k
    sel = (ks == lax.broadcasted_iota(jnp.int32, (8, LANE), 1)).astype(F32)
    w1t = dot(sel.astype(BF), w1_ref[...], 1, 1).astype(BF)
    b1 = jnp.sum(sel * b1_ref[...].astype(F32), axis=1, keepdims=True)
    quarter = nodes // 4
    qn = lax.broadcasted_iota(jnp.int32, (quarter, 256), 0).astype(F32)
    sn = lax.broadcasted_iota(jnp.int32, (nodes, 256), 0).astype(F32)

    def build(blk):
        cols = [ins[blk, e * 32 : (e + 1) * 32, :] for e in range(tiles5)]
        fi = jnp.concatenate(cols, axis=1)
        z = jax.nn.silu(dot(w1t, fi[0:16]) + b1).astype(BF).astype(F32)
        en = fi[16:32].astype(F32)
        pairs = []
        for q in range(4):
            lo = q * LANE
            zq = z[:, lo : lo + 256]
            hit_t = (qn + float(q * quarter)) == en[1:2, lo : lo + 256]
            hit_s = (sn == en[0:1, lo : lo + 256]).astype(F32).astype(BF)
            lhs = [jnp.where(hit_t, zq[k : k + 1], 0.0).astype(BF) for k in range(per)]
            pairs.append(dot(jnp.concatenate(lhs, axis=0), hit_s, 1, 1))
        pairs = jnp.concatenate(split(jnp.concatenate(pairs, axis=0), 2), axis=1)
        h = jnp.concatenate([ins[blk, tiles5 * 32 : tiles5 * 32 + nodes, :], hid[blk]], axis=1)
        got = dot(pairs, jnp.concatenate([h, h], axis=0)).astype(BF)
        for q in range(4):
            at = pl.ds(pl.multiple_of(blk * nodes + q * quarter, quarter), quarter)
            for k in range(per):
                part = got[(q * per + k) * quarter : (q * per + k + 1) * quarter]
                for t in range(2):
                    qst[t, at, k * LANE : (k + 1) * LANE] = part[:, t * LANE : (t + 1) * LANE]

    loop(blocks, build)
    gather_d1.across()
    gather_d2.finish()
    lhs = jnp.concatenate([dts[1, blk] for blk in range(blocks)], axis=1)
    total = dot(lhs, qst[1])
    count = jnp.zeros((1, LANE), F32)
    for blk in range(blocks):
        count = count + ins[blk, 16:32, :].astype(F32)[2:3]
    scale = 1.0 / jnp.sum(count, axis=1, keepdims=True)

    own = small_lo[aligned(z, plane_rows), :].astype(F32)
    for line in range(1, place.lines):
        net.wait(("small", "line", line), small_line.at[line], place.peer(line * PLANE))
        own = own + small_line[line].astype(F32)
    small_line[0] = own.astype(BF)
    q_me = lax.rem(c, PLANE)
    for q in range(1, PLANE):
        to = lax.rem(place.flip(q), PLANE)
        net.send(
            ("small", "plane", q),
            small_line.at[0, aligned(to, own_rows)],
            small_plane.at[q],
            place.peer(q),
        )
    gather_d1.finish()
    lhs = jnp.concatenate([dts[0, blk] for blk in range(blocks)], axis=1)
    total = (total + dot(lhs, qst[0])) * scale
    for k in range(per):
        tmp[pl.ds(k, LANE, stride=per), :] = total[:, k * LANE : (k + 1) * LANE]
    mine[0 : per * LANE] = tmp[...].astype(BF)
    own = small_line[0, aligned(q_me, own_rows), :].astype(F32)
    for q in range(1, PLANE):
        net.wait(("small", "plane", q), small_plane.at[q], place.peer(q))
        own = own + small_plane[q].astype(F32)
    mine[per * LANE : per * LANE + own_rows] = (own * scale).astype(BF)

    size = mine.shape[0]
    halves = (pl.ds(0, size // 2), pl.ds(size // 2, size // 2))
    keep_own = pltpu.make_async_copy(mine, full_out.at[me], own_sem)
    keep_own.start()
    for line in range(1, place.lines):
        net.send(("out", line), mine, full_out.at[me], place.peer(line * PLANE))
    for q in (1, 2):
        for a in range(2):
            net.send(
                ("out", 0, q, a), mine.at[halves[a]], full_out.at[me, halves[a]], place.peer(q)
            )

    def out_line(line):
        mask = line * PLANE
        blk = place.block(mask)
        net.wait(("out", line), full_out.at[blk], place.peer(mask))
        for q in (1, 2):
            for a in range(2):
                ref = full_out.at[blk, halves[a]]
                net.send(("out", line, q, a), ref, ref, place.peer(q))

    def out_cross(line):
        for q, a in ((1, 0), (2, 1)):
            ref = full_out.at[place.block(line * PLANE + q), halves[a]]
            net.wait(("out", line, q, a), ref, place.peer(q))
            net.send(("out", line, 3, a), ref, ref, place.peer(3 - q))

    def out_level(line):
        for q, a in ((1, 1), (2, 0)):
            ref = full_out.at[place.block(line * PLANE + q), halves[a]]
            net.wait(("out", line, q, a), ref, place.peer(q))
        for q, a in ((2, 0), (1, 1)):
            ref = full_out.at[place.block(line * PLANE + 3), halves[a]]
            net.wait(("out", line, 3, a), ref, place.peer(q))
        ref = full_out.at[pl.ds(place.level(line), PLANE)]
        net.send(("out", "sib", line), ref, ref, place.sibling)

    dzacc[...] = jnp.zeros_like(dzacc)

    def back_hidden(ib):
        for t in range(2):
            h = hsl[:, t * edges : (t + 1) * edges].astype(F32)
            d = dms[t, aligned(ib, ROUND), :]
            for v in range(ROUND):
                xbuf[v * LANE : (v + 1) * LANE, t * edges : (t + 1) * edges] = (
                    h * d[v : v + 1]
                ).astype(BF)
        dzacc[...] += dot(w2[:, aligned(ib, ROUND * LANE)], xbuf[...])

    loop(rounds // 4, back_hidden)
    for line in range(1, place.lines):
        out_line(line)
    loop(rounds // 2, lambda ib: back_hidden(ib + rounds // 4))
    keep_own.wait()
    for line in range(place.lines):
        out_cross(line)
    loop(rounds // 4, lambda ib: back_hidden(ib + 3 * rounds // 4))

    zp = zpre_s[...]
    sig = jax.nn.sigmoid(zp)
    slope = sig * (1.0 + zp * (1.0 - sig))
    lhs = jnp.concatenate(
        [feats, jnp.ones((1, edges), BF), jnp.zeros((15, edges), BF)], axis=0
    )
    total = jnp.zeros((32, LANE), F32)
    for t in range(2):
        dzpre = (dzacc[:, t * edges : (t + 1) * edges] * slope).astype(BF)
        total = total + dot(lhs, dzpre, 1, 1)
    w1_io[0] = total[0:24]
    net.send(("w1", "sib"), w1_io.at[0], w1_io.at[1], place.sibling)
    net.wait(("w1", "sib"), w1_io.at[1], place.sibling)
    total = w1_io[0] + w1_io[1]
    w1_io[2] = total
    at = 4
    for line in range(1, place.lines):
        net.send(("w1", "line", line), w1_io.at[2], w1_io.at[at + line], place.peer(line * PLANE))
    for line in range(1, place.lines):
        net.wait(("w1", "line", line), w1_io.at[at + line], place.peer(line * PLANE))
        total = total + w1_io[at + line]
    w1_io[3] = total
    at += place.lines
    for q in range(1, PLANE):
        net.send(("w1", "plane", q), w1_io.at[3], w1_io.at[at + q], place.peer(q))
    for q in range(1, PLANE):
        net.wait(("w1", "plane", q), w1_io.at[at + q], place.peer(q))
        total = total + w1_io[at + q]
    w1_out[...] = total * scale

    net.wait(("swap",), swap.at[1], place.sibling)
    mine_state = jnp.where(zero, h1.astype(F32), h2)
    mine_grad = jnp.where(zero, d0, d1.astype(F32))
    states_out[0] = jnp.where(zero, mine_state, swap[1, 0])
    states_out[1] = jnp.where(zero, swap[1, 0], mine_state)
    grads_out[0] = jnp.where(zero, mine_grad, swap[1, 1])
    grads_out[1] = jnp.where(zero, swap[1, 1], mine_grad)
    for line in range(place.lines):
        out_level(line)
    for line in range(place.lines):
        first = place.level(line) + (1 - 2 * s) * parts
        net.wait(("out", "sib", line), full_out.at[pl.ds(first, PLANE)], place.sibling)
    net.drain()


def final_kernel(a_ref, b_ref, sm_ref, w1_ref, st_ref, sg_ref, w2_out, b2_out, wi_out, bi_out,
                 wh_out, bh_out, gw1_out, gb1_out, st_out, sg_out):
    low = lax.broadcasted_iota(jnp.int32, (1, 8, LANE), 1) < 4
    rows = b2_out.shape[0] * 4
    a = a_ref[0, :rows].astype(F32).reshape(rows // 8, 8, LANE)
    b = b_ref[0, :rows].astype(F32).reshape(rows // 8, 8, LANE)
    even = jnp.where(low, a, pltpu.roll(b, 4, 1))
    odd = jnp.where(low, pltpu.roll(a, 4, 1), b)
    for p in range(rows // 8):
        w2_out[:, (2 * p) * LANE : (2 * p + 1) * LANE] = even[p]
        w2_out[:, (2 * p + 1) * LANE : (2 * p + 2) * LANE] = odd[p]

    @pl.when(pl.program_id(0) == 0)
    def _():
        own = sm_ref.shape[1]
        x = sm_ref[...].astype(F32).reshape(-1, LANE)
        for q in range(3):
            cols = slice(q * LANE, (q + 1) * LANE)
            wi_out[:, cols] = x[q * LANE : (q + 1) * LANE]
            wh_out[:, cols] = x[(3 + q) * LANE : (4 + q) * LANE]
            bi_out[:, cols] = x[7 * LANE + q : 7 * LANE + q + 1]
            bh_out[:, cols] = x[7 * LANE + 3 + q : 7 * LANE + 4 + q]
        b2_out[...] = x[6 * LANE : 7 * LANE]
        gw1_out[...] = w1_ref[0:16]
        gb1_out[...] = w1_ref[16:17]
        st_out[...] = st_ref[...]
        sg_out[...] = sg_ref[...]


def shards(
    node_input, edge_input, edge_source, edge_target, edge_valid, node_labeled,
    edge_w1, edge_b1, edge_w2, edge_b2, gru_wi, gru_bi, gru_wh, gru_bh, state_cot,
):
    micro, nodes, width = node_input.shape
    edges = edge_input.shape[2]
    parts = lax.axis_size("dp")
    blocks = 2 * parts
    per = width // blocks
    lines = parts // PLANE
    half = SMALL_ROWS // 2
    plane_rows = half // lines
    own_rows = plane_rows // PLANE
    size = width * per + own_rows
    vm = pl.BlockSpec(memory_space=VMEM)
    hbm = pl.BlockSpec(memory_space=pl.ANY)
    sds = jax.ShapeDtypeStruct
    full, states, grads, gw1 = pl.pallas_call(
        main_kernel,
        out_shape=(
            sds((blocks, size, width), BF), sds((2, nodes, width), F32),
            sds((2, nodes, width), F32), sds((24, width), F32),
        ),
        in_specs=[vm] * 8 + [hbm] + [vm] * 6,
        out_specs=[hbm, vm, vm, vm],
        scratch_shapes=[
            VMEM((width, width * width), BF), VMEM((width * width, edges), BF),
            VMEM((edges // LANE, 8 * width, LANE), F32), VMEM((2 * width, edges), BF),
            VMEM((width, edges), F32), VMEM((2, width, edges), F32),
            VMEM((width, 2 * edges), BF), VMEM((2, width, edges), F32),
            VMEM((width, 2 * edges), BF), VMEM((ROUND * width, 2 * edges), BF),
            VMEM((width, 2 * edges), F32), VMEM((nodes, edges), BF), VMEM((nodes, edges), BF),
            VMEM((blocks, 32 * (edges // LANE) + nodes, LANE), BF),
            VMEM((blocks, nodes, width), BF), VMEM((2, blocks, width, nodes), BF),
            VMEM((2, blocks * nodes, per * width), BF), VMEM((width * per, width), F32),
            VMEM((size, width), BF), VMEM((SMALL_ROWS, width), F32), VMEM((half, width), F32),
            VMEM((half, width), BF), VMEM((lines, plane_rows, width), BF),
            VMEM((PLANE, own_rows, width), BF), VMEM((4 + lines + PLANE, 24, width), F32),
            VMEM((2, 2, nodes, width), F32),
            pltpu.SemaphoreType.DMA((width // ROUND,)), pltpu.SemaphoreType.DMA,
            pltpu.SemaphoreType.DMA((SEMS,)), pltpu.SemaphoreType.DMA((SEMS,)),
        ],
        compiler_params=pltpu.CompilerParams(
            collective_id=0, has_side_effects=True, vmem_limit_bytes=62 * 2**20
        ),
    )(
        node_input, edge_input, edge_source, edge_target, edge_valid, node_labeled,
        edge_w1, edge_b1.reshape(1, -1), edge_w2, edge_b2.reshape(width, width),
        gru_wi, gru_bi.reshape(1, -1), gru_wh, gru_bh.reshape(1, -1), state_cot,
    )

    def whole(*shape):
        return pl.BlockSpec(shape, lambda c: (0,) * len(shape))

    small = full[:, width * per :, :]
    w2, b2, wi, bi, wh, bh, w1, b1, states, grads = pl.pallas_call(
        final_kernel,
        grid=(parts,),
        out_shape=(
            sds((width, width * width), F32), sds((width, width), F32),
            sds((width, 3 * width), F32), sds((1, 3 * width), F32),
            sds((width, 3 * width), F32), sds((1, 3 * width), F32),
            sds((16, width), F32), sds((1, width), F32),
            sds((2, nodes, width), F32), sds((2, nodes, width), F32),
        ),
        in_specs=[
            pl.BlockSpec((1, size, width), lambda c: (c, 0, 0)),
            pl.BlockSpec((1, size, width), lambda c: (c + parts, 0, 0)),
            whole(blocks, own_rows, width), whole(24, width),
            whole(2, nodes, width), whole(2, nodes, width),
        ],
        out_specs=(
            pl.BlockSpec((2 * per, width * width), lambda c: (c, 0)), whole(width, width),
            whole(width, 3 * width), whole(1, 3 * width), whole(width, 3 * width),
            whole(1, 3 * width), whole(16, width), whole(1, width),
            whole(2, nodes, width), whole(2, nodes, width),
        ),
    )(full, full, small, gw1, states, grads)
    return (
        states[None], grads[None], w1, b1.reshape(-1), w2, b2.reshape(-1),
        wi, bi.reshape(-1), wh, bh.reshape(-1),
    )


EDGE_BLOCK = 128


def passed_along(value, axis, steps):
    count = lax.axis_size(axis)
    leading, last = (max(0, -steps), min(count, count - steps))
    return lax.ppermute(value, axis, [(source, source + steps) for source in range(leading, last)])


def split_blocks(feats, source, target, valid, block):
    count = feats.shape[1] // block
    return (
        feats.reshape(feats.shape[0], count, block).transpose(1, 0, 2),
        source.reshape(count, block),
        target.reshape(count, block),
        valid.reshape(count, block),
    )


def block_front(feats_b, source_b, weights, state_low):
    width = state_low.shape[1]
    zpre = jnp.dot(feats_b.T, weights[0], preferred_element_type=jnp.float32) + weights[1].astype(
        jnp.float32
    )
    z_low = jax.nn.silu(zpre).astype(jnp.bfloat16)
    amat = (
        jnp.dot(z_low, weights[2], preferred_element_type=jnp.float32)
        + weights[3].astype(jnp.float32)
    ).astype(jnp.bfloat16)
    amat = amat.reshape(-1, width, width)
    node_ids = lax.iota(jnp.int32, state_low.shape[0])
    pick = (source_b[:, None] == node_ids[None, :]).astype(jnp.bfloat16)
    h_source = jnp.dot(pick, state_low, preferred_element_type=jnp.float32).astype(jnp.bfloat16)
    return (zpre, z_low, amat, h_source)


def target_table(target_b, valid_b, nodes):
    node_ids = lax.iota(jnp.int32, nodes)
    return ((target_b[:, None] == node_ids[None, :]) & (valid_b[:, None] > 0)).astype(jnp.bfloat16)


def forward_messages(state_low, blocks, weights):
    nodes, width = state_low.shape

    def add(total, pieces):
        feats_b, source_b, target_b, valid_b = pieces
        _, _, amat, h_source = block_front(feats_b, source_b, weights, state_low)
        message = jnp.einsum("eij,ej->ei", amat, h_source, preferred_element_type=jnp.float32)
        message = message * (valid_b > 0).astype(jnp.float32)[:, None]
        return (total + jax.ops.segment_sum(message, target_b, num_segments=nodes), None)

    summed, _ = lax.scan(add, jnp.zeros((nodes, width), jnp.float32), blocks)
    return summed


def gru_gates(gathered_low, state_low, weights):
    width = state_low.shape[1]
    gate_in = jnp.dot(gathered_low, weights[4], preferred_element_type=jnp.float32) + weights[
        5
    ].astype(jnp.float32)
    gate_state = jnp.dot(state_low, weights[6], preferred_element_type=jnp.float32) + weights[
        7
    ].astype(jnp.float32)
    reset = jax.nn.sigmoid(gate_in[:, :width] + gate_state[:, :width])
    update = jax.nn.sigmoid(gate_in[:, width : 2 * width] + gate_state[:, width : 2 * width])
    candidate = jnp.tanh(gate_in[:, 2 * width :] + reset * gate_state[:, 2 * width :])
    fresh = (1.0 - update) * candidate + update * state_low.astype(jnp.float32)
    return (fresh, gate_state, reset, update, candidate)


def backward_step(upstream, state_low, gathered_low, blocks, weights):
    nodes, width = state_low.shape
    fresh, gate_state, reset, update, candidate = gru_gates(gathered_low, state_low, weights)
    state = state_low.astype(jnp.float32)
    d_cand = upstream * (1.0 - update)
    d_update = upstream * (state - candidate)
    d_state = upstream * update
    d_npre = d_cand * (1.0 - candidate * candidate)
    d_upre = d_update * update * (1.0 - update)
    d_rpre = d_npre * gate_state[:, 2 * width :] * reset * (1.0 - reset)
    d_in = jnp.concatenate([d_rpre, d_upre, d_npre], axis=1).astype(jnp.bfloat16)
    d_hid = jnp.concatenate([d_rpre, d_upre, d_npre * reset], axis=1).astype(jnp.bfloat16)
    grad_wi = jnp.dot(gathered_low.T, d_in, preferred_element_type=jnp.float32)
    grad_bi = jnp.sum(d_in.astype(jnp.float32), axis=0)
    grad_wh = jnp.dot(state_low.T, d_hid, preferred_element_type=jnp.float32)
    grad_bh = jnp.sum(d_hid.astype(jnp.float32), axis=0)
    d_state = d_state + jnp.dot(d_hid, weights[6].T, preferred_element_type=jnp.float32)
    d_gathered = jnp.dot(d_in, weights[4].T, preferred_element_type=jnp.float32).astype(
        jnp.bfloat16
    )

    def back_block(carry, pieces):
        d_src, grad_w1, grad_b1, grad_w2, grad_b2 = carry
        feats_b, source_b, target_b, valid_b = pieces
        zpre, z_low, amat, h_source = block_front(feats_b, source_b, weights, state_low)
        put = target_table(target_b, valid_b, nodes)
        d_msg = jnp.dot(put, d_gathered, preferred_element_type=jnp.float32).astype(jnp.bfloat16)
        d_amat = d_msg.astype(jnp.float32)[:, :, None] * h_source.astype(jnp.float32)[:, None, :]
        d_amat = d_amat.reshape(d_amat.shape[0], width * width).astype(jnp.bfloat16)
        grad_w2 = grad_w2 + jnp.dot(z_low.T, d_amat, preferred_element_type=jnp.float32)
        grad_b2 = grad_b2 + jnp.sum(d_amat.astype(jnp.float32), axis=0)
        d_z = jnp.dot(d_amat, weights[2].T, preferred_element_type=jnp.float32)
        sig = jax.nn.sigmoid(zpre)
        d_zpre = (d_z * sig * (1.0 + zpre * (1.0 - sig))).astype(jnp.bfloat16)
        grad_w1 = grad_w1 + jnp.dot(feats_b, d_zpre, preferred_element_type=jnp.float32)
        grad_b1 = grad_b1 + jnp.sum(d_zpre.astype(jnp.float32), axis=0)
        d_source = jnp.einsum("eij,ei->ej", amat, d_msg, preferred_element_type=jnp.float32)
        d_src = d_src + jax.ops.segment_sum(d_source, source_b, num_segments=nodes)
        return ((d_src, grad_w1, grad_b1, grad_w2, grad_b2), None)

    start = (
        jnp.zeros((nodes, width), jnp.float32),
        jnp.zeros(weights[0].shape, jnp.float32),
        jnp.zeros(weights[1].shape, jnp.float32),
        jnp.zeros(weights[2].shape, jnp.float32),
        jnp.zeros(weights[3].shape, jnp.float32),
    )
    ends, _ = lax.scan(back_block, start, blocks)
    d_total = d_state + ends[0]
    return (d_total, (ends[1], ends[2], ends[3], ends[4], grad_wi, grad_bi, grad_wh, grad_bh))


def plain_shards(
    node_input,
    edge_input,
    edge_source,
    edge_target,
    edge_valid,
    node_labeled,
    edge_w1,
    edge_b1,
    edge_w2,
    edge_b2,
    gru_wi,
    gru_bi,
    gru_wh,
    gru_bh,
    state_cot,
):
    weights = (edge_w1, edge_b1, edge_w2, edge_b2, gru_wi, gru_bi, gru_wh, gru_bh)
    micro, nodes, width = node_input.shape
    block = min(EDGE_BLOCK, edge_input.shape[2])
    section_id = lax.axis_index("section")
    first = section_id == 0
    count_local = jnp.sum(node_labeled.astype(jnp.float32))

    def batch_blocks(index):
        feats = lax.dynamic_index_in_dim(edge_input, index, 0, keepdims=False)
        source = lax.dynamic_index_in_dim(edge_source, index, 0, keepdims=False)
        target = lax.dynamic_index_in_dim(edge_target, index, 0, keepdims=False)
        valid = lax.dynamic_index_in_dim(edge_valid, index, 0, keepdims=False)
        return split_blocks(feats, source, target, valid, block)

    received = jnp.zeros((nodes, width), jnp.bfloat16)
    saved = []
    states_out = jnp.zeros((micro, nodes, width), jnp.float32)
    for tick in range(micro + 1):
        batch = tick - section_id
        live = (batch >= 0) & (batch < micro)
        index = jnp.clip(batch, 0, micro - 1)
        state_low = jnp.where(first, node_input[min(tick, micro - 1)], received)
        blocks = batch_blocks(index)
        gathered_low = forward_messages(state_low, blocks, weights).astype(jnp.bfloat16)
        fresh = gru_gates(gathered_low, state_low, weights)[0]
        saved.append((state_low, gathered_low))
        sending = fresh.astype(jnp.bfloat16)
        value = jnp.where(first, sending.astype(jnp.float32), fresh)
        states_out = jnp.where(
            live, lax.dynamic_update_index_in_dim(states_out, value, index, 0), states_out
        )
        if tick < micro:
            received = passed_along(sending, "section", 1)
    grad_received = jnp.zeros((nodes, width), jnp.bfloat16)
    grads_out = jnp.zeros((micro, nodes, width), jnp.float32)
    totals = tuple((jnp.zeros(w.shape, jnp.float32) for w in weights))
    for tick in range(micro + 1):
        batch = micro - tick - section_id
        live = (batch >= 0) & (batch < micro)
        index = jnp.clip(batch, 0, micro - 1)
        state_low, gathered_low = saved[micro - tick]
        labels = lax.dynamic_index_in_dim(node_labeled, index, 0, keepdims=False).astype(
            jnp.float32
        )
        top = lax.dynamic_index_in_dim(state_cot, index, 0, keepdims=False) * labels[:, None]
        upstream = jnp.where(first, grad_received.astype(jnp.float32), top)
        d_total, terms = backward_step(
            upstream, state_low, gathered_low, batch_blocks(index), weights
        )
        totals = tuple((acc + jnp.where(live, term, 0.0) for acc, term in zip(totals, terms)))
        sending = d_total.astype(jnp.bfloat16)
        value = jnp.where(first, d_total, sending.astype(jnp.float32))
        grads_out = jnp.where(
            live, lax.dynamic_update_index_in_dim(grads_out, value, index, 0), grads_out
        )
        if tick < micro:
            grad_received = passed_along(sending, "section", -1)
    count_total = lax.psum(count_local, "dp")
    summed = lax.psum(
        (totals[0], totals[1], totals[2], totals[3], totals[4], totals[5], totals[6], totals[7]),
        ("section", "dp"),
    )
    scaled = [g / count_total for g in summed]
    return (
        states_out[None],
        grads_out[None],
        scaled[0],
        scaled[1],
        scaled[2],
        scaled[3],
        scaled[4],
        scaled[5],
        scaled[6],
        scaled[7],
    )


def solution(mesh):
    placed = (
        P(None, "dp", None), P(None, None, "dp"), P(None, "dp"), P(None, "dp"), P(None, "dp"),
        P(None, "dp"), P(), P(), P(), P(), P(), P(), P(), P(), P(None, "dp", None),
    )
    fits = LANE % (2 * mesh.shape["dp"]) == 0
    return jax.shard_map(
        shards if fits else plain_shards,
        mesh=mesh,
        in_specs=placed,
        out_specs=(P("section", None, "dp", None), P("section", None, "dp", None)) + (P(),) * 8,
        check_vma=False,
    )
```

```python
import functools

import jax
import jax.numpy as jnp
from jax import lax
from jax.experimental import pallas as pl
from jax.experimental.pallas import tpu as pltpu
from jax.sharding import PartitionSpec as P

BF, F32 = jnp.bfloat16, jnp.float32
VMEM = pltpu.VMEM
LANE = 128
ROUND = 16
SMALL_ROWS = 1024
PLANE = 4
SEMS = 160


def dot(a, b, ca=1, cb=0):
    return lax.dot_general(a, b, (((ca,), (cb,)), ((), ())), preferred_element_type=F32)


def split(x, parts):
    out = []
    for _ in range(parts - 1):
        piece = x.astype(BF)
        out.append(piece)
        x = x - piece.astype(F32)
    out.append(x.astype(BF))
    return out


def loop(count, body):
    def step(i, carry):
        body(i)
        return carry

    lax.fori_loop(0, count, step, 0)


def aligned(i, size):
    return pl.ds(pl.multiple_of(i * size, size), size)


def edge_tables(ends, nodes):
    ids = lax.broadcasted_iota(jnp.int32, (nodes, ends.shape[1]), 0).astype(F32)
    pick = (ids == ends[0:1]).astype(F32).astype(BF)
    put = (ids == ends[1:2]).astype(F32).astype(BF)
    return pick, put


def pack_ends(src_ref, tgt_ref, valid_ref, lab_ref, s):
    row = pl.ds(s, 1)
    src = src_ref[row, :].astype(F32)
    tgt = jnp.where(valid_ref[row, :] > 0, tgt_ref[row, :], -1).astype(F32)
    lab = lab_ref[row, :].astype(F32)
    edges, nodes = src.shape[1], lab.shape[1]
    lab = jnp.concatenate([lab, jnp.zeros((1, edges - nodes), F32)], axis=1)
    return jnp.concatenate([src, tgt, lab, jnp.zeros((13, edges), F32)], axis=0)


def edge_hidden(feats, w1, b1):
    bias = jnp.broadcast_to(b1.astype(F32), (LANE, LANE)).T[:, 0:1]
    return dot(w1, feats, 0, 0) + bias


def gru_forward(m, h, wi, bi, wh, bh):
    w = h.shape[1]
    gi = dot(m, wi) + bi.astype(F32)
    gh = dot(h, wh) + bh.astype(F32)
    r = jax.nn.sigmoid(gi[:, :w] + gh[:, :w])
    u = jax.nn.sigmoid(gi[:, w : 2 * w] + gh[:, w : 2 * w])
    n = jnp.tanh(gi[:, 2 * w :] + r * gh[:, 2 * w :])
    fresh = (1.0 - u) * n + u * h.astype(F32)
    return fresh, gh[:, 2 * w :], r, u, n


def gru_backward(g, h, gates, wi, wh):
    _, ghn, r, u, n = gates
    dn = g * (1.0 - u)
    du = g * (h.astype(F32) - n)
    dnpre = dn * (1.0 - n * n)
    dupre = du * u * (1.0 - u)
    drpre = dnpre * ghn * r * (1.0 - r)
    dgi = jnp.concatenate([drpre, dupre, dnpre], axis=1).astype(BF)
    dgh = jnp.concatenate([drpre, dupre, dnpre * r], axis=1).astype(BF)
    dm = dot(dgi, wi, 1, 1).astype(BF)
    dh = g * u + dot(dgh, wh, 1, 1)
    return dgi, dgh, dm, dh


class Net:
    def __init__(self, send_sems, recv_sems):
        self.send_sems, self.recv_sems = send_sems, recv_sems
        self.slots, self.sent = {}, []

    def slot(self, key):
        return self.slots.setdefault(key, len(self.slots))

    def send(self, key, src, dst, peer):
        copy = pltpu.make_async_remote_copy(
            src_ref=src,
            dst_ref=dst,
            send_sem=self.send_sems.at[len(self.sent)],
            recv_sem=self.recv_sems.at[self.slot(key)],
            device_id=peer,
            device_id_type=pl.DeviceIdType.MESH,
        )
        copy.start()
        self.sent.append(copy)

    def wait(self, key, region, peer):
        pltpu.make_async_remote_copy(
            src_ref=region,
            dst_ref=region,
            send_sem=self.send_sems.at[0],
            recv_sem=self.recv_sems.at[self.slot(key)],
            device_id=peer,
            device_id_type=pl.DeviceIdType.MESH,
        ).wait_recv()

    def drain(self):
        for copy in self.sent:
            copy.wait_send()


class Place:
    def __init__(self, parts):
        self.parts, self.plane = parts, PLANE
        self.lines = parts // PLANE
        self.s, self.c = lax.axis_index("section"), lax.axis_index("dp")
        self.sibling = {"section": 1 - self.s}

    def flip(self, mask):
        at, bit = self.c, 1
        while bit <= mask:
            if mask & bit:
                at = at + bit * (1 - 2 * lax.rem(lax.div(self.c, bit), 2))
            bit *= 2
        return at

    def peer(self, mask):
        return {"dp": self.flip(mask)}

    def block(self, mask):
        return self.s * self.parts + self.flip(mask)

    def spot(self, line):
        return self.s * self.lines + lax.div(self.flip(line * self.plane), self.plane)

    def level(self, line):
        own = lax.div(self.flip(line * self.plane), self.plane) * self.plane
        return self.s * self.parts + own


class LineGather:
    def __init__(self, net, place, name, buf):
        self.net, self.place, self.name, self.buf = net, place, name, buf

    def block(self, line):
        return self.buf.at[self.place.spot(line)]

    def begin(self):
        p = self.place
        for line in range(1, p.lines):
            ref = self.block(0)
            self.net.send((self.name, line), ref, ref, p.peer(line * PLANE))

    def middle(self):
        p = self.place
        for line in range(1, p.lines):
            self.net.wait((self.name, line), self.block(line), p.peer(line * PLANE))
        ref = self.buf.at[pl.ds(p.s * p.lines, p.lines)]
        self.net.send((self.name, "sib"), ref, ref, p.sibling)

    def finish(self):
        p = self.place
        ref = self.buf.at[pl.ds((1 - p.s) * p.lines, p.lines)]
        self.net.wait((self.name, "sib"), ref, p.sibling)


def main_kernel(
    x_ref, f_ref, src_ref, tgt_ref, val_ref, lab_ref, w1_ref, b1_ref, w2_hbm, b2_ref,
    wi_ref, bi_ref, wh_ref, bh_ref, cot_ref,
    full_out, states_out, grads_out, w1_out,
    w2, amat, acc, zaug, zpre_s, hs, hsl, dms, dml, dzacc, picks, puts,
    ins, hid, dts, qst, zall, part, sums, tmp, small, small_in, small_lo, small_line, small_plane,
    w1_io, swap, w2_sems, send_sems, recv_sems,
):
    edges, nodes = f_ref.shape[2], x_ref.shape[1]
    tiles5 = edges // LANE
    parts = full_out.shape[0] // 2
    blocks = 2 * parts
    per = LANE // blocks
    place = Place(parts)
    net = Net(send_sems, recv_sems)
    s, c = place.s, place.c
    me = place.block(0)
    here = place.spot(0)
    group = 2 * place.lines
    rounds = LANE // ROUND

    barrier = pltpu.get_barrier_semaphore()
    peers = [place.peer(q) for q in range(1, PLANE)]
    peers += [place.peer(line * PLANE) for line in range(1, place.lines)] + [place.sibling]
    for peer in peers:
        pl.semaphore_signal(
            barrier, inc=1, device_id=peer, device_id_type=pl.DeviceIdType.MESH
        )

    def w2_copy(ib):
        part = aligned(ib, ROUND * LANE)
        return pltpu.make_async_copy(w2_hbm.at[:, part], w2.at[:, part], w2_sems.at[ib])

    for ib in range(rounds):
        w2_copy(ib).start()

    feats = f_ref[s]
    ends = pack_ends(src_ref, tgt_ref, val_ref, lab_ref, s)
    h0 = x_ref[s]
    for e in range(tiles5):
        ins[here, e * 16 : (e + 1) * 16, :] = feats[:, e * LANE : (e + 1) * LANE]
    table = [ends[q : q + 1, e * LANE : (e + 1) * LANE] for q in range(2) for e in range(tiles5)]
    table.append(ends[2:3, :nodes])
    table.append(jnp.zeros((16 - len(table), LANE), F32))
    ins[here, tiles5 * 16 : (tiles5 + 1) * 16, :] = jnp.concatenate(table, axis=0).astype(BF)
    hid[0, here] = h0
    pick, put = edge_tables(ends, nodes)
    picks[...] = pick
    puts[...] = put
    zpre = edge_hidden(feats, w1_ref[...], b1_ref[...])
    zpre_s[...] = zpre
    zaug[0:LANE] = jax.nn.silu(zpre).astype(BF)
    zaug[LANE : 2 * LANE] = jnp.ones((LANE, edges), BF)

    def sources(t, h):
        got = dot(h, picks[...], 0, 0)
        hs[t] = got
        hsl[:, t * edges : (t + 1) * edges] = got.astype(BF)

    sources(0, h0)
    lane = lax.broadcasted_iota(jnp.int32, (LANE, LANE), 1)
    b2t = b2_ref[...].T
    tiles = [(e, min(256, edges - e)) for e in range(0, edges, 256)]

    gather_in = LineGather(net, place, "in", ins)
    gather_h0 = LineGather(net, place, "h0", hid.at[0])
    gather_h1 = LineGather(net, place, "h1", hid.at[1])
    gather_d2 = LineGather(net, place, "d2", dts.at[1])
    gather_d1 = LineGather(net, place, "d1", dts.at[0])

    def keep(i, e, w, p):
        p = p.reshape(16, 8, w).sum(0)
        for o in range(0, w, LANE):
            acc[(e + o) // LANE, aligned(i, 8), :] = p[:, o : o + LANE]

    def first(ib):
        w2_copy(ib).wait()
        lhs = []
        for v in range(ROUND):
            i = ib * ROUND + v
            bias = jnp.where(lane == i, b2t, jnp.zeros_like(b2t))
            lhs.append(jnp.concatenate([w2[:, aligned(i, LANE)].T, bias], axis=1))
        lhs = jnp.concatenate(lhs, axis=0)
        for e, w in tiles:
            a = dot(lhs, zaug[:, e : e + w]).astype(BF)
            amat[aligned(ib, ROUND * LANE), e : e + w] = a
            for v in range(ROUND):
                p = a[v * LANE : (v + 1) * LANE].astype(F32) * hs[0, :, e : e + w]
                keep(ib * ROUND + v, e, w, p)

    loop(rounds - 2, first)
    pl.semaphore_wait(barrier, len(peers))
    gather_in.begin()
    gather_h0.begin()
    loop(2, lambda ib: first(ib + rounds - 2))

    def again(ib):
        for e, w in tiles:
            for v in range(8):
                a = amat[aligned(ib * 8 + v, LANE), e : e + w]
                keep(ib * 8 + v, e, w, a.astype(F32) * hs[1, :, e : e + w])

    def gathered():
        msg = []
        for e in range(tiles5):
            part = acc[e, pl.ds(0, LANE, stride=8), :]
            for q in range(1, 8):
                part = part + acc[e, pl.ds(q, LANE, stride=8), :]
            msg.append(part)
        msg = jnp.concatenate(msg, axis=1)
        total = jnp.zeros((nodes, LANE), F32)
        for piece in split(msg, 3):
            total = total + dot(puts[...], piece, 1, 1)
        return total.astype(BF)

    weights = (wi_ref[...], bi_ref[...].reshape(1, -1), wh_ref[...], bh_ref[...].reshape(1, -1))
    m1 = gathered()
    gates1 = gru_forward(m1, h0, *weights)
    h1 = gates1[0].astype(BF)
    hid[1, here] = h1
    gather_h1.begin()
    sources(1, h1)
    loop(LANE // 8, again)
    gather_in.middle()
    gather_h0.middle()
    m2 = gathered()
    gates2 = gru_forward(m2, h1, *weights)
    h2 = gates2[0]
    label = jnp.broadcast_to(ends[2:3, :nodes], (LANE, nodes)).T
    g2 = cot_ref[s] * label
    dgi2, dgh2, dm2, dh2 = gru_backward(g2, h1, gates2, weights[0], weights[2])
    dt2 = dm2.T
    dts[1, here] = dt2
    gather_d2.begin()

    def spread(t, dt):
        got = dot(dt, puts[...])
        dms[t] = got
        dml[:, t * edges : (t + 1) * edges] = got.astype(BF)

    def to_source_tile(t, e):
        def body(ib, total):
            d = dms[t, aligned(ib, 8), e * LANE : (e + 1) * LANE]
            for v in range(8):
                a = amat[aligned(ib * 8 + v, LANE), e * LANE : (e + 1) * LANE].astype(F32)
                total = total + a * d[v : v + 1]
            return total

        return lax.fori_loop(0, LANE // 8, body, jnp.zeros((LANE, LANE), F32))

    def to_nodes(outs):
        back = jnp.concatenate(outs, axis=1)
        total = jnp.zeros((nodes, LANE), F32)
        for piece in split(back, 3):
            total = total + dot(picks[...], piece, 1, 1)
        return total

    spread(1, dt2)
    back2 = [to_source_tile(1, e) for e in range(tiles5)]
    gather_h1.middle()
    d1 = (dh2 + to_nodes(back2)).astype(BF)
    dgi1, dgh1, dm1, dh1 = gru_backward(d1.astype(F32), h0, gates1, weights[0], weights[2])
    dt1 = dm1.T
    dts[0, here] = dt1
    gather_d1.begin()
    gather_d2.middle()

    gather_in.finish()
    gather_h0.finish()
    gather_h1.finish()
    dzacc[...] = jnp.zeros_like(dzacc)

    def back_hidden(ib):
        total = dzacc[...]
        for a in range(2):
            for t in range(2):
                h = hsl[:, t * edges : (t + 1) * edges].astype(F32)
                d = dms[t, aligned(ib * 2 + a, 8), :]
                for v in range(8):
                    qst[a, v * LANE : (v + 1) * LANE, t * edges : (t + 1) * edges] = (
                        h * d[v : v + 1]
                    ).astype(BF)
            total = total + dot(w2[:, aligned(ib * 2 + a, 8 * LANE)], qst[a, :, 0 : 2 * edges])
        dzacc[...] = total

    units = PLANE * per
    ks = lax.broadcasted_iota(jnp.int32, (units, LANE), 0)
    ks = (lax.div(ks, per) * 2 + s) * per + lax.rem(ks, per) + lax.div(c, PLANE) * (2 * units)
    sel = (ks == lax.broadcasted_iota(jnp.int32, (units, LANE), 1)).astype(F32)
    w1t = dot(sel.astype(BF), w1_ref[...], 1, 1).astype(BF)
    b1 = jnp.sum(sel * b1_ref[...].astype(F32), axis=1, keepdims=True)
    quarter = nodes // 4
    qn = lax.broadcasted_iota(jnp.int32, (quarter, 256), 0).astype(F32)
    sn = lax.broadcasted_iota(jnp.int32, (nodes, 256), 0).astype(F32)

    def hidden(blk):
        cols = [ins[blk, e * 16 : (e + 1) * 16, :] for e in range(tiles5)]
        z = jax.nn.silu(dot(w1t, jnp.concatenate(cols, axis=1)) + b1)
        zall[blk] = z.astype(BF).astype(F32)

    def build(blk):
        z = zall[blk]
        en = ins[blk, tiles5 * 16 : (tiles5 + 1) * 16, :].astype(F32)
        pairs = []
        for q in range(4):
            lo = q * LANE
            zq = z[:, lo : lo + 256]
            src = jnp.concatenate([en[q : q + 1], en[q + 1 : q + 2]], axis=1)
            tgt = jnp.concatenate(
                [en[tiles5 + q : tiles5 + q + 1], en[tiles5 + q + 1 : tiles5 + q + 2]], axis=1
            )
            hit_t = (qn + float(q * quarter)) == tgt
            hit_s = (sn == src).astype(F32).astype(BF)
            lhs = [jnp.where(hit_t, zq[k : k + 1], 0.0).astype(BF) for k in range(units)]
            pairs.append(dot(jnp.concatenate(lhs, axis=0), hit_s, 1, 1))
        pairs = jnp.concatenate(split(jnp.concatenate(pairs, axis=0), 2), axis=1)
        h = jnp.concatenate([hid[0, blk], hid[1, blk]], axis=1)
        got = dot(pairs, jnp.concatenate([h, h], axis=0)).astype(BF)
        for q in range(4):
            at = pl.ds(pl.multiple_of(blk * nodes + q * quarter, quarter), quarter)
            for k in range(units):
                part = got[(q * units + k) * quarter : (q * units + k + 1) * quarter]
                for t in range(2):
                    qst[t, at, k * LANE : (k + 1) * LANE] = part[:, t * LANE : (t + 1) * LANE]

    for blk in range(group):
        hidden(blk)
    loop(group, build)
    gather_d1.middle()
    gather_d2.finish()
    lhs = jnp.concatenate([dts[1, blk] for blk in range(group)], axis=1)
    part[...] = dot(lhs, qst[1])
    gather_d1.finish()
    lhs = jnp.concatenate([dts[0, blk] for blk in range(group)], axis=1)
    part[...] += dot(lhs, qst[0])
    count = jnp.zeros((1, LANE), F32)
    for blk in range(group):
        count = count + ins[blk, tiles5 * 16 : (tiles5 + 1) * 16, :].astype(F32)[10:11]
    count = jnp.concatenate([count, jnp.zeros((15, LANE), F32)], axis=0)
    for p in range(PLANE):
        for k in range(per):
            col = (p * per + k) * LANE
            tmp[pl.ds(k, LANE, stride=per), :] = part[:, col : col + LANE]
        sums[0, p, 0 : per * LANE] = tmp[...].astype(BF)
        sums[0, p, per * LANE :] = count.astype(BF)
    for q in range(1, PLANE):
        to = lax.rem(place.flip(q), PLANE)
        net.send(("sums", q), sums.at[0, to], sums.at[1, q], place.peer(q))

    half = SMALL_ROWS // 2
    plane_rows = half // place.lines
    own_rows = plane_rows // PLANE
    gwi = dot(m1, dgi1, 0, 0) + dot(m2, dgi2, 0, 0)
    gwh = dot(h0, dgh1, 0, 0) + dot(h1, dgh2, 0, 0)
    for q in range(3):
        small[q * LANE : (q + 1) * LANE] = gwi[:, q * LANE : (q + 1) * LANE]
        small[(3 + q) * LANE : (4 + q) * LANE] = gwh[:, q * LANE : (q + 1) * LANE]
    spread(0, dt1)
    small[6 * LANE : 7 * LANE] = dot(dml[...], hsl[...], 1, 1)
    gbi = dgi1.astype(F32).sum(0, keepdims=True) + dgi2.astype(F32).sum(0, keepdims=True)
    gbh = dgh1.astype(F32).sum(0, keepdims=True) + dgh2.astype(F32).sum(0, keepdims=True)
    rows = [x[:, q * LANE : (q + 1) * LANE] for x in (gbi, gbh) for q in range(3)]
    rows.append(jnp.zeros((SMALL_ROWS - 7 * LANE - 6, LANE), F32))
    small[7 * LANE :] = jnp.concatenate(rows, axis=0)
    net.send(("small", "sib"), small.at[aligned(1 - s, half)], small_in, place.sibling)

    back1 = [to_source_tile(0, e) for e in range(2)]
    net.wait(("small", "sib"), small_in, place.sibling)
    small_lo[...] = (small[aligned(s, half), :] + small_in[...]).astype(BF)
    z = lax.div(c, PLANE)
    for line in range(1, place.lines):
        to = lax.div(place.flip(line * PLANE), PLANE)
        net.send(
            ("small", "line", line),
            small_lo.at[aligned(to, plane_rows)],
            small_line.at[line],
            place.peer(line * PLANE),
        )
    back1.append(to_source_tile(0, 2))
    own = small_lo[aligned(z, plane_rows), :].astype(F32)
    for line in range(1, place.lines):
        net.wait(("small", "line", line), small_line.at[line], place.peer(line * PLANE))
        own = own + small_line[line].astype(F32)
    small_line[0] = own.astype(BF)
    q_me = lax.rem(c, PLANE)
    for q in range(1, PLANE):
        to = lax.rem(place.flip(q), PLANE)
        net.send(
            ("small", "plane", q),
            small_line.at[0, aligned(to, own_rows)],
            small_plane.at[q],
            place.peer(q),
        )
    total = sums[0, q_me].astype(F32)
    for q in range(1, PLANE):
        net.wait(("sums", q), sums.at[1, q], place.peer(q))
        total = total + sums[1, q].astype(F32)
    scale = 1.0 / jnp.sum(total[per * LANE : per * LANE + 1], axis=1, keepdims=True)
    full_out[me, 0 : per * LANE] = (total[0 : per * LANE] * scale).astype(BF)

    size = full_out.shape[1]
    mine = full_out.at[me]
    tail = size // 5 // 16 * 16
    cut = (size - tail) // 32 * 16
    halves = (pl.ds(0, cut), pl.ds(cut, size - tail - cut))
    head, last = pl.ds(0, size - tail), pl.ds(size - tail, tail)
    net.send(("out", 1), mine.at[head], full_out.at[me, head], place.peer(PLANE))
    for q, a in ((1, 0), (2, 1), (1, 1), (2, 0)):
        net.send(("out", 0, q, a), mine.at[halves[a]], full_out.at[me, halves[a]], place.peer(q))
    for line in range(2, place.lines):
        net.send(("out", line), mine.at[head], full_out.at[me, head], place.peer(line * PLANE))
    back1 += [to_source_tile(0, e) for e in range(3, tiles5)]
    d0 = dh1 + to_nodes(back1)

    zero = s == 0
    swap[0, 0] = jnp.where(zero, h2, h1.astype(F32))
    swap[0, 1] = jnp.where(zero, d1.astype(F32), d0)
    net.send(("swap",), swap.at[0], swap.at[1], place.sibling)
    own = small_line[0, aligned(q_me, own_rows), :].astype(F32)
    for q in range(1, PLANE):
        net.wait(("small", "plane", q), small_plane.at[q], place.peer(q))
        own = own + small_plane[q].astype(F32)
    full_out[me, per * LANE : per * LANE + own_rows] = (own * scale).astype(BF)
    for q in range(1, PLANE):
        net.send(("last", 0, q), mine.at[last], full_out.at[me, last], place.peer(q))

    def out_line(line):
        mask = line * PLANE
        blk = place.block(mask)
        net.wait(("out", line), full_out.at[blk, head], place.peer(mask))
        for q, a in ((1, 0), (2, 1), (1, 1), (2, 0)):
            ref = full_out.at[blk, halves[a]]
            net.send(("out", line, q, a), ref, ref, place.peer(q))

    def out_cross(line):
        for q, a in ((1, 0), (2, 1)):
            ref = full_out.at[place.block(line * PLANE + q), halves[a]]
            net.wait(("out", line, q, a), ref, place.peer(q))
            net.send(("out", line, 3, a), ref, ref, place.peer(3 - q))

    def last_lines():
        for q in range(1, PLANE):
            net.wait(("last", 0, q), full_out.at[place.block(q), last], place.peer(q))
        ref = full_out.at[pl.ds(place.level(0), PLANE), last]
        for line in range(1, place.lines):
            net.send(("last", line), ref, ref, place.peer(line * PLANE))

    def out_level(line):
        for q, a in ((1, 1), (2, 0)):
            ref = full_out.at[place.block(line * PLANE + q), halves[a]]
            net.wait(("out", line, q, a), ref, place.peer(q))
        for q, a in ((2, 0), (1, 1)):
            ref = full_out.at[place.block(line * PLANE + 3), halves[a]]
            net.wait(("out", line, 3, a), ref, place.peer(q))
        ref = full_out.at[pl.ds(place.level(line), PLANE)]
        if line > 0:
            part = full_out.at[pl.ds(place.level(line), PLANE), last]
            net.wait(("last", line), part, place.peer(line * PLANE))
        net.send(("out", "sib", line), ref, ref, place.sibling)

    loop(3, back_hidden)
    out_cross(0)
    loop(2, lambda ib: back_hidden(ib + 3))
    out_line(1)
    last_lines()
    loop(rounds - 5, lambda ib: back_hidden(ib + 5))
    zp = zpre_s[...]
    sig = jax.nn.sigmoid(zp)
    slope = sig * (1.0 + zp * (1.0 - sig))
    lhs = jnp.concatenate(
        [feats, jnp.ones((1, edges), BF), jnp.zeros((15, edges), BF)], axis=0
    )
    total = jnp.zeros((32, LANE), F32)
    for t in range(2):
        dzpre = (dzacc[:, t * edges : (t + 1) * edges] * slope).astype(BF)
        total = total + dot(lhs, dzpre, 1, 1)
    w1_io[0] = total[0:24]
    net.send(("w1", "sib"), w1_io.at[0], w1_io.at[1], place.sibling)
    out_cross(1)
    out_level(0)
    net.wait(("w1", "sib"), w1_io.at[1], place.sibling)
    total = w1_io[0] + w1_io[1]
    w1_io[2] = total
    at = 4
    for line in range(1, place.lines):
        net.send(("w1", "line", line), w1_io.at[2], w1_io.at[at + line], place.peer(line * PLANE))
    net.wait(("swap",), swap.at[1], place.sibling)
    mine_state = jnp.where(zero, h1.astype(F32), h2)
    mine_grad = jnp.where(zero, d0, d1.astype(F32))
    states_out[0] = jnp.where(zero, mine_state, swap[1, 0])
    states_out[1] = jnp.where(zero, swap[1, 0], mine_state)
    grads_out[0] = jnp.where(zero, mine_grad, swap[1, 1])
    grads_out[1] = jnp.where(zero, swap[1, 1], mine_grad)
    for line in range(2, place.lines):
        out_line(line)
    out_level(1)
    for line in range(1, place.lines):
        net.wait(("w1", "line", line), w1_io.at[at + line], place.peer(line * PLANE))
        total = total + w1_io[at + line]
    w1_io[3] = total
    at += place.lines
    for q in range(1, PLANE):
        net.send(("w1", "plane", q), w1_io.at[3], w1_io.at[at + q], place.peer(q))
    for line in range(2, place.lines):
        out_cross(line)
    for q in range(1, PLANE):
        net.wait(("w1", "plane", q), w1_io.at[at + q], place.peer(q))
        total = total + w1_io[at + q]
    w1_out[...] = total * scale
    for line in range(2, place.lines):
        out_level(line)
    for line in range(place.lines):
        first = place.level(line) + (1 - 2 * s) * parts
        net.wait(("out", "sib", line), full_out.at[pl.ds(first, PLANE)], place.sibling)
    net.drain()


def final_kernel(full_ref, w1_ref, st_ref, sg_ref, w2_out, b2_out, wi_out, bi_out, wh_out, bh_out,
                 gw1_out, gb1_out, st_out, sg_out, flat, out_sems):
    blocks = full_ref.shape[0]
    parts = blocks // 2
    width = b2_out.shape[0]
    rows = width * (width // blocks)

    def put(c):
        part = aligned(c, 8)
        return pltpu.make_async_copy(flat.at[part], w2_out.at[part], out_sems.at[c])

    gw1_out[...] = w1_ref[0:16]
    gb1_out[...] = w1_ref[16:17]
    st_out[...] = st_ref[...]
    sg_out[...] = sg_ref[...]
    low = lax.broadcasted_iota(jnp.int32, (1, 8, LANE), 1) < 4

    def place_rows(c):
        a = full_ref[c, :rows].astype(F32).reshape(rows // 8, 8, LANE)
        b = full_ref[c + parts, :rows].astype(F32).reshape(rows // 8, 8, LANE)
        even = jnp.where(low, a, pltpu.roll(b, 4, 1))
        odd = jnp.where(low, pltpu.roll(a, 4, 1), b)
        for p in range(rows // 8):
            flat[aligned(c, 8), (2 * p) * LANE : (2 * p + 1) * LANE] = even[p]
            flat[aligned(c, 8), (2 * p + 1) * LANE : (2 * p + 2) * LANE] = odd[p]
        put(c).start()

    loop(parts, place_rows)
    x = full_ref[:, rows:].astype(F32).reshape(-1, LANE)
    for q in range(3):
        cols = slice(q * LANE, (q + 1) * LANE)
        wi_out[:, cols] = x[q * LANE : (q + 1) * LANE]
        wh_out[:, cols] = x[(3 + q) * LANE : (4 + q) * LANE]
        bi_out[cols] = x[7 * LANE + q]
        bh_out[cols] = x[7 * LANE + 3 + q]
    b2_out[...] = x[6 * LANE : 7 * LANE]
    loop(parts, lambda c: put(c).wait())


def shards(
    node_input, edge_input, edge_source, edge_target, edge_valid, node_labeled,
    edge_w1, edge_b1, edge_w2, edge_b2, gru_wi, gru_bi, gru_wh, gru_bh, state_cot,
):
    micro, nodes, width = node_input.shape
    edges = edge_input.shape[2]
    parts = lax.axis_size("dp")
    blocks = 2 * parts
    per = width // blocks
    lines = parts // PLANE
    group, units = 2 * lines, PLANE * per
    half = SMALL_ROWS // 2
    plane_rows = half // lines
    own_rows = plane_rows // PLANE
    size = width * per + own_rows
    vm = pl.BlockSpec(memory_space=VMEM)
    hbm = pl.BlockSpec(memory_space=pl.ANY)
    sds = jax.ShapeDtypeStruct
    full, states, grads, gw1 = pl.pallas_call(
        main_kernel,
        out_shape=(
            VMEM((blocks, size, width), BF), VMEM((2, nodes, width), F32),
            VMEM((2, nodes, width), F32), VMEM((24, width), F32),
        ),
        in_specs=[vm] * 8 + [hbm] + [vm] * 6,
        out_specs=[vm] * 4,
        scratch_shapes=[
            VMEM((width, width * width), BF), VMEM((width * width, edges), BF),
            VMEM((edges // LANE, 8 * width, LANE), F32), VMEM((2 * width, edges), BF),
            VMEM((width, edges), F32), VMEM((2, width, edges), F32),
            VMEM((width, 2 * edges), BF), VMEM((2, width, edges), F32),
            VMEM((width, 2 * edges), BF),
            VMEM((width, 2 * edges), F32), VMEM((nodes, edges), BF), VMEM((nodes, edges), BF),
            VMEM((group, 16 * (edges // LANE + 1), LANE), BF),
            VMEM((2, group, nodes, width), BF), VMEM((2, group, width, nodes), BF),
            VMEM((2, group * nodes, units * width), BF), VMEM((group, units, edges), F32),
            VMEM((width, units * width), F32),
            VMEM((2, PLANE, per * width + 16, width), BF), VMEM((width * per, width), F32),
            VMEM((SMALL_ROWS, width), F32), VMEM((half, width), F32),
            VMEM((half, width), BF), VMEM((lines, plane_rows, width), BF),
            VMEM((PLANE, own_rows, width), BF), VMEM((4 + lines + PLANE, 24, width), F32),
            VMEM((2, 2, nodes, width), F32),
            pltpu.SemaphoreType.DMA((width // ROUND,)),
            pltpu.SemaphoreType.DMA((SEMS,)), pltpu.SemaphoreType.DMA((SEMS,)),
        ],
        compiler_params=pltpu.CompilerParams(
            collective_id=0, has_side_effects=True, vmem_limit_bytes=57 * 2**20
        ),
    )(
        node_input, edge_input, edge_source, edge_target, edge_valid, node_labeled,
        edge_w1, edge_b1.reshape(1, -1), edge_w2, edge_b2.reshape(width, width),
        gru_wi, gru_bi, gru_wh, gru_bh, state_cot,
    )

    w2, b2, wi, bi, wh, bh, w1, b1, states, grads = pl.pallas_call(
        final_kernel,
        out_shape=(
            sds((width, width * width), F32), sds((width, width), F32),
            sds((width, 3 * width), F32), sds((3 * width,), F32),
            sds((width, 3 * width), F32), sds((3 * width,), F32),
            sds((16, width), F32), sds((1, width), F32),
            sds((2, nodes, width), F32), sds((2, nodes, width), F32),
        ),
        in_specs=[vm] * 4,
        out_specs=[hbm] + [vm] * 9,
        scratch_shapes=[
            VMEM((width, width * width), F32), pltpu.SemaphoreType.DMA((parts,)),
        ],
        compiler_params=pltpu.CompilerParams(vmem_limit_bytes=40 * 2**20),
    )(full, gw1, states, grads)
    return (
        states[None], grads[None], w1, b1.reshape(-1), w2, b2.reshape(-1),
        wi, bi, wh, bh,
    )


EDGE_BLOCK = 128


def passed_along(value, axis, steps):
    count = lax.axis_size(axis)
    leading, last = (max(0, -steps), min(count, count - steps))
    return lax.ppermute(value, axis, [(source, source + steps) for source in range(leading, last)])


def split_blocks(feats, source, target, valid, block):
    count = feats.shape[1] // block
    return (
        feats.reshape(feats.shape[0], count, block).transpose(1, 0, 2),
        source.reshape(count, block),
        target.reshape(count, block),
        valid.reshape(count, block),
    )


def block_front(feats_b, source_b, weights, state_low):
    width = state_low.shape[1]
    zpre = jnp.dot(feats_b.T, weights[0], preferred_element_type=jnp.float32) + weights[1].astype(
        jnp.float32
    )
    z_low = jax.nn.silu(zpre).astype(jnp.bfloat16)
    amat = (
        jnp.dot(z_low, weights[2], preferred_element_type=jnp.float32)
        + weights[3].astype(jnp.float32)
    ).astype(jnp.bfloat16)
    amat = amat.reshape(-1, width, width)
    node_ids = lax.iota(jnp.int32, state_low.shape[0])
    pick = (source_b[:, None] == node_ids[None, :]).astype(jnp.bfloat16)
    h_source = jnp.dot(pick, state_low, preferred_element_type=jnp.float32).astype(jnp.bfloat16)
    return (zpre, z_low, amat, h_source)


def target_table(target_b, valid_b, nodes):
    node_ids = lax.iota(jnp.int32, nodes)
    return ((target_b[:, None] == node_ids[None, :]) & (valid_b[:, None] > 0)).astype(jnp.bfloat16)


def forward_messages(state_low, blocks, weights):
    nodes, width = state_low.shape

    def add(total, pieces):
        feats_b, source_b, target_b, valid_b = pieces
        _, _, amat, h_source = block_front(feats_b, source_b, weights, state_low)
        message = jnp.einsum("eij,ej->ei", amat, h_source, preferred_element_type=jnp.float32)
        message = message * (valid_b > 0).astype(jnp.float32)[:, None]
        return (total + jax.ops.segment_sum(message, target_b, num_segments=nodes), None)

    summed, _ = lax.scan(add, jnp.zeros((nodes, width), jnp.float32), blocks)
    return summed


def gru_gates(gathered_low, state_low, weights):
    width = state_low.shape[1]
    gate_in = jnp.dot(gathered_low, weights[4], preferred_element_type=jnp.float32) + weights[
        5
    ].astype(jnp.float32)
    gate_state = jnp.dot(state_low, weights[6], preferred_element_type=jnp.float32) + weights[
        7
    ].astype(jnp.float32)
    reset = jax.nn.sigmoid(gate_in[:, :width] + gate_state[:, :width])
    update = jax.nn.sigmoid(gate_in[:, width : 2 * width] + gate_state[:, width : 2 * width])
    candidate = jnp.tanh(gate_in[:, 2 * width :] + reset * gate_state[:, 2 * width :])
    fresh = (1.0 - update) * candidate + update * state_low.astype(jnp.float32)
    return (fresh, gate_state, reset, update, candidate)


def backward_step(upstream, state_low, gathered_low, blocks, weights):
    nodes, width = state_low.shape
    fresh, gate_state, reset, update, candidate = gru_gates(gathered_low, state_low, weights)
    state = state_low.astype(jnp.float32)
    d_cand = upstream * (1.0 - update)
    d_update = upstream * (state - candidate)
    d_state = upstream * update
    d_npre = d_cand * (1.0 - candidate * candidate)
    d_upre = d_update * update * (1.0 - update)
    d_rpre = d_npre * gate_state[:, 2 * width :] * reset * (1.0 - reset)
    d_in = jnp.concatenate([d_rpre, d_upre, d_npre], axis=1).astype(jnp.bfloat16)
    d_hid = jnp.concatenate([d_rpre, d_upre, d_npre * reset], axis=1).astype(jnp.bfloat16)
    grad_wi = jnp.dot(gathered_low.T, d_in, preferred_element_type=jnp.float32)
    grad_bi = jnp.sum(d_in.astype(jnp.float32), axis=0)
    grad_wh = jnp.dot(state_low.T, d_hid, preferred_element_type=jnp.float32)
    grad_bh = jnp.sum(d_hid.astype(jnp.float32), axis=0)
    d_state = d_state + jnp.dot(d_hid, weights[6].T, preferred_element_type=jnp.float32)
    d_gathered = jnp.dot(d_in, weights[4].T, preferred_element_type=jnp.float32).astype(
        jnp.bfloat16
    )

    def back_block(carry, pieces):
        d_src, grad_w1, grad_b1, grad_w2, grad_b2 = carry
        feats_b, source_b, target_b, valid_b = pieces
        zpre, z_low, amat, h_source = block_front(feats_b, source_b, weights, state_low)
        put = target_table(target_b, valid_b, nodes)
        d_msg = jnp.dot(put, d_gathered, preferred_element_type=jnp.float32).astype(jnp.bfloat16)
        d_amat = d_msg.astype(jnp.float32)[:, :, None] * h_source.astype(jnp.float32)[:, None, :]
        d_amat = d_amat.reshape(d_amat.shape[0], width * width).astype(jnp.bfloat16)
        grad_w2 = grad_w2 + jnp.dot(z_low.T, d_amat, preferred_element_type=jnp.float32)
        grad_b2 = grad_b2 + jnp.sum(d_amat.astype(jnp.float32), axis=0)
        d_z = jnp.dot(d_amat, weights[2].T, preferred_element_type=jnp.float32)
        sig = jax.nn.sigmoid(zpre)
        d_zpre = (d_z * sig * (1.0 + zpre * (1.0 - sig))).astype(jnp.bfloat16)
        grad_w1 = grad_w1 + jnp.dot(feats_b, d_zpre, preferred_element_type=jnp.float32)
        grad_b1 = grad_b1 + jnp.sum(d_zpre.astype(jnp.float32), axis=0)
        d_source = jnp.einsum("eij,ei->ej", amat, d_msg, preferred_element_type=jnp.float32)
        d_src = d_src + jax.ops.segment_sum(d_source, source_b, num_segments=nodes)
        return ((d_src, grad_w1, grad_b1, grad_w2, grad_b2), None)

    start = (
        jnp.zeros((nodes, width), jnp.float32),
        jnp.zeros(weights[0].shape, jnp.float32),
        jnp.zeros(weights[1].shape, jnp.float32),
        jnp.zeros(weights[2].shape, jnp.float32),
        jnp.zeros(weights[3].shape, jnp.float32),
    )
    ends, _ = lax.scan(back_block, start, blocks)
    d_total = d_state + ends[0]
    return (d_total, (ends[1], ends[2], ends[3], ends[4], grad_wi, grad_bi, grad_wh, grad_bh))


def plain_shards(
    node_input,
    edge_input,
    edge_source,
    edge_target,
    edge_valid,
    node_labeled,
    edge_w1,
    edge_b1,
    edge_w2,
    edge_b2,
    gru_wi,
    gru_bi,
    gru_wh,
    gru_bh,
    state_cot,
):
    weights = (edge_w1, edge_b1, edge_w2, edge_b2, gru_wi, gru_bi, gru_wh, gru_bh)
    micro, nodes, width = node_input.shape
    block = min(EDGE_BLOCK, edge_input.shape[2])
    section_id = lax.axis_index("section")
    first = section_id == 0
    count_local = jnp.sum(node_labeled.astype(jnp.float32))

    def batch_blocks(index):
        feats = lax.dynamic_index_in_dim(edge_input, index, 0, keepdims=False)
        source = lax.dynamic_index_in_dim(edge_source, index, 0, keepdims=False)
        target = lax.dynamic_index_in_dim(edge_target, index, 0, keepdims=False)
        valid = lax.dynamic_index_in_dim(edge_valid, index, 0, keepdims=False)
        return split_blocks(feats, source, target, valid, block)

    received = jnp.zeros((nodes, width), jnp.bfloat16)
    saved = []
    states_out = jnp.zeros((micro, nodes, width), jnp.float32)
    for tick in range(micro + 1):
        batch = tick - section_id
        live = (batch >= 0) & (batch < micro)
        index = jnp.clip(batch, 0, micro - 1)
        state_low = jnp.where(first, node_input[min(tick, micro - 1)], received)
        blocks = batch_blocks(index)
        gathered_low = forward_messages(state_low, blocks, weights).astype(jnp.bfloat16)
        fresh = gru_gates(gathered_low, state_low, weights)[0]
        saved.append((state_low, gathered_low))
        sending = fresh.astype(jnp.bfloat16)
        value = jnp.where(first, sending.astype(jnp.float32), fresh)
        states_out = jnp.where(
            live, lax.dynamic_update_index_in_dim(states_out, value, index, 0), states_out
        )
        if tick < micro:
            received = passed_along(sending, "section", 1)
    grad_received = jnp.zeros((nodes, width), jnp.bfloat16)
    grads_out = jnp.zeros((micro, nodes, width), jnp.float32)
    totals = tuple((jnp.zeros(w.shape, jnp.float32) for w in weights))
    for tick in range(micro + 1):
        batch = micro - tick - section_id
        live = (batch >= 0) & (batch < micro)
        index = jnp.clip(batch, 0, micro - 1)
        state_low, gathered_low = saved[micro - tick]
        labels = lax.dynamic_index_in_dim(node_labeled, index, 0, keepdims=False).astype(
            jnp.float32
        )
        top = lax.dynamic_index_in_dim(state_cot, index, 0, keepdims=False) * labels[:, None]
        upstream = jnp.where(first, grad_received.astype(jnp.float32), top)
        d_total, terms = backward_step(
            upstream, state_low, gathered_low, batch_blocks(index), weights
        )
        totals = tuple((acc + jnp.where(live, term, 0.0) for acc, term in zip(totals, terms)))
        sending = d_total.astype(jnp.bfloat16)
        value = jnp.where(first, d_total, sending.astype(jnp.float32))
        grads_out = jnp.where(
            live, lax.dynamic_update_index_in_dim(grads_out, value, index, 0), grads_out
        )
        if tick < micro:
            grad_received = passed_along(sending, "section", -1)
    count_total = lax.psum(count_local, "dp")
    summed = lax.psum(
        (totals[0], totals[1], totals[2], totals[3], totals[4], totals[5], totals[6], totals[7]),
        ("section", "dp"),
    )
    scaled = [g / count_total for g in summed]
    return (
        states_out[None],
        grads_out[None],
        scaled[0],
        scaled[1],
        scaled[2],
        scaled[3],
        scaled[4],
        scaled[5],
        scaled[6],
        scaled[7],
    )


def solution(mesh):
    placed = (
        P(None, "dp", None), P(None, None, "dp"), P(None, "dp"), P(None, "dp"), P(None, "dp"),
        P(None, "dp"), P(), P(), P(), P(), P(), P(), P(), P(), P(None, "dp", None),
    )
    fits = LANE % (2 * mesh.shape["dp"]) == 0
    return jax.shard_map(
        shards if fits else plain_shards,
        mesh=mesh,
        in_specs=placed,
        out_specs=(P("section", None, "dp", None), P("section", None, "dp", None)) + (P(),) * 8,
        check_vma=False,
    )
```

```python
import functools

import jax
import jax.numpy as jnp
from jax import lax
from jax.experimental import pallas as pl
from jax.experimental.pallas import tpu as pltpu
from jax.sharding import PartitionSpec as P

BF, F32 = jnp.bfloat16, jnp.float32
VMEM = pltpu.VMEM
LANE = 128
ROUND = 32
SMALL_ROWS = 1024
PLANE = 4
SEMS = 160


def dot(a, b, ca=1, cb=0):
    return lax.dot_general(a, b, (((ca,), (cb,)), ((), ())), preferred_element_type=F32)


def split(x, parts):
    out = []
    for _ in range(parts - 1):
        piece = x.astype(BF)
        out.append(piece)
        x = x - piece.astype(F32)
    out.append(x.astype(BF))
    return out


def loop(count, body):
    def step(i, carry):
        body(i)
        return carry

    lax.fori_loop(0, count, step, 0)


def aligned(i, size):
    return pl.ds(pl.multiple_of(i * size, size), size)


def edge_tables(ends, nodes):
    ids = lax.broadcasted_iota(jnp.int32, (nodes, ends.shape[1]), 0).astype(F32)
    pick = (ids == ends[0:1]).astype(F32).astype(BF)
    put = (ids == ends[1:2]).astype(F32).astype(BF)
    return pick, put


def pack_ends(src_ref, tgt_ref, valid_ref, lab_ref, s):
    row = pl.ds(s, 1)
    src = src_ref[row, :].astype(F32)
    tgt = jnp.where(valid_ref[row, :] > 0, tgt_ref[row, :], -1).astype(F32)
    lab = lab_ref[row, :].astype(F32)
    edges, nodes = src.shape[1], lab.shape[1]
    lab = jnp.concatenate([lab, jnp.zeros((1, edges - nodes), F32)], axis=1)
    return jnp.concatenate([src, tgt, lab, jnp.zeros((13, edges), F32)], axis=0)


def edge_hidden(feats, w1, b1):
    bias = jnp.broadcast_to(b1.astype(F32), (LANE, LANE)).T[:, 0:1]
    return dot(w1, feats, 0, 0) + bias


def gru_forward(m, h, wi, bi, wh, bh):
    w = h.shape[1]
    gi = dot(m, wi) + bi.astype(F32)
    gh = dot(h, wh) + bh.astype(F32)
    r = jax.nn.sigmoid(gi[:, :w] + gh[:, :w])
    u = jax.nn.sigmoid(gi[:, w : 2 * w] + gh[:, w : 2 * w])
    n = jnp.tanh(gi[:, 2 * w :] + r * gh[:, 2 * w :])
    fresh = (1.0 - u) * n + u * h.astype(F32)
    return fresh, gh[:, 2 * w :], r, u, n


def gru_backward(g, h, gates, wi, wh):
    _, ghn, r, u, n = gates
    dn = g * (1.0 - u)
    du = g * (h.astype(F32) - n)
    dnpre = dn * (1.0 - n * n)
    dupre = du * u * (1.0 - u)
    drpre = dnpre * ghn * r * (1.0 - r)
    dgi = jnp.concatenate([drpre, dupre, dnpre], axis=1).astype(BF)
    dgh = jnp.concatenate([drpre, dupre, dnpre * r], axis=1).astype(BF)
    dm = dot(dgi, wi, 1, 1).astype(BF)
    dh = g * u + dot(dgh, wh, 1, 1)
    return dgi, dgh, dm, dh


class Net:
    def __init__(self, send_sems, recv_sems):
        self.send_sems, self.recv_sems = send_sems, recv_sems
        self.slots, self.sent, self.settled = {}, [], 0

    def slot(self, key):
        return self.slots.setdefault(key, len(self.slots))

    def send(self, key, src, dst, peer):
        copy = pltpu.make_async_remote_copy(
            src_ref=src,
            dst_ref=dst,
            send_sem=self.send_sems.at[len(self.sent)],
            recv_sem=self.recv_sems.at[self.slot(key)],
            device_id=peer,
            device_id_type=pl.DeviceIdType.MESH,
        )
        copy.start()
        self.sent.append(copy)

    def wait(self, key, region, peer):
        pltpu.make_async_remote_copy(
            src_ref=region,
            dst_ref=region,
            send_sem=self.send_sems.at[0],
            recv_sem=self.recv_sems.at[self.slot(key)],
            device_id=peer,
            device_id_type=pl.DeviceIdType.MESH,
        ).wait_recv()

    def drain(self):
        self.settle(len(self.sent))

    def settle(self, count):
        for copy in self.sent[self.settled : count]:
            copy.wait_send()
        self.settled = max(self.settled, count)


class Place:
    def __init__(self, parts):
        self.parts, self.plane = parts, PLANE
        self.lines = parts // PLANE
        self.s, self.c = lax.axis_index("section"), lax.axis_index("dp")
        self.sibling = {"section": 1 - self.s}

    def flip(self, mask):
        at, bit = self.c, 1
        while bit <= mask:
            if mask & bit:
                at = at + bit * (1 - 2 * lax.rem(lax.div(self.c, bit), 2))
            bit *= 2
        return at

    def peer(self, mask):
        return {"dp": self.flip(mask)}

    def block(self, mask):
        return self.s * self.parts + self.flip(mask)

    def spot(self, line):
        return self.s * self.lines + lax.div(self.flip(line * self.plane), self.plane)

    def level(self, line):
        own = lax.div(self.flip(line * self.plane), self.plane) * self.plane
        return self.s * self.parts + own


class LineGather:
    def __init__(self, net, place, name, buf):
        self.net, self.place, self.name, self.buf = net, place, name, buf

    def block(self, line):
        return self.buf.at[self.place.spot(line)]

    def begin(self):
        p = self.place
        for line in range(1, p.lines):
            ref = self.block(0)
            self.net.send((self.name, line), ref, ref, p.peer(line * PLANE))

    def middle(self):
        p = self.place
        for line in range(1, p.lines):
            self.net.wait((self.name, line), self.block(line), p.peer(line * PLANE))
        ref = self.buf.at[pl.ds(p.s * p.lines, p.lines)]
        self.net.send((self.name, "sib"), ref, ref, p.sibling)

    def finish(self):
        p = self.place
        ref = self.buf.at[pl.ds((1 - p.s) * p.lines, p.lines)]
        self.net.wait((self.name, "sib"), ref, p.sibling)


def main_kernel(
    x_ref, f_ref, src_ref, tgt_ref, val_ref, lab_ref, w1_ref, b1_ref, w2_hbm, b2_ref,
    wi_ref, bi_ref, wh_ref, bh_ref, cot_ref,
    full_out, states_out, grads_out, w1_out,
    w2, amat, acc, zaug, zpre_s, hs, hsl, dms, dml, dzacc, picks, puts,
    ins, hid, dts, qst, zall, part, sums, tmp, small, small_in, small_lo, small_line, small_plane,
    w1_io, swap, w2_sems, send_sems, recv_sems,
):
    edges, nodes = f_ref.shape[2], x_ref.shape[1]
    tiles5 = edges // LANE
    parts = full_out.shape[0] // 2
    blocks = 2 * parts
    per = LANE // blocks
    place = Place(parts)
    net = Net(send_sems, recv_sems)
    s, c = place.s, place.c
    me = place.block(0)
    here = place.spot(0)
    group = 2 * place.lines
    rounds = LANE // ROUND

    barrier = pltpu.get_barrier_semaphore()
    peers = [place.peer(q) for q in range(1, PLANE)]
    peers += [place.peer(line * PLANE) for line in range(1, place.lines)] + [place.sibling]
    for peer in peers:
        pl.semaphore_signal(
            barrier, inc=1, device_id=peer, device_id_type=pl.DeviceIdType.MESH
        )

    def w2_copy(ib):
        part = aligned(ib, ROUND * LANE)
        return pltpu.make_async_copy(w2_hbm.at[:, part], w2.at[:, part], w2_sems.at[ib])

    for ib in range(rounds):
        w2_copy(ib).start()

    feats = f_ref[s]
    ends = pack_ends(src_ref, tgt_ref, val_ref, lab_ref, s)
    h0 = x_ref[s]
    for e in range(tiles5):
        ins[here, e * 16 : (e + 1) * 16, :] = feats[:, e * LANE : (e + 1) * LANE]
    table = [ends[q : q + 1, e * LANE : (e + 1) * LANE] for q in range(2) for e in range(tiles5)]
    table.append(ends[2:3, :nodes])
    table.append(jnp.zeros((16 - len(table), LANE), F32))
    ins[here, tiles5 * 16 : (tiles5 + 1) * 16, :] = jnp.concatenate(table, axis=0).astype(BF)
    hid[0, here] = h0
    pick, put = edge_tables(ends, nodes)
    picks[...] = pick
    puts[...] = put
    zpre = edge_hidden(feats, w1_ref[...], b1_ref[...])
    zpre_s[...] = zpre
    zaug[0:LANE] = jax.nn.silu(zpre).astype(BF)
    zaug[LANE : 2 * LANE] = jnp.ones((LANE, edges), BF)

    def sources(t, h):
        got = dot(h, picks[...], 0, 0)
        hs[t] = got
        hsl[:, t * edges : (t + 1) * edges] = got.astype(BF)

    sources(0, h0)
    lane = lax.broadcasted_iota(jnp.int32, (LANE, LANE), 1)
    b2t = b2_ref[...].T
    tiles = [(e, min(256, edges - e)) for e in range(0, edges, 256)]

    gather_in = LineGather(net, place, "in", ins)
    gather_h0 = LineGather(net, place, "h0", hid.at[0])
    gather_h1 = LineGather(net, place, "h1", hid.at[1])
    gather_d2 = LineGather(net, place, "d2", dts.at[1])
    gather_d1 = LineGather(net, place, "d1", dts.at[0])

    def keep(i, e, w, p):
        p = p.reshape(16, 8, w).sum(0)
        for o in range(0, w, LANE):
            acc[(e + o) // LANE, aligned(i, 8), :] = p[:, o : o + LANE]

    def first(ib):
        w2_copy(ib).wait()
        lhs = []
        for v in range(ROUND):
            i = ib * ROUND + v
            bias = jnp.where(lane == i, b2t, jnp.zeros_like(b2t))
            lhs.append(jnp.concatenate([w2[:, aligned(i, LANE)].T, bias], axis=1))
        lhs = jnp.concatenate(lhs, axis=0)
        for e, w in tiles:
            a = dot(lhs, zaug[:, e : e + w]).astype(BF)
            amat[aligned(ib, ROUND * LANE), e : e + w] = a
            for v in range(ROUND):
                p = a[v * LANE : (v + 1) * LANE].astype(F32) * hs[0, :, e : e + w]
                keep(ib * ROUND + v, e, w, p)

    loop(rounds // 2, first)
    pl.semaphore_wait(barrier, len(peers))
    gather_in.begin()
    gather_h0.begin()
    loop(rounds - rounds // 2, lambda ib: first(ib + rounds // 2))

    def again(ib):
        for e, w in tiles:
            for v in range(8):
                a = amat[aligned(ib * 8 + v, LANE), e : e + w]
                keep(ib * 8 + v, e, w, a.astype(F32) * hs[1, :, e : e + w])

    def gathered():
        msg = []
        for e in range(tiles5):
            part = acc[e, pl.ds(0, LANE, stride=8), :]
            for q in range(1, 8):
                part = part + acc[e, pl.ds(q, LANE, stride=8), :]
            msg.append(part)
        msg = jnp.concatenate(msg, axis=1)
        total = jnp.zeros((nodes, LANE), F32)
        for piece in split(msg, 3):
            total = total + dot(puts[...], piece, 1, 1)
        return total.astype(BF)

    weights = (wi_ref[...], bi_ref[...].reshape(1, -1), wh_ref[...], bh_ref[...].reshape(1, -1))
    m1 = gathered()
    gates1 = gru_forward(m1, h0, *weights)
    h1 = gates1[0].astype(BF)
    hid[1, here] = h1
    gather_h1.begin()
    sources(1, h1)
    loop(LANE // 8, again)
    m2 = gathered()
    gates2 = gru_forward(m2, h1, *weights)
    h2 = gates2[0]
    label = jnp.broadcast_to(ends[2:3, :nodes], (LANE, nodes)).T
    g2 = cot_ref[s] * label
    dgi2, dgh2, dm2, dh2 = gru_backward(g2, h1, gates2, weights[0], weights[2])
    dt2 = dm2.T
    dts[1, here] = dt2
    gather_d2.begin()

    def spread(t, dt):
        got = dot(dt, puts[...])
        dms[t] = got
        dml[:, t * edges : (t + 1) * edges] = got.astype(BF)

    def to_source_tile(t, e):
        def body(ib, total):
            d = dms[t, aligned(ib, 8), e * LANE : (e + 1) * LANE]
            for v in range(8):
                a = amat[aligned(ib * 8 + v, LANE), e * LANE : (e + 1) * LANE].astype(F32)
                total = total + a * d[v : v + 1]
            return total

        return lax.fori_loop(0, LANE // 8, body, jnp.zeros((LANE, LANE), F32))

    def to_nodes(outs):
        back = jnp.concatenate(outs, axis=1)
        total = jnp.zeros((nodes, LANE), F32)
        for piece in split(back, 3):
            total = total + dot(picks[...], piece, 1, 1)
        return total

    spread(1, dt2)
    back2 = [to_source_tile(1, e) for e in range(tiles5)]
    gather_in.middle()
    gather_h0.middle()
    gather_h1.middle()
    d1 = (dh2 + to_nodes(back2)).astype(BF)
    dgi1, dgh1, dm1, dh1 = gru_backward(d1.astype(F32), h0, gates1, weights[0], weights[2])
    dt1 = dm1.T
    dts[0, here] = dt1
    gather_d1.begin()
    gather_d2.middle()

    gather_in.finish()
    gather_h0.finish()
    gather_h1.finish()
    dzacc[...] = jnp.zeros_like(dzacc)

    def back_hidden(ib):
        total = dzacc[...]
        for a in range(2):
            d = [dms[t, aligned(ib * 2 + a, 8), :] for t in range(2)]
            for v in range(8):
                both = hs[0] * d[0][v : v + 1] + hs[1] * d[1][v : v + 1]
                qst[a, v * LANE : (v + 1) * LANE, 0:edges] = both.astype(BF)
            total = total + dot(w2[:, aligned(ib * 2 + a, 8 * LANE)], qst[a, :, 0:edges])
        dzacc[...] = total

    units = PLANE * per
    ks = lax.broadcasted_iota(jnp.int32, (units, LANE), 0)
    ks = (lax.div(ks, per) * 2 + s) * per + lax.rem(ks, per) + lax.div(c, PLANE) * (2 * units)
    sel = (ks == lax.broadcasted_iota(jnp.int32, (units, LANE), 1)).astype(F32)
    w1t = dot(sel.astype(BF), w1_ref[...], 1, 1).astype(BF)
    b1 = jnp.sum(sel * b1_ref[...].astype(F32), axis=1, keepdims=True)
    quarter = nodes // 4
    qn = lax.broadcasted_iota(jnp.int32, (quarter, 256), 0).astype(F32)
    sn = lax.broadcasted_iota(jnp.int32, (nodes, 256), 0).astype(F32)

    def hidden(blk):
        cols = [ins[blk, e * 16 : (e + 1) * 16, :] for e in range(tiles5)]
        z = jax.nn.silu(dot(w1t, jnp.concatenate(cols, axis=1)) + b1)
        zall[blk] = z.astype(BF).astype(F32)

    def build(blk):
        z = zall[blk]
        en = ins[blk, tiles5 * 16 : (tiles5 + 1) * 16, :].astype(F32)
        pairs = []
        for q in range(4):
            lo = q * LANE
            zq = z[:, lo : lo + 256]
            src = jnp.concatenate([en[q : q + 1], en[q + 1 : q + 2]], axis=1)
            tgt = jnp.concatenate(
                [en[tiles5 + q : tiles5 + q + 1], en[tiles5 + q + 1 : tiles5 + q + 2]], axis=1
            )
            hit_t = (qn + float(q * quarter)) == tgt
            hit_s = (sn == src).astype(F32).astype(BF)
            lhs = [jnp.where(hit_t, zq[k : k + 1], 0.0).astype(BF) for k in range(units)]
            pairs.append(dot(jnp.concatenate(lhs, axis=0), hit_s, 1, 1))
        pairs = jnp.concatenate(split(jnp.concatenate(pairs, axis=0), 2), axis=1)
        h = jnp.concatenate([hid[0, blk], hid[1, blk]], axis=1)
        got = dot(pairs, jnp.concatenate([h, h], axis=0)).astype(BF)
        for q in range(4):
            at = pl.ds(pl.multiple_of(blk * nodes + q * quarter, quarter), quarter)
            for k in range(units):
                part = got[(q * units + k) * quarter : (q * units + k + 1) * quarter]
                for t in range(2):
                    qst[t, at, k * LANE : (k + 1) * LANE] = part[:, t * LANE : (t + 1) * LANE]

    for blk in range(group):
        hidden(blk)
    loop(group, build)
    gather_d1.middle()
    gather_d2.finish()
    lhs = jnp.concatenate([dts[1, blk] for blk in range(group)], axis=1)
    part[...] = dot(lhs, qst[1])
    count = jnp.zeros((1, LANE), F32)
    for blk in range(group):
        count = count + ins[blk, tiles5 * 16 : (tiles5 + 1) * 16, :].astype(F32)[10:11]
    count = jnp.concatenate([count, jnp.zeros((15, LANE), F32)], axis=0).astype(BF)
    mid = per * LANE // 2
    early = len(net.sent)
    pieces = (pl.ds(0, 16 + mid), pl.ds(16 + mid, per * LANE - mid))

    def send_sums(ch, q):
        ref = sums.at[0, lax.rem(place.flip(q), PLANE), pieces[ch]]
        net.send(("sums", ch, q), ref, sums.at[1, q, pieces[ch]], place.peer(q))

    def add_sums(ch):
        total = sums[0, q_me, pieces[ch], :].astype(F32)
        for q in range(1, PLANE):
            net.wait(("sums", ch, q), sums.at[1, q, pieces[ch]], place.peer(q))
            total = total + sums[1, q, pieces[ch], :].astype(F32)
        return total

    gather_d1.finish()
    lhs = jnp.concatenate([dts[0, blk] for blk in range(group)], axis=1)
    for q in (3, 1, 2, 0):
        to = lax.rem(place.flip(q), PLANE)
        cols = aligned(to, per * LANE)
        got = part[:, cols] + dot(lhs, qst[0, :, cols])
        for k in range(per):
            tmp[q, pl.ds(k, LANE, stride=per), :] = got[:, k * LANE : (k + 1) * LANE]
        sums[0, to, 0:16] = count
        sums[0, to, 16:] = tmp[q].astype(BF)
        if q:
            send_sums(0, q)
    for q in (3, 1, 2):
        send_sums(1, q)

    half = SMALL_ROWS // 2
    plane_rows = half // place.lines
    own_rows = plane_rows // PLANE
    gwi = dot(m1, dgi1, 0, 0) + dot(m2, dgi2, 0, 0)
    gwh = dot(h0, dgh1, 0, 0) + dot(h1, dgh2, 0, 0)
    for q in range(3):
        small[q * LANE : (q + 1) * LANE] = gwi[:, q * LANE : (q + 1) * LANE]
        small[(3 + q) * LANE : (4 + q) * LANE] = gwh[:, q * LANE : (q + 1) * LANE]
    spread(0, dt1)
    small[6 * LANE : 7 * LANE] = dot(dml[...], hsl[...], 1, 1)
    gbi = dgi1.astype(F32).sum(0, keepdims=True) + dgi2.astype(F32).sum(0, keepdims=True)
    gbh = dgh1.astype(F32).sum(0, keepdims=True) + dgh2.astype(F32).sum(0, keepdims=True)
    rows = [x[:, q * LANE : (q + 1) * LANE] for x in (gbi, gbh) for q in range(3)]
    rows.append(jnp.zeros((SMALL_ROWS - 7 * LANE - 6, LANE), F32))
    small[7 * LANE :] = jnp.concatenate(rows, axis=0)
    net.send(("small", "sib"), small.at[aligned(1 - s, half)], small_in, place.sibling)

    q_me = lax.rem(c, PLANE)
    back1 = [to_source_tile(0, e) for e in range(2)]
    net.wait(("small", "sib"), small_in, place.sibling)
    small_lo[...] = (small[aligned(s, half), :] + small_in[...]).astype(BF)
    z = lax.div(c, PLANE)
    for line in range(1, place.lines):
        to = lax.div(place.flip(line * PLANE), PLANE)
        net.send(
            ("small", "line", line),
            small_lo.at[aligned(to, plane_rows)],
            small_line.at[line],
            place.peer(line * PLANE),
        )

    size = full_out.shape[1]
    tail = size // 8 // 16 * 16
    top = size - tail
    cut = (mid // 32 * 16, mid + (top - mid) // 32 * 16)
    halves = (
        (pl.ds(0, cut[0]), pl.ds(cut[0], mid - cut[0])),
        (pl.ds(mid, cut[1] - mid), pl.ds(cut[1], top - cut[1])),
    )
    chunk = (pl.ds(0, mid), pl.ds(mid, top - mid))
    last = pl.ds(top, tail)
    order = ((1, 0), (2, 1), (1, 1), (2, 0))

    def out_begin(ch):
        def along(line):
            ref = full_out.at[me, chunk[ch]]
            net.send(("out", ch, line), ref, ref, place.peer(line * PLANE))

        along(1)
        for q, a in order:
            ref = full_out.at[me, halves[ch][a]]
            net.send(("out", ch, 0, q, a), ref, ref, place.peer(q))
        for line in range(2, place.lines):
            along(line)

    def out_line(ch, line):
        mask = line * PLANE
        blk = place.block(mask)
        net.wait(("out", ch, line), full_out.at[blk, chunk[ch]], place.peer(mask))
        for q, a in order:
            ref = full_out.at[blk, halves[ch][a]]
            net.send(("out", ch, line, q, a), ref, ref, place.peer(q))

    def out_cross(ch, line):
        for q, a in ((1, 0), (2, 1)):
            ref = full_out.at[place.block(line * PLANE + q), halves[ch][a]]
            net.wait(("out", ch, line, q, a), ref, place.peer(q))
            net.send(("out", ch, line, 3, a), ref, ref, place.peer(3 - q))

    def last_planes():
        for q in range(1, PLANE):
            ref = full_out.at[me, last]
            net.send(("last", 0, q), ref, ref, place.peer(q))

    def last_lines():
        for q in range(1, PLANE):
            net.wait(("last", 0, q), full_out.at[place.block(q), last], place.peer(q))
        ref = full_out.at[pl.ds(place.level(0), PLANE), last]
        for line in range(1, place.lines):
            net.send(("last", line), ref, ref, place.peer(line * PLANE))

    def out_level(line):
        for ch in range(2):
            for q, a in ((1, 1), (2, 0)):
                ref = full_out.at[place.block(line * PLANE + q), halves[ch][a]]
                net.wait(("out", ch, line, q, a), ref, place.peer(q))
            for q, a in ((2, 0), (1, 1)):
                ref = full_out.at[place.block(line * PLANE + 3), halves[ch][a]]
                net.wait(("out", ch, line, 3, a), ref, place.peer(q))
        if line > 0:
            part = full_out.at[pl.ds(place.level(line), PLANE), last]
            net.wait(("last", line), part, place.peer(line * PLANE))
        ref = full_out.at[pl.ds(place.level(line), PLANE)]
        net.send(("out", "sib", line), ref, ref, place.sibling)

    net.settle(early)
    total = add_sums(0)
    scale = 1.0 / jnp.sum(total[0:1], axis=1, keepdims=True)
    full_out[me, 0:mid] = (total[16:] * scale).astype(BF)
    out_begin(0)
    back1 += [to_source_tile(0, e) for e in range(2, 4)]
    own = small_lo[aligned(z, plane_rows), :].astype(F32)
    for line in range(1, place.lines):
        net.wait(("small", "line", line), small_line.at[line], place.peer(line * PLANE))
        own = own + small_line[line].astype(F32)
    small_line[0] = own.astype(BF)
    for q in range(1, PLANE):
        to = lax.rem(place.flip(q), PLANE)
        net.send(
            ("small", "plane", q),
            small_line.at[0, aligned(to, own_rows)],
            small_plane.at[q],
            place.peer(q),
        )
    full_out[me, mid : per * LANE] = (add_sums(1) * scale).astype(BF)
    out_begin(1)
    mark = len(net.sent)
    out_cross(0, 0)
    back1 += [to_source_tile(0, e) for e in range(4, tiles5)]
    d0 = dh1 + to_nodes(back1)

    zero = s == 0
    swap[0, 0] = jnp.where(zero, h2, h1.astype(F32))
    swap[0, 1] = jnp.where(zero, d1.astype(F32), d0)
    net.send(("swap",), swap.at[0], swap.at[1], place.sibling)
    own = small_line[0, aligned(q_me, own_rows), :].astype(F32)
    for q in range(1, PLANE):
        net.wait(("small", "plane", q), small_plane.at[q], place.peer(q))
        own = own + small_plane[q].astype(F32)
    full_out[me, per * LANE : per * LANE + own_rows] = (own * scale).astype(BF)
    last_planes()
    out_line(0, 1)
    out_cross(1, 0)
    loop(2, back_hidden)
    for line in range(2, place.lines):
        out_line(0, line)
    out_line(1, 1)
    out_cross(0, 1)
    last_lines()
    loop(3, lambda ib: back_hidden(ib + 2))
    for line in range(2, place.lines):
        out_line(1, line)
    out_cross(1, 1)
    out_cross(0, 2)
    out_level(0)
    net.settle(mark)
    mark = len(net.sent)
    loop(LANE // 16 - 5, lambda ib: back_hidden(ib + 5))
    zp = zpre_s[...]
    sig = jax.nn.sigmoid(zp)
    slope = sig * (1.0 + zp * (1.0 - sig))
    lhs = jnp.concatenate(
        [feats, jnp.ones((1, edges), BF), jnp.zeros((15, edges), BF)], axis=0
    )
    total = dot(lhs, (dzacc[...] * slope).astype(BF), 1, 1)
    w1_io[0] = total[0:24]
    net.send(("w1", "sib"), w1_io.at[0], w1_io.at[1], place.sibling)
    for line in range(3, place.lines):
        out_cross(0, line)
    out_cross(1, 2)
    net.wait(("w1", "sib"), w1_io.at[1], place.sibling)
    total = w1_io[0] + w1_io[1]
    w1_io[2] = total
    at = 4
    for line in range(1, place.lines):
        net.send(("w1", "line", line), w1_io.at[2], w1_io.at[at + line], place.peer(line * PLANE))
    net.wait(("swap",), swap.at[1], place.sibling)
    mine_state = jnp.where(zero, h1.astype(F32), h2)
    mine_grad = jnp.where(zero, d0, d1.astype(F32))
    states_out[0] = jnp.where(zero, mine_state, swap[1, 0])
    states_out[1] = jnp.where(zero, swap[1, 0], mine_state)
    grads_out[0] = jnp.where(zero, mine_grad, swap[1, 1])
    grads_out[1] = jnp.where(zero, swap[1, 1], mine_grad)
    for line in range(3, place.lines):
        out_cross(1, line)
    out_level(1)
    for line in range(1, place.lines):
        net.wait(("w1", "line", line), w1_io.at[at + line], place.peer(line * PLANE))
        total = total + w1_io[at + line]
    w1_io[3] = total
    at += place.lines
    for q in range(1, PLANE):
        net.send(("w1", "plane", q), w1_io.at[3], w1_io.at[at + q], place.peer(q))
    net.settle(mark)
    for line in range(2, place.lines):
        out_level(line)
    for q in range(1, PLANE):
        net.wait(("w1", "plane", q), w1_io.at[at + q], place.peer(q))
        total = total + w1_io[at + q]
    w1_out[...] = total * scale
    for line in range(place.lines):
        first = place.level(line) + (1 - 2 * s) * parts
        net.wait(("out", "sib", line), full_out.at[pl.ds(first, PLANE)], place.sibling)
    net.drain()


def final_kernel(full_ref, w1_ref, st_ref, sg_ref, w2_out, b2_out, wi_out, bi_out, wh_out, bh_out,
                 gw1_out, gb1_out, st_out, sg_out, flat, out_sems):
    blocks = full_ref.shape[0]
    parts = blocks // 2
    width = b2_out.shape[0]
    rows = width * (width // blocks)

    def put(c):
        part = aligned(c, 8)
        return pltpu.make_async_copy(flat.at[part], w2_out.at[part], out_sems.at[c])

    gw1_out[...] = w1_ref[0:16]
    gb1_out[...] = w1_ref[16:17]
    st_out[...] = st_ref[...]
    sg_out[...] = sg_ref[...]
    low = lax.broadcasted_iota(jnp.int32, (1, 8, LANE), 1) < 4

    def place_rows(c):
        a = full_ref[c, :rows].astype(F32).reshape(rows // 8, 8, LANE)
        b = full_ref[c + parts, :rows].astype(F32).reshape(rows // 8, 8, LANE)
        even = jnp.where(low, a, pltpu.roll(b, 4, 1))
        odd = jnp.where(low, pltpu.roll(a, 4, 1), b)
        for p in range(rows // 8):
            flat[aligned(c, 8), (2 * p) * LANE : (2 * p + 1) * LANE] = even[p]
            flat[aligned(c, 8), (2 * p + 1) * LANE : (2 * p + 2) * LANE] = odd[p]
        put(c).start()

    loop(parts, place_rows)
    x = full_ref[:, rows:].astype(F32).reshape(-1, LANE)
    for q in range(3):
        cols = slice(q * LANE, (q + 1) * LANE)
        wi_out[:, cols] = x[q * LANE : (q + 1) * LANE]
        wh_out[:, cols] = x[(3 + q) * LANE : (4 + q) * LANE]
        bi_out[cols] = x[7 * LANE + q]
        bh_out[cols] = x[7 * LANE + 3 + q]
    b2_out[...] = x[6 * LANE : 7 * LANE]
    loop(parts, lambda c: put(c).wait())


def shards(
    node_input, edge_input, edge_source, edge_target, edge_valid, node_labeled,
    edge_w1, edge_b1, edge_w2, edge_b2, gru_wi, gru_bi, gru_wh, gru_bh, state_cot,
):
    micro, nodes, width = node_input.shape
    edges = edge_input.shape[2]
    parts = lax.axis_size("dp")
    blocks = 2 * parts
    per = width // blocks
    lines = parts // PLANE
    group, units = 2 * lines, PLANE * per
    half = SMALL_ROWS // 2
    plane_rows = half // lines
    own_rows = plane_rows // PLANE
    size = width * per + own_rows
    vm = pl.BlockSpec(memory_space=VMEM)
    hbm = pl.BlockSpec(memory_space=pl.ANY)
    sds = jax.ShapeDtypeStruct
    full, states, grads, gw1 = pl.pallas_call(
        main_kernel,
        out_shape=(
            VMEM((blocks, size, width), BF), VMEM((2, nodes, width), F32),
            VMEM((2, nodes, width), F32), VMEM((24, width), F32),
        ),
        in_specs=[vm] * 8 + [hbm] + [vm] * 6,
        out_specs=[vm] * 4,
        scratch_shapes=[
            VMEM((width, width * width), BF), VMEM((width * width, edges), BF),
            VMEM((edges // LANE, 8 * width, LANE), F32), VMEM((2 * width, edges), BF),
            VMEM((width, edges), F32), VMEM((2, width, edges), F32),
            VMEM((width, 2 * edges), BF), VMEM((2, width, edges), F32),
            VMEM((width, 2 * edges), BF),
            VMEM((width, edges), F32), VMEM((nodes, edges), BF), VMEM((nodes, edges), BF),
            VMEM((group, 16 * (edges // LANE + 1), LANE), BF),
            VMEM((2, group, nodes, width), BF), VMEM((2, group, width, nodes), BF),
            VMEM((2, group * nodes, units * width), BF), VMEM((group, units, edges), F32),
            VMEM((width, units * width), F32),
            VMEM((2, PLANE, per * width + 16, width), BF),
            VMEM((PLANE, width * per, width), F32),
            VMEM((SMALL_ROWS, width), F32), VMEM((half, width), F32),
            VMEM((half, width), BF), VMEM((lines, plane_rows, width), BF),
            VMEM((PLANE, own_rows, width), BF), VMEM((4 + lines + PLANE, 24, width), F32),
            VMEM((2, 2, nodes, width), F32),
            pltpu.SemaphoreType.DMA((width // ROUND,)),
            pltpu.SemaphoreType.DMA((SEMS,)), pltpu.SemaphoreType.DMA((SEMS,)),
        ],
        compiler_params=pltpu.CompilerParams(
            collective_id=0, has_side_effects=True, vmem_limit_bytes=57 * 2**20
        ),
    )(
        node_input, edge_input, edge_source, edge_target, edge_valid, node_labeled,
        edge_w1, edge_b1.reshape(1, -1), edge_w2, edge_b2.reshape(width, width),
        gru_wi, gru_bi, gru_wh, gru_bh, state_cot,
    )

    w2, b2, wi, bi, wh, bh, w1, b1, states, grads = pl.pallas_call(
        final_kernel,
        out_shape=(
            sds((width, width * width), F32), sds((width, width), F32),
            sds((width, 3 * width), F32), sds((3 * width,), F32),
            sds((width, 3 * width), F32), sds((3 * width,), F32),
            sds((16, width), F32), sds((1, width), F32),
            sds((2, nodes, width), F32), sds((2, nodes, width), F32),
        ),
        in_specs=[vm] * 4,
        out_specs=[hbm] + [vm] * 9,
        scratch_shapes=[
            VMEM((width, width * width), F32), pltpu.SemaphoreType.DMA((parts,)),
        ],
        compiler_params=pltpu.CompilerParams(vmem_limit_bytes=40 * 2**20),
    )(full, gw1, states, grads)
    return (
        states[None], grads[None], w1, b1.reshape(-1), w2, b2.reshape(-1),
        wi, bi, wh, bh,
    )


EDGE_BLOCK = 128


def passed_along(value, axis, steps):
    count = lax.axis_size(axis)
    leading, last = (max(0, -steps), min(count, count - steps))
    return lax.ppermute(value, axis, [(source, source + steps) for source in range(leading, last)])


def split_blocks(feats, source, target, valid, block):
    count = feats.shape[1] // block
    return (
        feats.reshape(feats.shape[0], count, block).transpose(1, 0, 2),
        source.reshape(count, block),
        target.reshape(count, block),
        valid.reshape(count, block),
    )


def block_front(feats_b, source_b, weights, state_low):
    width = state_low.shape[1]
    zpre = jnp.dot(feats_b.T, weights[0], preferred_element_type=jnp.float32) + weights[1].astype(
        jnp.float32
    )
    z_low = jax.nn.silu(zpre).astype(jnp.bfloat16)
    amat = (
        jnp.dot(z_low, weights[2], preferred_element_type=jnp.float32)
        + weights[3].astype(jnp.float32)
    ).astype(jnp.bfloat16)
    amat = amat.reshape(-1, width, width)
    node_ids = lax.iota(jnp.int32, state_low.shape[0])
    pick = (source_b[:, None] == node_ids[None, :]).astype(jnp.bfloat16)
    h_source = jnp.dot(pick, state_low, preferred_element_type=jnp.float32).astype(jnp.bfloat16)
    return (zpre, z_low, amat, h_source)


def target_table(target_b, valid_b, nodes):
    node_ids = lax.iota(jnp.int32, nodes)
    return ((target_b[:, None] == node_ids[None, :]) & (valid_b[:, None] > 0)).astype(jnp.bfloat16)


def forward_messages(state_low, blocks, weights):
    nodes, width = state_low.shape

    def add(total, pieces):
        feats_b, source_b, target_b, valid_b = pieces
        _, _, amat, h_source = block_front(feats_b, source_b, weights, state_low)
        message = jnp.einsum("eij,ej->ei", amat, h_source, preferred_element_type=jnp.float32)
        message = message * (valid_b > 0).astype(jnp.float32)[:, None]
        return (total + jax.ops.segment_sum(message, target_b, num_segments=nodes), None)

    summed, _ = lax.scan(add, jnp.zeros((nodes, width), jnp.float32), blocks)
    return summed


def gru_gates(gathered_low, state_low, weights):
    width = state_low.shape[1]
    gate_in = jnp.dot(gathered_low, weights[4], preferred_element_type=jnp.float32) + weights[
        5
    ].astype(jnp.float32)
    gate_state = jnp.dot(state_low, weights[6], preferred_element_type=jnp.float32) + weights[
        7
    ].astype(jnp.float32)
    reset = jax.nn.sigmoid(gate_in[:, :width] + gate_state[:, :width])
    update = jax.nn.sigmoid(gate_in[:, width : 2 * width] + gate_state[:, width : 2 * width])
    candidate = jnp.tanh(gate_in[:, 2 * width :] + reset * gate_state[:, 2 * width :])
    fresh = (1.0 - update) * candidate + update * state_low.astype(jnp.float32)
    return (fresh, gate_state, reset, update, candidate)


def backward_step(upstream, state_low, gathered_low, blocks, weights):
    nodes, width = state_low.shape
    fresh, gate_state, reset, update, candidate = gru_gates(gathered_low, state_low, weights)
    state = state_low.astype(jnp.float32)
    d_cand = upstream * (1.0 - update)
    d_update = upstream * (state - candidate)
    d_state = upstream * update
    d_npre = d_cand * (1.0 - candidate * candidate)
    d_upre = d_update * update * (1.0 - update)
    d_rpre = d_npre * gate_state[:, 2 * width :] * reset * (1.0 - reset)
    d_in = jnp.concatenate([d_rpre, d_upre, d_npre], axis=1).astype(jnp.bfloat16)
    d_hid = jnp.concatenate([d_rpre, d_upre, d_npre * reset], axis=1).astype(jnp.bfloat16)
    grad_wi = jnp.dot(gathered_low.T, d_in, preferred_element_type=jnp.float32)
    grad_bi = jnp.sum(d_in.astype(jnp.float32), axis=0)
    grad_wh = jnp.dot(state_low.T, d_hid, preferred_element_type=jnp.float32)
    grad_bh = jnp.sum(d_hid.astype(jnp.float32), axis=0)
    d_state = d_state + jnp.dot(d_hid, weights[6].T, preferred_element_type=jnp.float32)
    d_gathered = jnp.dot(d_in, weights[4].T, preferred_element_type=jnp.float32).astype(
        jnp.bfloat16
    )

    def back_block(carry, pieces):
        d_src, grad_w1, grad_b1, grad_w2, grad_b2 = carry
        feats_b, source_b, target_b, valid_b = pieces
        zpre, z_low, amat, h_source = block_front(feats_b, source_b, weights, state_low)
        put = target_table(target_b, valid_b, nodes)
        d_msg = jnp.dot(put, d_gathered, preferred_element_type=jnp.float32).astype(jnp.bfloat16)
        d_amat = d_msg.astype(jnp.float32)[:, :, None] * h_source.astype(jnp.float32)[:, None, :]
        d_amat = d_amat.reshape(d_amat.shape[0], width * width).astype(jnp.bfloat16)
        grad_w2 = grad_w2 + jnp.dot(z_low.T, d_amat, preferred_element_type=jnp.float32)
        grad_b2 = grad_b2 + jnp.sum(d_amat.astype(jnp.float32), axis=0)
        d_z = jnp.dot(d_amat, weights[2].T, preferred_element_type=jnp.float32)
        sig = jax.nn.sigmoid(zpre)
        d_zpre = (d_z * sig * (1.0 + zpre * (1.0 - sig))).astype(jnp.bfloat16)
        grad_w1 = grad_w1 + jnp.dot(feats_b, d_zpre, preferred_element_type=jnp.float32)
        grad_b1 = grad_b1 + jnp.sum(d_zpre.astype(jnp.float32), axis=0)
        d_source = jnp.einsum("eij,ei->ej", amat, d_msg, preferred_element_type=jnp.float32)
        d_src = d_src + jax.ops.segment_sum(d_source, source_b, num_segments=nodes)
        return ((d_src, grad_w1, grad_b1, grad_w2, grad_b2), None)

    start = (
        jnp.zeros((nodes, width), jnp.float32),
        jnp.zeros(weights[0].shape, jnp.float32),
        jnp.zeros(weights[1].shape, jnp.float32),
        jnp.zeros(weights[2].shape, jnp.float32),
        jnp.zeros(weights[3].shape, jnp.float32),
    )
    ends, _ = lax.scan(back_block, start, blocks)
    d_total = d_state + ends[0]
    return (d_total, (ends[1], ends[2], ends[3], ends[4], grad_wi, grad_bi, grad_wh, grad_bh))


def plain_shards(
    node_input,
    edge_input,
    edge_source,
    edge_target,
    edge_valid,
    node_labeled,
    edge_w1,
    edge_b1,
    edge_w2,
    edge_b2,
    gru_wi,
    gru_bi,
    gru_wh,
    gru_bh,
    state_cot,
):
    weights = (edge_w1, edge_b1, edge_w2, edge_b2, gru_wi, gru_bi, gru_wh, gru_bh)
    micro, nodes, width = node_input.shape
    block = min(EDGE_BLOCK, edge_input.shape[2])
    section_id = lax.axis_index("section")
    first = section_id == 0
    count_local = jnp.sum(node_labeled.astype(jnp.float32))

    def batch_blocks(index):
        feats = lax.dynamic_index_in_dim(edge_input, index, 0, keepdims=False)
        source = lax.dynamic_index_in_dim(edge_source, index, 0, keepdims=False)
        target = lax.dynamic_index_in_dim(edge_target, index, 0, keepdims=False)
        valid = lax.dynamic_index_in_dim(edge_valid, index, 0, keepdims=False)
        return split_blocks(feats, source, target, valid, block)

    received = jnp.zeros((nodes, width), jnp.bfloat16)
    saved = []
    states_out = jnp.zeros((micro, nodes, width), jnp.float32)
    for tick in range(micro + 1):
        batch = tick - section_id
        live = (batch >= 0) & (batch < micro)
        index = jnp.clip(batch, 0, micro - 1)
        state_low = jnp.where(first, node_input[min(tick, micro - 1)], received)
        blocks = batch_blocks(index)
        gathered_low = forward_messages(state_low, blocks, weights).astype(jnp.bfloat16)
        fresh = gru_gates(gathered_low, state_low, weights)[0]
        saved.append((state_low, gathered_low))
        sending = fresh.astype(jnp.bfloat16)
        value = jnp.where(first, sending.astype(jnp.float32), fresh)
        states_out = jnp.where(
            live, lax.dynamic_update_index_in_dim(states_out, value, index, 0), states_out
        )
        if tick < micro:
            received = passed_along(sending, "section", 1)
    grad_received = jnp.zeros((nodes, width), jnp.bfloat16)
    grads_out = jnp.zeros((micro, nodes, width), jnp.float32)
    totals = tuple((jnp.zeros(w.shape, jnp.float32) for w in weights))
    for tick in range(micro + 1):
        batch = micro - tick - section_id
        live = (batch >= 0) & (batch < micro)
        index = jnp.clip(batch, 0, micro - 1)
        state_low, gathered_low = saved[micro - tick]
        labels = lax.dynamic_index_in_dim(node_labeled, index, 0, keepdims=False).astype(
            jnp.float32
        )
        top = lax.dynamic_index_in_dim(state_cot, index, 0, keepdims=False) * labels[:, None]
        upstream = jnp.where(first, grad_received.astype(jnp.float32), top)
        d_total, terms = backward_step(
            upstream, state_low, gathered_low, batch_blocks(index), weights
        )
        totals = tuple((acc + jnp.where(live, term, 0.0) for acc, term in zip(totals, terms)))
        sending = d_total.astype(jnp.bfloat16)
        value = jnp.where(first, d_total, sending.astype(jnp.float32))
        grads_out = jnp.where(
            live, lax.dynamic_update_index_in_dim(grads_out, value, index, 0), grads_out
        )
        if tick < micro:
            grad_received = passed_along(sending, "section", -1)
    count_total = lax.psum(count_local, "dp")
    summed = lax.psum(
        (totals[0], totals[1], totals[2], totals[3], totals[4], totals[5], totals[6], totals[7]),
        ("section", "dp"),
    )
    scaled = [g / count_total for g in summed]
    return (
        states_out[None],
        grads_out[None],
        scaled[0],
        scaled[1],
        scaled[2],
        scaled[3],
        scaled[4],
        scaled[5],
        scaled[6],
        scaled[7],
    )


def solution(mesh):
    placed = (
        P(None, "dp", None), P(None, None, "dp"), P(None, "dp"), P(None, "dp"), P(None, "dp"),
        P(None, "dp"), P(), P(), P(), P(), P(), P(), P(), P(), P(None, "dp", None),
    )
    fits = LANE % (2 * mesh.shape["dp"]) == 0
    return jax.shard_map(
        shards if fits else plain_shards,
        mesh=mesh,
        in_specs=placed,
        out_specs=(P("section", None, "dp", None), P("section", None, "dp", None)) + (P(),) * 8,
        check_vma=False,
    )
```

```python
import functools

import jax
import jax.numpy as jnp
from jax import lax
from jax.experimental import pallas as pl
from jax.experimental.pallas import tpu as pltpu
from jax.sharding import PartitionSpec as P

BF, F32 = jnp.bfloat16, jnp.float32
VMEM = pltpu.VMEM
LANE = 128
ROUND = 32
SMALL_ROWS = 1024
PLANE = 4
SEMS = 160


def dot(a, b, ca=1, cb=0):
    return lax.dot_general(a, b, (((ca,), (cb,)), ((), ())), preferred_element_type=F32)


def split(x, parts):
    out = []
    for _ in range(parts - 1):
        piece = x.astype(BF)
        out.append(piece)
        x = x - piece.astype(F32)
    out.append(x.astype(BF))
    return out


def loop(count, body):
    def step(i, carry):
        body(i)
        return carry

    lax.fori_loop(0, count, step, 0)


def aligned(i, size):
    return pl.ds(pl.multiple_of(i * size, size), size)


def edge_tables(ends, nodes):
    ids = lax.broadcasted_iota(jnp.int32, (nodes, ends.shape[1]), 0).astype(F32)
    pick = (ids == ends[0:1]).astype(F32).astype(BF)
    put = (ids == ends[1:2]).astype(F32).astype(BF)
    return pick, put


def pack_ends(src_ref, tgt_ref, valid_ref, lab_ref, s):
    row = pl.ds(s, 1)
    src = src_ref[row, :].astype(F32)
    tgt = jnp.where(valid_ref[row, :] > 0, tgt_ref[row, :], -1).astype(F32)
    lab = lab_ref[row, :].astype(F32)
    edges, nodes = src.shape[1], lab.shape[1]
    lab = jnp.concatenate([lab, jnp.zeros((1, edges - nodes), F32)], axis=1)
    return jnp.concatenate([src, tgt, lab, jnp.zeros((13, edges), F32)], axis=0)


def edge_hidden(feats, w1, b1):
    bias = jnp.broadcast_to(b1.astype(F32), (LANE, LANE)).T[:, 0:1]
    return dot(w1, feats, 0, 0) + bias


def gru_forward(m, h, wi, bi, wh, bh):
    w = h.shape[1]
    gi = dot(m, wi) + bi.astype(F32)
    gh = dot(h, wh) + bh.astype(F32)
    r = jax.nn.sigmoid(gi[:, :w] + gh[:, :w])
    u = jax.nn.sigmoid(gi[:, w : 2 * w] + gh[:, w : 2 * w])
    n = jnp.tanh(gi[:, 2 * w :] + r * gh[:, 2 * w :])
    fresh = (1.0 - u) * n + u * h.astype(F32)
    return fresh, gh[:, 2 * w :], r, u, n


def gru_backward(g, h, gates, wi, wh):
    _, ghn, r, u, n = gates
    dn = g * (1.0 - u)
    du = g * (h.astype(F32) - n)
    dnpre = dn * (1.0 - n * n)
    dupre = du * u * (1.0 - u)
    drpre = dnpre * ghn * r * (1.0 - r)
    dgi = jnp.concatenate([drpre, dupre, dnpre], axis=1).astype(BF)
    dgh = jnp.concatenate([drpre, dupre, dnpre * r], axis=1).astype(BF)
    dm = dot(dgi, wi, 1, 1).astype(BF)
    dh = g * u + dot(dgh, wh, 1, 1)
    return dgi, dgh, dm, dh


class Net:
    def __init__(self, send_sems, recv_sems):
        self.send_sems, self.recv_sems = send_sems, recv_sems
        self.slots, self.sent, self.settled = {}, [], 0

    def slot(self, key):
        return self.slots.setdefault(key, len(self.slots))

    def send(self, key, src, dst, peer):
        copy = pltpu.make_async_remote_copy(
            src_ref=src,
            dst_ref=dst,
            send_sem=self.send_sems.at[len(self.sent)],
            recv_sem=self.recv_sems.at[self.slot(key)],
            device_id=peer,
            device_id_type=pl.DeviceIdType.MESH,
        )
        copy.start()
        self.sent.append(copy)

    def wait(self, key, region, peer):
        pltpu.make_async_remote_copy(
            src_ref=region,
            dst_ref=region,
            send_sem=self.send_sems.at[0],
            recv_sem=self.recv_sems.at[self.slot(key)],
            device_id=peer,
            device_id_type=pl.DeviceIdType.MESH,
        ).wait_recv()

    def drain(self):
        self.settle(len(self.sent))

    def settle(self, count):
        for copy in self.sent[self.settled : count]:
            copy.wait_send()
        self.settled = max(self.settled, count)


class Place:
    def __init__(self, parts):
        self.parts, self.plane = parts, PLANE
        self.lines = parts // PLANE
        self.s, self.c = lax.axis_index("section"), lax.axis_index("dp")
        self.sibling = {"section": 1 - self.s}

    def flip(self, mask):
        at, bit = self.c, 1
        while bit <= mask:
            if mask & bit:
                at = at + bit * (1 - 2 * lax.rem(lax.div(self.c, bit), 2))
            bit *= 2
        return at

    def peer(self, mask):
        return {"dp": self.flip(mask)}

    def block(self, mask):
        return self.s * self.parts + self.flip(mask)

    def spot(self, line):
        return self.s * self.lines + lax.div(self.flip(line * self.plane), self.plane)

    def level(self, line):
        own = lax.div(self.flip(line * self.plane), self.plane) * self.plane
        return self.s * self.parts + own


class LineGather:
    def __init__(self, net, place, name, buf):
        self.net, self.place, self.name, self.buf = net, place, name, buf

    def block(self, line):
        return self.buf.at[self.place.spot(line)]

    def begin(self):
        p = self.place
        for line in range(1, p.lines):
            ref = self.block(0)
            self.net.send((self.name, line), ref, ref, p.peer(line * PLANE))

    def middle(self):
        p = self.place
        for line in range(1, p.lines):
            self.net.wait((self.name, line), self.block(line), p.peer(line * PLANE))
        ref = self.buf.at[pl.ds(p.s * p.lines, p.lines)]
        self.net.send((self.name, "sib"), ref, ref, p.sibling)

    def finish(self):
        p = self.place
        ref = self.buf.at[pl.ds((1 - p.s) * p.lines, p.lines)]
        self.net.wait((self.name, "sib"), ref, p.sibling)


def main_kernel(
    x_ref, f_ref, src_ref, tgt_ref, val_ref, lab_ref, w1_ref, b1_ref, w2_hbm, b2_ref,
    wi_ref, bi_ref, wh_ref, bh_ref, cot_ref,
    full_out, states_out, grads_out, w1_out,
    w2, amat, acc, zaug, zpre_s, hs, hsl, dms, dml, dzacc, picks, puts,
    ins, hid, dts, qst, zall, part, sums, tmp, small, small_in, small_lo, small_line, small_plane,
    w1_io, swap, w2_sems, send_sems, recv_sems,
):
    edges, nodes = f_ref.shape[2], x_ref.shape[1]
    tiles5 = edges // LANE
    parts = full_out.shape[0] // 2
    blocks = 2 * parts
    per = LANE // blocks
    place = Place(parts)
    net = Net(send_sems, recv_sems)
    s, c = place.s, place.c
    me = place.block(0)
    here = place.spot(0)
    group = 2 * place.lines
    rounds = LANE // ROUND

    barrier = pltpu.get_barrier_semaphore()
    peers = [place.peer(q) for q in range(1, PLANE)]
    peers += [place.peer(line * PLANE) for line in range(1, place.lines)] + [place.sibling]
    for peer in peers:
        pl.semaphore_signal(
            barrier, inc=1, device_id=peer, device_id_type=pl.DeviceIdType.MESH
        )

    def w2_copy(ib):
        part = aligned(ib, ROUND * LANE)
        return pltpu.make_async_copy(w2_hbm.at[:, part], w2.at[:, part], w2_sems.at[ib])

    for ib in range(rounds):
        w2_copy(ib).start()

    feats = f_ref[s]
    ends = pack_ends(src_ref, tgt_ref, val_ref, lab_ref, s)
    h0 = x_ref[s]
    for e in range(tiles5):
        ins[here, e * 16 : (e + 1) * 16, :] = feats[:, e * LANE : (e + 1) * LANE]
    table = [ends[q : q + 1, e * LANE : (e + 1) * LANE] for q in range(2) for e in range(tiles5)]
    table.append(ends[2:3, :nodes])
    table.append(jnp.zeros((16 - len(table), LANE), F32))
    ins[here, tiles5 * 16 : (tiles5 + 1) * 16, :] = jnp.concatenate(table, axis=0).astype(BF)
    hid[0, here] = h0
    pick, put = edge_tables(ends, nodes)
    picks[...] = pick
    puts[...] = put
    zpre = edge_hidden(feats, w1_ref[...], b1_ref[...])
    zpre_s[...] = zpre
    zaug[0:LANE] = jax.nn.silu(zpre).astype(BF)
    zaug[LANE : 2 * LANE] = jnp.ones((LANE, edges), BF)

    def sources(t, h):
        got = dot(h, picks[...], 0, 0)
        hs[t] = got
        hsl[:, t * edges : (t + 1) * edges] = got.astype(BF)

    sources(0, h0)
    lane = lax.broadcasted_iota(jnp.int32, (LANE, LANE), 1)
    b2t = b2_ref[...].T
    tiles = [(e, min(256, edges - e)) for e in range(0, edges, 256)]

    gather_in = LineGather(net, place, "in", ins)
    gather_h0 = LineGather(net, place, "h0", hid.at[0])
    gather_h1 = LineGather(net, place, "h1", hid.at[1])
    gather_d2 = LineGather(net, place, "d2", dts.at[1])
    gather_d1 = LineGather(net, place, "d1", dts.at[0])

    def keep(i, e, w, p):
        p = p.reshape(16, 8, w).sum(0)
        for o in range(0, w, LANE):
            acc[(e + o) // LANE, aligned(i, 8), :] = p[:, o : o + LANE]

    def first(ib):
        w2_copy(ib).wait()
        lhs = []
        for v in range(ROUND):
            i = ib * ROUND + v
            bias = jnp.where(lane == i, b2t, jnp.zeros_like(b2t))
            lhs.append(jnp.concatenate([w2[:, aligned(i, LANE)].T, bias], axis=1))
        lhs = jnp.concatenate(lhs, axis=0)
        for e, w in tiles:
            a = dot(lhs, zaug[:, e : e + w]).astype(BF)
            amat[aligned(ib, ROUND * LANE), e : e + w] = a
            for v in range(ROUND):
                p = a[v * LANE : (v + 1) * LANE].astype(F32) * hs[0, :, e : e + w]
                keep(ib * ROUND + v, e, w, p)

    loop(rounds // 2, first)
    pl.semaphore_wait(barrier, len(peers))
    gather_in.begin()
    gather_h0.begin()
    loop(rounds - rounds // 2, lambda ib: first(ib + rounds // 2))

    def again(ib):
        for e, w in tiles:
            for v in range(8):
                a = amat[aligned(ib * 8 + v, LANE), e : e + w]
                keep(ib * 8 + v, e, w, a.astype(F32) * hs[1, :, e : e + w])

    def gathered():
        msg = []
        for e in range(tiles5):
            part = acc[e, pl.ds(0, LANE, stride=8), :]
            for q in range(1, 8):
                part = part + acc[e, pl.ds(q, LANE, stride=8), :]
            msg.append(part)
        msg = jnp.concatenate(msg, axis=1)
        total = jnp.zeros((nodes, LANE), F32)
        for piece in split(msg, 3):
            total = total + dot(puts[...], piece, 1, 1)
        return total.astype(BF)

    weights = (wi_ref[...], bi_ref[...].reshape(1, -1), wh_ref[...], bh_ref[...].reshape(1, -1))
    m1 = gathered()
    gates1 = gru_forward(m1, h0, *weights)
    h1 = gates1[0].astype(BF)
    hid[1, here] = h1
    gather_h1.begin()
    sources(1, h1)
    loop(LANE // 8, again)
    m2 = gathered()
    gates2 = gru_forward(m2, h1, *weights)
    h2 = gates2[0]
    label = jnp.broadcast_to(ends[2:3, :nodes], (LANE, nodes)).T
    g2 = cot_ref[s] * label
    dgi2, dgh2, dm2, dh2 = gru_backward(g2, h1, gates2, weights[0], weights[2])
    dt2 = dm2.T
    dts[1, here] = dt2
    gather_d2.begin()

    def spread(t, dt):
        got = dot(dt, puts[...])
        dms[t] = got
        dml[:, t * edges : (t + 1) * edges] = got.astype(BF)

    def to_source_tile(t, e):
        def body(ib, total):
            d = dms[t, aligned(ib, 8), e * LANE : (e + 1) * LANE]
            for v in range(8):
                a = amat[aligned(ib * 8 + v, LANE), e * LANE : (e + 1) * LANE].astype(F32)
                total = total + a * d[v : v + 1]
            return total

        return lax.fori_loop(0, LANE // 8, body, jnp.zeros((LANE, LANE), F32))

    def to_nodes(outs):
        back = jnp.concatenate(outs, axis=1)
        total = jnp.zeros((nodes, LANE), F32)
        for piece in split(back, 3):
            total = total + dot(picks[...], piece, 1, 1)
        return total

    spread(1, dt2)
    back2 = [to_source_tile(1, e) for e in range(tiles5)]
    gather_in.middle()
    gather_h0.middle()
    gather_h1.middle()
    d1 = (dh2 + to_nodes(back2)).astype(BF)
    dgi1, dgh1, dm1, dh1 = gru_backward(d1.astype(F32), h0, gates1, weights[0], weights[2])
    dt1 = dm1.T
    dts[0, here] = dt1
    gather_d1.begin()
    gather_d2.middle()

    gather_in.finish()
    gather_h0.finish()
    gather_h1.finish()
    dzacc[...] = jnp.zeros_like(dzacc)

    def back_hidden(ib):
        total = dzacc[...]
        for a in range(2):
            d = [dms[t, aligned(ib * 2 + a, 8), :] for t in range(2)]
            for v in range(8):
                both = hs[0] * d[0][v : v + 1] + hs[1] * d[1][v : v + 1]
                qst[a, v * LANE : (v + 1) * LANE, 0:edges] = both.astype(BF)
            total = total + dot(w2[:, aligned(ib * 2 + a, 8 * LANE)], qst[a, :, 0:edges])
        dzacc[...] = total

    units = PLANE * per
    ks = lax.broadcasted_iota(jnp.int32, (units, LANE), 0)
    ks = (lax.div(ks, per) * 2 + s) * per + lax.rem(ks, per) + lax.div(c, PLANE) * (2 * units)
    sel = (ks == lax.broadcasted_iota(jnp.int32, (units, LANE), 1)).astype(F32)
    w1t = dot(sel.astype(BF), w1_ref[...], 1, 1).astype(BF)
    b1 = jnp.sum(sel * b1_ref[...].astype(F32), axis=1, keepdims=True)
    quarter = nodes // 4
    qn = lax.broadcasted_iota(jnp.int32, (quarter, 256), 0).astype(F32)
    sn = lax.broadcasted_iota(jnp.int32, (nodes, 256), 0).astype(F32)

    def hidden(blk):
        cols = [ins[blk, e * 16 : (e + 1) * 16, :] for e in range(tiles5)]
        z = jax.nn.silu(dot(w1t, jnp.concatenate(cols, axis=1)) + b1)
        zall[blk] = z.astype(BF).astype(F32)

    def build(blk):
        z = zall[blk]
        en = ins[blk, tiles5 * 16 : (tiles5 + 1) * 16, :].astype(F32)
        pairs = []
        for q in range(4):
            lo = q * LANE
            zq = z[:, lo : lo + 256]
            src = jnp.concatenate([en[q : q + 1], en[q + 1 : q + 2]], axis=1)
            tgt = jnp.concatenate(
                [en[tiles5 + q : tiles5 + q + 1], en[tiles5 + q + 1 : tiles5 + q + 2]], axis=1
            )
            hit_t = (qn + float(q * quarter)) == tgt
            hit_s = (sn == src).astype(F32).astype(BF)
            lhs = [jnp.where(hit_t, zq[k : k + 1], 0.0).astype(BF) for k in range(units)]
            pairs.append(dot(jnp.concatenate(lhs, axis=0), hit_s, 1, 1))
        pairs = jnp.concatenate(split(jnp.concatenate(pairs, axis=0), 2), axis=1)
        h = jnp.concatenate([hid[0, blk], hid[1, blk]], axis=1)
        got = dot(pairs, jnp.concatenate([h, h], axis=0)).astype(BF)
        for q in range(4):
            at = pl.ds(pl.multiple_of(blk * nodes + q * quarter, quarter), quarter)
            for k in range(units):
                part = got[(q * units + k) * quarter : (q * units + k + 1) * quarter]
                for t in range(2):
                    qst[t, at, k * LANE : (k + 1) * LANE] = part[:, t * LANE : (t + 1) * LANE]

    for blk in range(group):
        hidden(blk)

    def build_pair(b):
        build(2 * b)
        build(2 * b + 1)

    loop(group // 2, build_pair)
    gather_d1.middle()
    gather_d2.finish()
    lhs = jnp.concatenate([dts[1, blk] for blk in range(group)], axis=1)
    part[...] = dot(lhs, qst[1])
    count = jnp.zeros((1, LANE), F32)
    for blk in range(group):
        count = count + ins[blk, tiles5 * 16 : (tiles5 + 1) * 16, :].astype(F32)[10:11]
    count = jnp.concatenate([count, jnp.zeros((15, LANE), F32)], axis=0).astype(BF)
    mid = per * LANE // 2
    early = len(net.sent)
    pieces = (pl.ds(0, 16 + mid), pl.ds(16 + mid, per * LANE - mid))

    def send_sums(ch, q):
        ref = sums.at[0, lax.rem(place.flip(q), PLANE), pieces[ch]]
        net.send(("sums", ch, q), ref, sums.at[1, q, pieces[ch]], place.peer(q))

    def add_sums(ch):
        total = sums[0, q_me, pieces[ch], :].astype(F32)
        for q in range(1, PLANE):
            net.wait(("sums", ch, q), sums.at[1, q, pieces[ch]], place.peer(q))
            total = total + sums[1, q, pieces[ch], :].astype(F32)
        return total

    gather_d1.finish()
    lhs = jnp.concatenate([dts[0, blk] for blk in range(group)], axis=1)
    for q in (3, 1, 2, 0):
        to = lax.rem(place.flip(q), PLANE)
        cols = aligned(to, per * LANE)
        got = part[:, cols] + dot(lhs, qst[0, :, cols])
        for k in range(per):
            tmp[q, pl.ds(k, LANE, stride=per), :] = got[:, k * LANE : (k + 1) * LANE]
        sums[0, to, 0:16] = count
        sums[0, to, 16:] = tmp[q].astype(BF)
        if q:
            send_sums(0, q)
    for q in (3, 1, 2):
        send_sums(1, q)

    half = SMALL_ROWS // 2
    plane_rows = half // place.lines
    own_rows = plane_rows // PLANE
    gwi = dot(m1, dgi1, 0, 0) + dot(m2, dgi2, 0, 0)
    gwh = dot(h0, dgh1, 0, 0) + dot(h1, dgh2, 0, 0)
    for q in range(3):
        small[q * LANE : (q + 1) * LANE] = gwi[:, q * LANE : (q + 1) * LANE]
        small[(3 + q) * LANE : (4 + q) * LANE] = gwh[:, q * LANE : (q + 1) * LANE]
    spread(0, dt1)
    small[6 * LANE : 7 * LANE] = dot(dml[...], hsl[...], 1, 1)
    gbi = dgi1.astype(F32).sum(0, keepdims=True) + dgi2.astype(F32).sum(0, keepdims=True)
    gbh = dgh1.astype(F32).sum(0, keepdims=True) + dgh2.astype(F32).sum(0, keepdims=True)
    rows = [x[:, q * LANE : (q + 1) * LANE] for x in (gbi, gbh) for q in range(3)]
    rows.append(jnp.zeros((SMALL_ROWS - 7 * LANE - 6, LANE), F32))
    small[7 * LANE :] = jnp.concatenate(rows, axis=0)
    net.send(("small", "sib"), small.at[aligned(1 - s, half)], small_in, place.sibling)

    q_me = lax.rem(c, PLANE)
    back1 = [to_source_tile(0, e) for e in range(2)]
    net.wait(("small", "sib"), small_in, place.sibling)
    small_lo[...] = (small[aligned(s, half), :] + small_in[...]).astype(BF)
    z = lax.div(c, PLANE)
    for line in range(1, place.lines):
        to = lax.div(place.flip(line * PLANE), PLANE)
        net.send(
            ("small", "line", line),
            small_lo.at[aligned(to, plane_rows)],
            small_line.at[line],
            place.peer(line * PLANE),
        )

    size = full_out.shape[1]
    tail = size // 8 // 16 * 16
    top = size - tail
    cut = (mid // 32 * 16, mid + (top - mid) // 32 * 16)
    halves = (
        (pl.ds(0, cut[0]), pl.ds(cut[0], mid - cut[0])),
        (pl.ds(mid, cut[1] - mid), pl.ds(cut[1], top - cut[1])),
    )
    chunk = (pl.ds(0, mid), pl.ds(mid, top - mid))
    last = pl.ds(top, tail)

    def out_begin(ch):
        def along(line):
            ref = full_out.at[me, chunk[ch]]
            net.send(("out", ch, line), ref, ref, place.peer(line * PLANE))

        along(1)
        for q in (1, 2):
            ref = full_out.at[me, chunk[ch]]
            net.send(("out", ch, 0, q), ref, ref, place.peer(q))
        for line in range(2, place.lines):
            along(line)

    def out_line(ch, line):
        mask = line * PLANE
        blk = place.block(mask)
        net.wait(("out", ch, line), full_out.at[blk, chunk[ch]], place.peer(mask))
        for q in (1, 2):
            ref = full_out.at[blk, chunk[ch]]
            net.send(("out", ch, line, q), ref, ref, place.peer(q))

    def out_cross(ch, line):
        for q, a in ((1, 0), (2, 1)):
            blk = place.block(line * PLANE + q)
            net.wait(("out", ch, line, q), full_out.at[blk, chunk[ch]], place.peer(q))
            ref = full_out.at[blk, halves[ch][a]]
            net.send(("out", ch, line, 3, a), ref, ref, place.peer(3 - q))

    def last_planes():
        for q in range(1, PLANE):
            ref = full_out.at[me, last]
            net.send(("last", 0, q), ref, ref, place.peer(q))

    def last_lines():
        for q in range(1, PLANE):
            net.wait(("last", 0, q), full_out.at[place.block(q), last], place.peer(q))
        ref = full_out.at[pl.ds(place.level(0), PLANE), last]
        for line in range(1, place.lines):
            net.send(("last", line), ref, ref, place.peer(line * PLANE))

    def out_level(line):
        for ch in range(2):
            for q, a in ((2, 0), (1, 1)):
                ref = full_out.at[place.block(line * PLANE + 3), halves[ch][a]]
                net.wait(("out", ch, line, 3, a), ref, place.peer(q))
        if line > 0:
            part = full_out.at[pl.ds(place.level(line), PLANE), last]
            net.wait(("last", line), part, place.peer(line * PLANE))
        ref = full_out.at[pl.ds(place.level(line), PLANE)]
        net.send(("out", "sib", line), ref, ref, place.sibling)

    net.settle(early)
    total = add_sums(0)
    scale = 1.0 / jnp.sum(total[0:1], axis=1, keepdims=True)
    full_out[me, 0:mid] = (total[16:] * scale).astype(BF)
    out_begin(0)
    back1 += [to_source_tile(0, e) for e in range(2, 4)]
    own = small_lo[aligned(z, plane_rows), :].astype(F32)
    for line in range(1, place.lines):
        net.wait(("small", "line", line), small_line.at[line], place.peer(line * PLANE))
        own = own + small_line[line].astype(F32)
    small_line[0] = own.astype(BF)
    for q in range(1, PLANE):
        to = lax.rem(place.flip(q), PLANE)
        net.send(
            ("small", "plane", q),
            small_line.at[0, aligned(to, own_rows)],
            small_plane.at[q],
            place.peer(q),
        )
    full_out[me, mid : per * LANE] = (add_sums(1) * scale).astype(BF)
    out_begin(1)
    mark = len(net.sent)
    out_cross(0, 0)
    back1 += [to_source_tile(0, e) for e in range(4, tiles5)]
    d0 = dh1 + to_nodes(back1)

    zero = s == 0
    swap[0, 0] = jnp.where(zero, h2, h1.astype(F32))
    swap[0, 1] = jnp.where(zero, d1.astype(F32), d0)
    net.send(("swap",), swap.at[0], swap.at[1], place.sibling)
    own = small_line[0, aligned(q_me, own_rows), :].astype(F32)
    for q in range(1, PLANE):
        net.wait(("small", "plane", q), small_plane.at[q], place.peer(q))
        own = own + small_plane[q].astype(F32)
    full_out[me, per * LANE : per * LANE + own_rows] = (own * scale).astype(BF)
    last_planes()
    out_line(0, 1)
    out_cross(1, 0)
    loop(3, back_hidden)
    for line in range(2, place.lines):
        out_line(0, line)
    out_line(1, 1)
    out_cross(0, 1)
    last_lines()
    loop(3, lambda ib: back_hidden(ib + 3))
    for line in range(2, place.lines):
        out_line(1, line)
    out_cross(1, 1)
    out_cross(0, 2)
    out_level(0)
    mark = len(net.sent)
    loop(LANE // 16 - 6, lambda ib: back_hidden(ib + 6))
    zp = zpre_s[...]
    sig = jax.nn.sigmoid(zp)
    slope = sig * (1.0 + zp * (1.0 - sig))
    lhs = jnp.concatenate(
        [feats, jnp.ones((1, edges), BF), jnp.zeros((15, edges), BF)], axis=0
    )
    total = dot(lhs, (dzacc[...] * slope).astype(BF), 1, 1)
    w1_io[0] = total[0:24]
    net.send(("w1", "sib"), w1_io.at[0], w1_io.at[1], place.sibling)
    for line in range(3, place.lines):
        out_cross(0, line)
    out_cross(1, 2)
    net.wait(("w1", "sib"), w1_io.at[1], place.sibling)
    total = w1_io[0] + w1_io[1]
    w1_io[2] = total
    at = 4
    for line in range(1, place.lines):
        net.send(("w1", "line", line), w1_io.at[2], w1_io.at[at + line], place.peer(line * PLANE))
    net.wait(("swap",), swap.at[1], place.sibling)
    mine_state = jnp.where(zero, h1.astype(F32), h2)
    mine_grad = jnp.where(zero, d0, d1.astype(F32))
    states_out[0] = jnp.where(zero, mine_state, swap[1, 0])
    states_out[1] = jnp.where(zero, swap[1, 0], mine_state)
    grads_out[0] = jnp.where(zero, mine_grad, swap[1, 1])
    grads_out[1] = jnp.where(zero, swap[1, 1], mine_grad)
    for line in range(3, place.lines):
        out_cross(1, line)
    out_level(1)
    for line in range(1, place.lines):
        net.wait(("w1", "line", line), w1_io.at[at + line], place.peer(line * PLANE))
        total = total + w1_io[at + line]
    w1_io[3] = total
    at += place.lines
    for q in range(1, PLANE):
        net.send(("w1", "plane", q), w1_io.at[3], w1_io.at[at + q], place.peer(q))
    net.settle(mark)
    for line in range(2, place.lines):
        out_level(line)
    for q in range(1, PLANE):
        net.wait(("w1", "plane", q), w1_io.at[at + q], place.peer(q))
        total = total + w1_io[at + q]
    w1_out[...] = total * scale
    for line in range(place.lines):
        first = place.level(line) + (1 - 2 * s) * parts
        net.wait(("out", "sib", line), full_out.at[pl.ds(first, PLANE)], place.sibling)
    net.drain()


def final_kernel(full_ref, w1_ref, st_ref, sg_ref, w2_out, b2_out, wi_out, bi_out, wh_out, bh_out,
                 gw1_out, gb1_out, st_out, sg_out, flat, out_sems):
    blocks = full_ref.shape[0]
    parts = blocks // 2
    width = b2_out.shape[0]
    rows = width * (width // blocks)

    def put(c):
        part = aligned(c, 8)
        return pltpu.make_async_copy(flat.at[part], w2_out.at[part], out_sems.at[c])

    gw1_out[...] = w1_ref[0:16]
    gb1_out[...] = w1_ref[16:17]
    st_out[...] = st_ref[...]
    sg_out[...] = sg_ref[...]
    low = lax.broadcasted_iota(jnp.int32, (1, 8, LANE), 1) < 4

    def place_rows(c):
        a = full_ref[c, :rows].astype(F32).reshape(rows // 8, 8, LANE)
        b = full_ref[c + parts, :rows].astype(F32).reshape(rows // 8, 8, LANE)
        even = jnp.where(low, a, pltpu.roll(b, 4, 1))
        odd = jnp.where(low, pltpu.roll(a, 4, 1), b)
        for p in range(rows // 8):
            flat[aligned(c, 8), (2 * p) * LANE : (2 * p + 1) * LANE] = even[p]
            flat[aligned(c, 8), (2 * p + 1) * LANE : (2 * p + 2) * LANE] = odd[p]
        put(c).start()

    loop(parts, place_rows)
    x = full_ref[:, rows:].astype(F32).reshape(-1, LANE)
    for q in range(3):
        cols = slice(q * LANE, (q + 1) * LANE)
        wi_out[:, cols] = x[q * LANE : (q + 1) * LANE]
        wh_out[:, cols] = x[(3 + q) * LANE : (4 + q) * LANE]
        bi_out[cols] = x[7 * LANE + q]
        bh_out[cols] = x[7 * LANE + 3 + q]
    b2_out[...] = x[6 * LANE : 7 * LANE]
    loop(parts, lambda c: put(c).wait())


def shards(
    node_input, edge_input, edge_source, edge_target, edge_valid, node_labeled,
    edge_w1, edge_b1, edge_w2, edge_b2, gru_wi, gru_bi, gru_wh, gru_bh, state_cot,
):
    micro, nodes, width = node_input.shape
    edges = edge_input.shape[2]
    parts = lax.axis_size("dp")
    blocks = 2 * parts
    per = width // blocks
    lines = parts // PLANE
    group, units = 2 * lines, PLANE * per
    half = SMALL_ROWS // 2
    plane_rows = half // lines
    own_rows = plane_rows // PLANE
    size = width * per + own_rows
    vm = pl.BlockSpec(memory_space=VMEM)
    hbm = pl.BlockSpec(memory_space=pl.ANY)
    sds = jax.ShapeDtypeStruct
    full, states, grads, gw1 = pl.pallas_call(
        main_kernel,
        out_shape=(
            VMEM((blocks, size, width), BF), VMEM((2, nodes, width), F32),
            VMEM((2, nodes, width), F32), VMEM((24, width), F32),
        ),
        in_specs=[vm] * 8 + [hbm] + [vm] * 6,
        out_specs=[vm] * 4,
        scratch_shapes=[
            VMEM((width, width * width), BF), VMEM((width * width, edges), BF),
            VMEM((edges // LANE, 8 * width, LANE), F32), VMEM((2 * width, edges), BF),
            VMEM((width, edges), F32), VMEM((2, width, edges), F32),
            VMEM((width, 2 * edges), BF), VMEM((2, width, edges), F32),
            VMEM((width, 2 * edges), BF),
            VMEM((width, edges), F32), VMEM((nodes, edges), BF), VMEM((nodes, edges), BF),
            VMEM((group, 16 * (edges // LANE + 1), LANE), BF),
            VMEM((2, group, nodes, width), BF), VMEM((2, group, width, nodes), BF),
            VMEM((2, group * nodes, units * width), BF), VMEM((group, units, edges), F32),
            VMEM((width, units * width), F32),
            VMEM((2, PLANE, per * width + 16, width), BF),
            VMEM((PLANE, width * per, width), F32),
            VMEM((SMALL_ROWS, width), F32), VMEM((half, width), F32),
            VMEM((half, width), BF), VMEM((lines, plane_rows, width), BF),
            VMEM((PLANE, own_rows, width), BF), VMEM((4 + lines + PLANE, 24, width), F32),
            VMEM((2, 2, nodes, width), F32),
            pltpu.SemaphoreType.DMA((width // ROUND,)),
            pltpu.SemaphoreType.DMA((SEMS,)), pltpu.SemaphoreType.DMA((SEMS,)),
        ],
        compiler_params=pltpu.CompilerParams(
            collective_id=0, has_side_effects=True, vmem_limit_bytes=57 * 2**20
        ),
    )(
        node_input, edge_input, edge_source, edge_target, edge_valid, node_labeled,
        edge_w1, edge_b1.reshape(1, -1), edge_w2, edge_b2.reshape(width, width),
        gru_wi, gru_bi, gru_wh, gru_bh, state_cot,
    )

    w2, b2, wi, bi, wh, bh, w1, b1, states, grads = pl.pallas_call(
        final_kernel,
        out_shape=(
            sds((width, width * width), F32), sds((width, width), F32),
            sds((width, 3 * width), F32), sds((3 * width,), F32),
            sds((width, 3 * width), F32), sds((3 * width,), F32),
            sds((16, width), F32), sds((1, width), F32),
            sds((2, nodes, width), F32), sds((2, nodes, width), F32),
        ),
        in_specs=[vm] * 4,
        out_specs=[hbm] + [vm] * 9,
        scratch_shapes=[
            VMEM((width, width * width), F32), pltpu.SemaphoreType.DMA((parts,)),
        ],
        compiler_params=pltpu.CompilerParams(vmem_limit_bytes=40 * 2**20),
    )(full, gw1, states, grads)
    return (
        states[None], grads[None], w1, b1.reshape(-1), w2, b2.reshape(-1),
        wi, bi, wh, bh,
    )


EDGE_BLOCK = 128


def passed_along(value, axis, steps):
    count = lax.axis_size(axis)
    leading, last = (max(0, -steps), min(count, count - steps))
    return lax.ppermute(value, axis, [(source, source + steps) for source in range(leading, last)])


def split_blocks(feats, source, target, valid, block):
    count = feats.shape[1] // block
    return (
        feats.reshape(feats.shape[0], count, block).transpose(1, 0, 2),
        source.reshape(count, block),
        target.reshape(count, block),
        valid.reshape(count, block),
    )


def block_front(feats_b, source_b, weights, state_low):
    width = state_low.shape[1]
    zpre = jnp.dot(feats_b.T, weights[0], preferred_element_type=jnp.float32) + weights[1].astype(
        jnp.float32
    )
    z_low = jax.nn.silu(zpre).astype(jnp.bfloat16)
    amat = (
        jnp.dot(z_low, weights[2], preferred_element_type=jnp.float32)
        + weights[3].astype(jnp.float32)
    ).astype(jnp.bfloat16)
    amat = amat.reshape(-1, width, width)
    node_ids = lax.iota(jnp.int32, state_low.shape[0])
    pick = (source_b[:, None] == node_ids[None, :]).astype(jnp.bfloat16)
    h_source = jnp.dot(pick, state_low, preferred_element_type=jnp.float32).astype(jnp.bfloat16)
    return (zpre, z_low, amat, h_source)


def target_table(target_b, valid_b, nodes):
    node_ids = lax.iota(jnp.int32, nodes)
    return ((target_b[:, None] == node_ids[None, :]) & (valid_b[:, None] > 0)).astype(jnp.bfloat16)


def forward_messages(state_low, blocks, weights):
    nodes, width = state_low.shape

    def add(total, pieces):
        feats_b, source_b, target_b, valid_b = pieces
        _, _, amat, h_source = block_front(feats_b, source_b, weights, state_low)
        message = jnp.einsum("eij,ej->ei", amat, h_source, preferred_element_type=jnp.float32)
        message = message * (valid_b > 0).astype(jnp.float32)[:, None]
        return (total + jax.ops.segment_sum(message, target_b, num_segments=nodes), None)

    summed, _ = lax.scan(add, jnp.zeros((nodes, width), jnp.float32), blocks)
    return summed


def gru_gates(gathered_low, state_low, weights):
    width = state_low.shape[1]
    gate_in = jnp.dot(gathered_low, weights[4], preferred_element_type=jnp.float32) + weights[
        5
    ].astype(jnp.float32)
    gate_state = jnp.dot(state_low, weights[6], preferred_element_type=jnp.float32) + weights[
        7
    ].astype(jnp.float32)
    reset = jax.nn.sigmoid(gate_in[:, :width] + gate_state[:, :width])
    update = jax.nn.sigmoid(gate_in[:, width : 2 * width] + gate_state[:, width : 2 * width])
    candidate = jnp.tanh(gate_in[:, 2 * width :] + reset * gate_state[:, 2 * width :])
    fresh = (1.0 - update) * candidate + update * state_low.astype(jnp.float32)
    return (fresh, gate_state, reset, update, candidate)


def backward_step(upstream, state_low, gathered_low, blocks, weights):
    nodes, width = state_low.shape
    fresh, gate_state, reset, update, candidate = gru_gates(gathered_low, state_low, weights)
    state = state_low.astype(jnp.float32)
    d_cand = upstream * (1.0 - update)
    d_update = upstream * (state - candidate)
    d_state = upstream * update
    d_npre = d_cand * (1.0 - candidate * candidate)
    d_upre = d_update * update * (1.0 - update)
    d_rpre = d_npre * gate_state[:, 2 * width :] * reset * (1.0 - reset)
    d_in = jnp.concatenate([d_rpre, d_upre, d_npre], axis=1).astype(jnp.bfloat16)
    d_hid = jnp.concatenate([d_rpre, d_upre, d_npre * reset], axis=1).astype(jnp.bfloat16)
    grad_wi = jnp.dot(gathered_low.T, d_in, preferred_element_type=jnp.float32)
    grad_bi = jnp.sum(d_in.astype(jnp.float32), axis=0)
    grad_wh = jnp.dot(state_low.T, d_hid, preferred_element_type=jnp.float32)
    grad_bh = jnp.sum(d_hid.astype(jnp.float32), axis=0)
    d_state = d_state + jnp.dot(d_hid, weights[6].T, preferred_element_type=jnp.float32)
    d_gathered = jnp.dot(d_in, weights[4].T, preferred_element_type=jnp.float32).astype(
        jnp.bfloat16
    )

    def back_block(carry, pieces):
        d_src, grad_w1, grad_b1, grad_w2, grad_b2 = carry
        feats_b, source_b, target_b, valid_b = pieces
        zpre, z_low, amat, h_source = block_front(feats_b, source_b, weights, state_low)
        put = target_table(target_b, valid_b, nodes)
        d_msg = jnp.dot(put, d_gathered, preferred_element_type=jnp.float32).astype(jnp.bfloat16)
        d_amat = d_msg.astype(jnp.float32)[:, :, None] * h_source.astype(jnp.float32)[:, None, :]
        d_amat = d_amat.reshape(d_amat.shape[0], width * width).astype(jnp.bfloat16)
        grad_w2 = grad_w2 + jnp.dot(z_low.T, d_amat, preferred_element_type=jnp.float32)
        grad_b2 = grad_b2 + jnp.sum(d_amat.astype(jnp.float32), axis=0)
        d_z = jnp.dot(d_amat, weights[2].T, preferred_element_type=jnp.float32)
        sig = jax.nn.sigmoid(zpre)
        d_zpre = (d_z * sig * (1.0 + zpre * (1.0 - sig))).astype(jnp.bfloat16)
        grad_w1 = grad_w1 + jnp.dot(feats_b, d_zpre, preferred_element_type=jnp.float32)
        grad_b1 = grad_b1 + jnp.sum(d_zpre.astype(jnp.float32), axis=0)
        d_source = jnp.einsum("eij,ei->ej", amat, d_msg, preferred_element_type=jnp.float32)
        d_src = d_src + jax.ops.segment_sum(d_source, source_b, num_segments=nodes)
        return ((d_src, grad_w1, grad_b1, grad_w2, grad_b2), None)

    start = (
        jnp.zeros((nodes, width), jnp.float32),
        jnp.zeros(weights[0].shape, jnp.float32),
        jnp.zeros(weights[1].shape, jnp.float32),
        jnp.zeros(weights[2].shape, jnp.float32),
        jnp.zeros(weights[3].shape, jnp.float32),
    )
    ends, _ = lax.scan(back_block, start, blocks)
    d_total = d_state + ends[0]
    return (d_total, (ends[1], ends[2], ends[3], ends[4], grad_wi, grad_bi, grad_wh, grad_bh))


def plain_shards(
    node_input,
    edge_input,
    edge_source,
    edge_target,
    edge_valid,
    node_labeled,
    edge_w1,
    edge_b1,
    edge_w2,
    edge_b2,
    gru_wi,
    gru_bi,
    gru_wh,
    gru_bh,
    state_cot,
):
    weights = (edge_w1, edge_b1, edge_w2, edge_b2, gru_wi, gru_bi, gru_wh, gru_bh)
    micro, nodes, width = node_input.shape
    block = min(EDGE_BLOCK, edge_input.shape[2])
    section_id = lax.axis_index("section")
    first = section_id == 0
    count_local = jnp.sum(node_labeled.astype(jnp.float32))

    def batch_blocks(index):
        feats = lax.dynamic_index_in_dim(edge_input, index, 0, keepdims=False)
        source = lax.dynamic_index_in_dim(edge_source, index, 0, keepdims=False)
        target = lax.dynamic_index_in_dim(edge_target, index, 0, keepdims=False)
        valid = lax.dynamic_index_in_dim(edge_valid, index, 0, keepdims=False)
        return split_blocks(feats, source, target, valid, block)

    received = jnp.zeros((nodes, width), jnp.bfloat16)
    saved = []
    states_out = jnp.zeros((micro, nodes, width), jnp.float32)
    for tick in range(micro + 1):
        batch = tick - section_id
        live = (batch >= 0) & (batch < micro)
        index = jnp.clip(batch, 0, micro - 1)
        state_low = jnp.where(first, node_input[min(tick, micro - 1)], received)
        blocks = batch_blocks(index)
        gathered_low = forward_messages(state_low, blocks, weights).astype(jnp.bfloat16)
        fresh = gru_gates(gathered_low, state_low, weights)[0]
        saved.append((state_low, gathered_low))
        sending = fresh.astype(jnp.bfloat16)
        value = jnp.where(first, sending.astype(jnp.float32), fresh)
        states_out = jnp.where(
            live, lax.dynamic_update_index_in_dim(states_out, value, index, 0), states_out
        )
        if tick < micro:
            received = passed_along(sending, "section", 1)
    grad_received = jnp.zeros((nodes, width), jnp.bfloat16)
    grads_out = jnp.zeros((micro, nodes, width), jnp.float32)
    totals = tuple((jnp.zeros(w.shape, jnp.float32) for w in weights))
    for tick in range(micro + 1):
        batch = micro - tick - section_id
        live = (batch >= 0) & (batch < micro)
        index = jnp.clip(batch, 0, micro - 1)
        state_low, gathered_low = saved[micro - tick]
        labels = lax.dynamic_index_in_dim(node_labeled, index, 0, keepdims=False).astype(
            jnp.float32
        )
        top = lax.dynamic_index_in_dim(state_cot, index, 0, keepdims=False) * labels[:, None]
        upstream = jnp.where(first, grad_received.astype(jnp.float32), top)
        d_total, terms = backward_step(
            upstream, state_low, gathered_low, batch_blocks(index), weights
        )
        totals = tuple((acc + jnp.where(live, term, 0.0) for acc, term in zip(totals, terms)))
        sending = d_total.astype(jnp.bfloat16)
        value = jnp.where(first, d_total, sending.astype(jnp.float32))
        grads_out = jnp.where(
            live, lax.dynamic_update_index_in_dim(grads_out, value, index, 0), grads_out
        )
        if tick < micro:
            grad_received = passed_along(sending, "section", -1)
    count_total = lax.psum(count_local, "dp")
    summed = lax.psum(
        (totals[0], totals[1], totals[2], totals[3], totals[4], totals[5], totals[6], totals[7]),
        ("section", "dp"),
    )
    scaled = [g / count_total for g in summed]
    return (
        states_out[None],
        grads_out[None],
        scaled[0],
        scaled[1],
        scaled[2],
        scaled[3],
        scaled[4],
        scaled[5],
        scaled[6],
        scaled[7],
    )


def solution(mesh):
    placed = (
        P(None, "dp", None), P(None, None, "dp"), P(None, "dp"), P(None, "dp"), P(None, "dp"),
        P(None, "dp"), P(), P(), P(), P(), P(), P(), P(), P(), P(None, "dp", None),
    )
    fits = LANE % (2 * mesh.shape["dp"]) == 0
    return jax.shard_map(
        shards if fits else plain_shards,
        mesh=mesh,
        in_specs=placed,
        out_specs=(P("section", None, "dp", None), P("section", None, "dp", None)) + (P(),) * 8,
        check_vma=False,
    )
```

```python
import functools

import jax
import jax.numpy as jnp
from jax import lax
from jax.experimental import pallas as pl
from jax.experimental.pallas import tpu as pltpu
from jax.sharding import PartitionSpec as P

BF, F32 = jnp.bfloat16, jnp.float32
VMEM = pltpu.VMEM
LANE = 128
ROUND = 32
SMALL_ROWS = 1024
PLANE = 4
SEMS = 160


def dot(a, b, ca=1, cb=0):
    return lax.dot_general(a, b, (((ca,), (cb,)), ((), ())), preferred_element_type=F32)


def split(x, parts):
    out = []
    for _ in range(parts - 1):
        piece = x.astype(BF)
        out.append(piece)
        x = x - piece.astype(F32)
    out.append(x.astype(BF))
    return out


def loop(count, body):
    def step(i, carry):
        body(i)
        return carry

    lax.fori_loop(0, count, step, 0)


def aligned(i, size):
    return pl.ds(pl.multiple_of(i * size, size), size)


def edge_tables(ends, nodes):
    ids = lax.broadcasted_iota(jnp.int32, (nodes, ends.shape[1]), 0).astype(F32)
    pick = (ids == ends[0:1]).astype(F32).astype(BF)
    put = (ids == ends[1:2]).astype(F32).astype(BF)
    return pick, put


def pack_ends(src_ref, tgt_ref, valid_ref, lab_ref, s):
    row = pl.ds(s, 1)
    src = src_ref[row, :].astype(F32)
    tgt = jnp.where(valid_ref[row, :] > 0, tgt_ref[row, :], -1).astype(F32)
    lab = lab_ref[row, :].astype(F32)
    edges, nodes = src.shape[1], lab.shape[1]
    lab = jnp.concatenate([lab, jnp.zeros((1, edges - nodes), F32)], axis=1)
    return jnp.concatenate([src, tgt, lab, jnp.zeros((13, edges), F32)], axis=0)


def edge_hidden(feats, w1, b1):
    bias = jnp.broadcast_to(b1.astype(F32), (LANE, LANE)).T[:, 0:1]
    return dot(w1, feats, 0, 0) + bias


def gru_forward(m, h, wi, bi, wh, bh):
    w = h.shape[1]
    gi = dot(m, wi) + bi.astype(F32)
    gh = dot(h, wh) + bh.astype(F32)
    r = jax.nn.sigmoid(gi[:, :w] + gh[:, :w])
    u = jax.nn.sigmoid(gi[:, w : 2 * w] + gh[:, w : 2 * w])
    n = jnp.tanh(gi[:, 2 * w :] + r * gh[:, 2 * w :])
    fresh = (1.0 - u) * n + u * h.astype(F32)
    return fresh, gh[:, 2 * w :], r, u, n


def gru_backward(g, h, gates, wi, wh):
    _, ghn, r, u, n = gates
    dn = g * (1.0 - u)
    du = g * (h.astype(F32) - n)
    dnpre = dn * (1.0 - n * n)
    dupre = du * u * (1.0 - u)
    drpre = dnpre * ghn * r * (1.0 - r)
    dgi = jnp.concatenate([drpre, dupre, dnpre], axis=1).astype(BF)
    dgh = jnp.concatenate([drpre, dupre, dnpre * r], axis=1).astype(BF)
    dm = dot(dgi, wi, 1, 1).astype(BF)
    dh = g * u + dot(dgh, wh, 1, 1)
    return dgi, dgh, dm, dh


class Net:
    def __init__(self, send_sems, recv_sems):
        self.send_sems, self.recv_sems = send_sems, recv_sems
        self.slots, self.sent, self.settled = {}, [], 0

    def slot(self, key):
        return self.slots.setdefault(key, len(self.slots))

    def send(self, key, src, dst, peer):
        copy = pltpu.make_async_remote_copy(
            src_ref=src,
            dst_ref=dst,
            send_sem=self.send_sems.at[len(self.sent)],
            recv_sem=self.recv_sems.at[self.slot(key)],
            device_id=peer,
            device_id_type=pl.DeviceIdType.MESH,
        )
        copy.start()
        self.sent.append(copy)

    def wait(self, key, region, peer):
        pltpu.make_async_remote_copy(
            src_ref=region,
            dst_ref=region,
            send_sem=self.send_sems.at[0],
            recv_sem=self.recv_sems.at[self.slot(key)],
            device_id=peer,
            device_id_type=pl.DeviceIdType.MESH,
        ).wait_recv()

    def drain(self):
        self.settle(len(self.sent))

    def settle(self, count):
        for copy in self.sent[self.settled : count]:
            copy.wait_send()
        self.settled = max(self.settled, count)


class Place:
    def __init__(self, parts):
        self.parts, self.plane = parts, PLANE
        self.lines = parts // PLANE
        self.s, self.c = lax.axis_index("section"), lax.axis_index("dp")
        self.sibling = {"section": 1 - self.s}

    def flip(self, mask):
        at, bit = self.c, 1
        while bit <= mask:
            if mask & bit:
                at = at + bit * (1 - 2 * lax.rem(lax.div(self.c, bit), 2))
            bit *= 2
        return at

    def peer(self, mask):
        return {"dp": self.flip(mask)}

    def block(self, mask):
        return self.s * self.parts + self.flip(mask)

    def spot(self, line):
        return self.s * self.lines + lax.div(self.flip(line * self.plane), self.plane)

    def level(self, line):
        own = lax.div(self.flip(line * self.plane), self.plane) * self.plane
        return self.s * self.parts + own


class LineGather:
    def __init__(self, net, place, name, buf):
        self.net, self.place, self.name, self.buf = net, place, name, buf

    def block(self, line):
        return self.buf.at[self.place.spot(line)]

    def begin(self):
        p = self.place
        for line in range(1, p.lines):
            ref = self.block(0)
            self.net.send((self.name, line), ref, ref, p.peer(line * PLANE))

    def middle(self):
        p = self.place
        for line in range(1, p.lines):
            self.net.wait((self.name, line), self.block(line), p.peer(line * PLANE))
        ref = self.buf.at[pl.ds(p.s * p.lines, p.lines)]
        self.net.send((self.name, "sib"), ref, ref, p.sibling)

    def finish(self):
        p = self.place
        ref = self.buf.at[pl.ds((1 - p.s) * p.lines, p.lines)]
        self.net.wait((self.name, "sib"), ref, p.sibling)


def main_kernel(
    x_ref, f_ref, src_ref, tgt_ref, val_ref, lab_ref, w1_ref, b1_ref, w2_hbm, b2_ref,
    wi_ref, bi_ref, wh_ref, bh_ref, cot_ref,
    full_out, states_out, grads_out, w1_out,
    w2, amat, acc, zaug, zpre_s, hs, hsl, dms, dml, dzacc, picks, puts,
    ins, hid, dts, qst, zall, part, sums, tmp, small, small_in, small_lo, small_line, small_plane,
    w1_io, swap, w2_sems, send_sems, recv_sems,
):
    edges, nodes = f_ref.shape[2], x_ref.shape[1]
    tiles5 = edges // LANE
    parts = full_out.shape[0] // 2
    blocks = 2 * parts
    per = LANE // blocks
    place = Place(parts)
    net = Net(send_sems, recv_sems)
    s, c = place.s, place.c
    me = place.block(0)
    here = place.spot(0)
    group = 2 * place.lines
    rounds = LANE // ROUND

    barrier = pltpu.get_barrier_semaphore()
    peers = [place.peer(q) for q in range(1, PLANE)]
    peers += [place.peer(line * PLANE) for line in range(1, place.lines)] + [place.sibling]
    for peer in peers:
        pl.semaphore_signal(
            barrier, inc=1, device_id=peer, device_id_type=pl.DeviceIdType.MESH
        )

    def w2_copy(ib):
        part = aligned(ib, ROUND * LANE)
        return pltpu.make_async_copy(w2_hbm.at[:, part], w2.at[:, part], w2_sems.at[ib])

    for ib in range(rounds):
        w2_copy(ib).start()

    feats = f_ref[s]
    ends = pack_ends(src_ref, tgt_ref, val_ref, lab_ref, s)
    h0 = x_ref[s]
    for e in range(tiles5):
        ins[here, e * 16 : (e + 1) * 16, :] = feats[:, e * LANE : (e + 1) * LANE]
    table = [ends[q : q + 1, e * LANE : (e + 1) * LANE] for q in range(2) for e in range(tiles5)]
    table.append(ends[2:3, :nodes])
    table.append(jnp.zeros((16 - len(table), LANE), F32))
    ins[here, tiles5 * 16 : (tiles5 + 1) * 16, :] = jnp.concatenate(table, axis=0).astype(BF)
    hid[0, here] = h0
    pick, put = edge_tables(ends, nodes)
    picks[...] = pick
    puts[...] = put
    zpre = edge_hidden(feats, w1_ref[...], b1_ref[...])
    zpre_s[...] = zpre
    zaug[0:LANE] = jax.nn.silu(zpre).astype(BF)
    zaug[LANE : 2 * LANE] = jnp.ones((LANE, edges), BF)

    def sources(t, h):
        got = dot(h, picks[...], 0, 0)
        hs[t] = got
        hsl[:, t * edges : (t + 1) * edges] = got.astype(BF)

    sources(0, h0)
    lane = lax.broadcasted_iota(jnp.int32, (LANE, LANE), 1)
    b2t = b2_ref[...].T
    tiles = [(e, min(256, edges - e)) for e in range(0, edges, 256)]

    gather_in = LineGather(net, place, "in", ins)
    gather_h0 = LineGather(net, place, "h0", hid.at[0])
    gather_h1 = LineGather(net, place, "h1", hid.at[1])
    gather_d2 = LineGather(net, place, "d2", dts.at[1])
    gather_d1 = LineGather(net, place, "d1", dts.at[0])

    def keep(i, e, w, p):
        p = p.reshape(16, 8, w).sum(0)
        for o in range(0, w, LANE):
            acc[(e + o) // LANE, aligned(i, 8), :] = p[:, o : o + LANE]

    def first(ib):
        w2_copy(ib).wait()
        lhs = []
        for v in range(ROUND):
            i = ib * ROUND + v
            bias = jnp.where(lane == i, b2t, jnp.zeros_like(b2t))
            lhs.append(jnp.concatenate([w2[:, aligned(i, LANE)].T, bias], axis=1))
        lhs = jnp.concatenate(lhs, axis=0)
        for e, w in tiles:
            a = dot(lhs, zaug[:, e : e + w]).astype(BF)
            amat[aligned(ib, ROUND * LANE), e : e + w] = a
            for v in range(ROUND):
                p = a[v * LANE : (v + 1) * LANE].astype(F32) * hs[0, :, e : e + w]
                keep(ib * ROUND + v, e, w, p)

    loop(rounds // 2, first)
    pl.semaphore_wait(barrier, len(peers))
    gather_in.begin()
    gather_h0.begin()
    loop(rounds - rounds // 2, lambda ib: first(ib + rounds // 2))

    def again(ib):
        for e, w in tiles:
            for v in range(8):
                a = amat[aligned(ib * 8 + v, LANE), e : e + w]
                keep(ib * 8 + v, e, w, a.astype(F32) * hs[1, :, e : e + w])

    def gathered():
        msg = []
        for e in range(tiles5):
            part = acc[e, pl.ds(0, LANE, stride=8), :]
            for q in range(1, 8):
                part = part + acc[e, pl.ds(q, LANE, stride=8), :]
            msg.append(part)
        msg = jnp.concatenate(msg, axis=1)
        total = jnp.zeros((nodes, LANE), F32)
        for piece in split(msg, 3):
            total = total + dot(puts[...], piece, 1, 1)
        return total.astype(BF)

    weights = (wi_ref[...], bi_ref[...].reshape(1, -1), wh_ref[...], bh_ref[...].reshape(1, -1))
    m1 = gathered()
    gates1 = gru_forward(m1, h0, *weights)
    h1 = gates1[0].astype(BF)
    hid[1, here] = h1
    gather_h1.begin()
    sources(1, h1)
    loop(LANE // 8, again)
    m2 = gathered()
    gates2 = gru_forward(m2, h1, *weights)
    h2 = gates2[0]
    label = jnp.broadcast_to(ends[2:3, :nodes], (LANE, nodes)).T
    g2 = cot_ref[s] * label
    dgi2, dgh2, dm2, dh2 = gru_backward(g2, h1, gates2, weights[0], weights[2])
    dt2 = dm2.T
    dts[1, here] = dt2
    gather_d2.begin()

    def spread(t, dt):
        got = dot(dt, puts[...])
        dms[t] = got
        dml[:, t * edges : (t + 1) * edges] = got.astype(BF)

    def to_source_tile(t, e):
        def body(ib, total):
            d = dms[t, aligned(ib, 8), e * LANE : (e + 1) * LANE]
            for v in range(8):
                a = amat[aligned(ib * 8 + v, LANE), e * LANE : (e + 1) * LANE].astype(F32)
                total = total + a * d[v : v + 1]
            return total

        return lax.fori_loop(0, LANE // 8, body, jnp.zeros((LANE, LANE), F32))

    def to_nodes(outs):
        back = jnp.concatenate(outs, axis=1)
        total = jnp.zeros((nodes, LANE), F32)
        for piece in split(back, 3):
            total = total + dot(picks[...], piece, 1, 1)
        return total

    spread(1, dt2)
    back2 = [to_source_tile(1, e) for e in range(tiles5)]
    gather_in.middle()
    gather_h0.middle()
    gather_h1.middle()
    d1 = (dh2 + to_nodes(back2)).astype(BF)
    dgi1, dgh1, dm1, dh1 = gru_backward(d1.astype(F32), h0, gates1, weights[0], weights[2])
    dt1 = dm1.T
    dts[0, here] = dt1
    gather_d1.begin()
    gather_d2.middle()

    gather_in.finish()
    gather_h0.finish()
    gather_h1.finish()
    dzacc[...] = jnp.zeros_like(dzacc)

    def back_hidden(ib):
        total = dzacc[...]
        for a in range(2):
            d = [dms[t, aligned(ib * 2 + a, 8), :] for t in range(2)]
            for v in range(8):
                both = hs[0] * d[0][v : v + 1] + hs[1] * d[1][v : v + 1]
                qst[a, v * LANE : (v + 1) * LANE, 0:edges] = both.astype(BF)
            total = total + dot(w2[:, aligned(ib * 2 + a, 8 * LANE)], qst[a, :, 0:edges])
        dzacc[...] = total

    units = PLANE * per
    ks = lax.broadcasted_iota(jnp.int32, (units, LANE), 0)
    ks = (lax.div(ks, per) * 2 + s) * per + lax.rem(ks, per) + lax.div(c, PLANE) * (2 * units)
    sel = (ks == lax.broadcasted_iota(jnp.int32, (units, LANE), 1)).astype(F32)
    w1t = dot(sel.astype(BF), w1_ref[...], 1, 1).astype(BF)
    b1 = jnp.sum(sel * b1_ref[...].astype(F32), axis=1, keepdims=True)
    quarter = nodes // 4
    qn = lax.broadcasted_iota(jnp.int32, (quarter, 256), 0).astype(F32)
    sn = lax.broadcasted_iota(jnp.int32, (nodes, 256), 0).astype(F32)

    def hidden(blk):
        cols = [ins[blk, e * 16 : (e + 1) * 16, :] for e in range(tiles5)]
        z = jax.nn.silu(dot(w1t, jnp.concatenate(cols, axis=1)) + b1)
        zall[blk] = z.astype(BF).astype(F32)

    def build(blk):
        z = zall[blk]
        en = ins[blk, tiles5 * 16 : (tiles5 + 1) * 16, :].astype(F32)
        pairs = []
        for q in range(4):
            lo = q * LANE
            zq = z[:, lo : lo + 256]
            src = jnp.concatenate([en[q : q + 1], en[q + 1 : q + 2]], axis=1)
            tgt = jnp.concatenate(
                [en[tiles5 + q : tiles5 + q + 1], en[tiles5 + q + 1 : tiles5 + q + 2]], axis=1
            )
            hit_t = (qn + float(q * quarter)) == tgt
            hit_s = (sn == src).astype(F32).astype(BF)
            lhs = [jnp.where(hit_t, zq[k : k + 1], 0.0).astype(BF) for k in range(units)]
            pairs.append(dot(jnp.concatenate(lhs, axis=0), hit_s, 1, 1))
        pairs = jnp.concatenate(split(jnp.concatenate(pairs, axis=0), 2), axis=1)
        h = jnp.concatenate([hid[0, blk], hid[1, blk]], axis=1)
        got = dot(pairs, jnp.concatenate([h, h], axis=0)).astype(BF)
        for q in range(4):
            at = pl.ds(pl.multiple_of(blk * nodes + q * quarter, quarter), quarter)
            for k in range(units):
                part = got[(q * units + k) * quarter : (q * units + k + 1) * quarter]
                for t in range(2):
                    qst[t, at, k * LANE : (k + 1) * LANE] = part[:, t * LANE : (t + 1) * LANE]

    for blk in range(group):
        hidden(blk)

    def build_pair(b):
        build(2 * b)
        build(2 * b + 1)

    loop(group // 2, build_pair)
    gather_d1.middle()
    gather_d2.finish()
    lhs = jnp.concatenate([dts[1, blk] for blk in range(group)], axis=1)
    part[...] = dot(lhs, qst[1])
    count = jnp.zeros((1, LANE), F32)
    for blk in range(group):
        count = count + ins[blk, tiles5 * 16 : (tiles5 + 1) * 16, :].astype(F32)[10:11]
    count = jnp.concatenate([count, jnp.zeros((15, LANE), F32)], axis=0).astype(BF)
    mid = per * LANE // 2
    early = len(net.sent)
    pieces = (pl.ds(0, 16 + mid), pl.ds(16 + mid, per * LANE - mid))

    def send_sums(ch, q):
        ref = sums.at[0, lax.rem(place.flip(q), PLANE), pieces[ch]]
        net.send(("sums", ch, q), ref, sums.at[1, q, pieces[ch]], place.peer(q))

    def add_sums(ch):
        total = sums[0, q_me, pieces[ch], :].astype(F32)
        for q in range(1, PLANE):
            net.wait(("sums", ch, q), sums.at[1, q, pieces[ch]], place.peer(q))
            total = total + sums[1, q, pieces[ch], :].astype(F32)
        return total

    gather_d1.finish()
    lhs = jnp.concatenate([dts[0, blk] for blk in range(group)], axis=1)
    for q in (3, 1, 2, 0):
        to = lax.rem(place.flip(q), PLANE)
        cols = aligned(to, per * LANE)
        got = part[:, cols] + dot(lhs, qst[0, :, cols])
        for k in range(per):
            tmp[q, pl.ds(k, LANE, stride=per), :] = got[:, k * LANE : (k + 1) * LANE]
        sums[0, to, 0:16] = count
        sums[0, to, 16:] = tmp[q].astype(BF)
        if q:
            send_sums(0, q)
    for q in (3, 1, 2):
        send_sums(1, q)

    half = SMALL_ROWS // 2
    plane_rows = half // place.lines
    own_rows = plane_rows // PLANE
    gwi = dot(m1, dgi1, 0, 0) + dot(m2, dgi2, 0, 0)
    gwh = dot(h0, dgh1, 0, 0) + dot(h1, dgh2, 0, 0)
    for q in range(3):
        small[q * LANE : (q + 1) * LANE] = gwi[:, q * LANE : (q + 1) * LANE]
        small[(3 + q) * LANE : (4 + q) * LANE] = gwh[:, q * LANE : (q + 1) * LANE]
    spread(0, dt1)
    small[6 * LANE : 7 * LANE] = dot(dml[...], hsl[...], 1, 1)
    gbi = dgi1.astype(F32).sum(0, keepdims=True) + dgi2.astype(F32).sum(0, keepdims=True)
    gbh = dgh1.astype(F32).sum(0, keepdims=True) + dgh2.astype(F32).sum(0, keepdims=True)
    rows = [x[:, q * LANE : (q + 1) * LANE] for x in (gbi, gbh) for q in range(3)]
    rows.append(jnp.zeros((SMALL_ROWS - 7 * LANE - 6, LANE), F32))
    small[7 * LANE :] = jnp.concatenate(rows, axis=0)
    net.send(("small", "sib"), small.at[aligned(1 - s, half)], small_in, place.sibling)

    q_me = lax.rem(c, PLANE)
    back1 = [to_source_tile(0, e) for e in range(2)]
    net.wait(("small", "sib"), small_in, place.sibling)
    small_lo[...] = (small[aligned(s, half), :] + small_in[...]).astype(BF)
    z = lax.div(c, PLANE)
    for line in range(1, place.lines):
        to = lax.div(place.flip(line * PLANE), PLANE)
        net.send(
            ("small", "line", line),
            small_lo.at[aligned(to, plane_rows)],
            small_line.at[line],
            place.peer(line * PLANE),
        )

    size = full_out.shape[1]
    tail = size // 8 // 16 * 16
    top = size - tail
    cut = (mid // 32 * 16, mid + (top - mid) // 32 * 16)
    halves = (
        (pl.ds(0, cut[0]), pl.ds(cut[0], mid - cut[0])),
        (pl.ds(mid, cut[1] - mid), pl.ds(cut[1], top - cut[1])),
    )
    chunk = (pl.ds(0, mid), pl.ds(mid, top - mid))
    last = pl.ds(top, tail)

    def out_begin(ch):
        def along(line):
            ref = full_out.at[me, chunk[ch]]
            net.send(("out", ch, line), ref, ref, place.peer(line * PLANE))

        along(1)
        for q in (1, 2):
            ref = full_out.at[me, chunk[ch]]
            net.send(("out", ch, 0, q), ref, ref, place.peer(q))
        for line in range(2, place.lines):
            along(line)

    def out_line(ch, line):
        mask = line * PLANE
        blk = place.block(mask)
        net.wait(("out", ch, line), full_out.at[blk, chunk[ch]], place.peer(mask))
        for q in (1, 2):
            ref = full_out.at[blk, chunk[ch]]
            net.send(("out", ch, line, q), ref, ref, place.peer(q))

    def out_cross(ch, line):
        for q, a in ((1, 0), (2, 1)):
            blk = place.block(line * PLANE + q)
            net.wait(("out", ch, line, q), full_out.at[blk, chunk[ch]], place.peer(q))
            ref = full_out.at[blk, halves[ch][a]]
            net.send(("out", ch, line, 3, a), ref, ref, place.peer(3 - q))

    def last_planes():
        for q in range(1, PLANE):
            ref = full_out.at[me, last]
            net.send(("last", 0, q), ref, ref, place.peer(q))

    def last_lines():
        for q in range(1, PLANE):
            net.wait(("last", 0, q), full_out.at[place.block(q), last], place.peer(q))
        ref = full_out.at[pl.ds(place.level(0), PLANE), last]
        for line in range(1, place.lines):
            net.send(("last", line), ref, ref, place.peer(line * PLANE))

    def out_level(line):
        for ch in range(2):
            for q, a in ((2, 0), (1, 1)):
                ref = full_out.at[place.block(line * PLANE + 3), halves[ch][a]]
                net.wait(("out", ch, line, 3, a), ref, place.peer(q))
        if line > 0:
            part = full_out.at[pl.ds(place.level(line), PLANE), last]
            net.wait(("last", line), part, place.peer(line * PLANE))
        ref = full_out.at[pl.ds(place.level(line), PLANE)]
        net.send(("out", "sib", line), ref, ref, place.sibling)

    net.settle(early)
    total = add_sums(0)
    scale = 1.0 / jnp.sum(total[0:1], axis=1, keepdims=True)
    full_out[me, 0:mid] = (total[16:] * scale).astype(BF)
    out_begin(0)
    back1 += [to_source_tile(0, e) for e in range(2, 4)]
    own = small_lo[aligned(z, plane_rows), :].astype(F32)
    for line in range(1, place.lines):
        net.wait(("small", "line", line), small_line.at[line], place.peer(line * PLANE))
        own = own + small_line[line].astype(F32)
    small_line[0] = own.astype(BF)
    for q in range(1, PLANE):
        to = lax.rem(place.flip(q), PLANE)
        net.send(
            ("small", "plane", q),
            small_line.at[0, aligned(to, own_rows)],
            small_plane.at[q],
            place.peer(q),
        )
    full_out[me, mid : per * LANE] = (add_sums(1) * scale).astype(BF)
    out_begin(1)
    mark = len(net.sent)
    out_cross(0, 0)
    back1 += [to_source_tile(0, e) for e in range(4, tiles5)]
    d0 = dh1 + to_nodes(back1)

    zero = s == 0
    swap[0, 0] = jnp.where(zero, h2, h1.astype(F32))
    swap[0, 1] = jnp.where(zero, d1.astype(F32), d0)
    net.send(("swap",), swap.at[0], swap.at[1], place.sibling)
    own = small_line[0, aligned(q_me, own_rows), :].astype(F32)
    for q in range(1, PLANE):
        net.wait(("small", "plane", q), small_plane.at[q], place.peer(q))
        own = own + small_plane[q].astype(F32)
    full_out[me, per * LANE : per * LANE + own_rows] = (own * scale).astype(BF)
    last_planes()
    out_line(0, 1)
    out_cross(1, 0)
    loop(4, back_hidden)
    for line in range(2, place.lines):
        out_line(0, line)
    out_line(1, 1)
    out_cross(0, 1)
    last_lines()
    loop(3, lambda ib: back_hidden(ib + 4))
    for line in range(2, place.lines):
        out_line(1, line)
    out_cross(1, 1)
    out_cross(0, 2)
    out_level(0)
    mark = len(net.sent)
    loop(LANE // 16 - 7, lambda ib: back_hidden(ib + 7))
    zp = zpre_s[...]
    sig = jax.nn.sigmoid(zp)
    slope = sig * (1.0 + zp * (1.0 - sig))
    lhs = jnp.concatenate(
        [feats, jnp.ones((1, edges), BF), jnp.zeros((15, edges), BF)], axis=0
    )
    total = dot(lhs, (dzacc[...] * slope).astype(BF), 1, 1)
    w1_io[0] = total[0:24]
    net.send(("w1", "sib"), w1_io.at[0], w1_io.at[1], place.sibling)
    for line in range(3, place.lines):
        out_cross(0, line)
    out_cross(1, 2)
    net.wait(("w1", "sib"), w1_io.at[1], place.sibling)
    total = w1_io[0] + w1_io[1]
    w1_io[2] = total
    at = 4
    for line in range(1, place.lines):
        net.send(("w1", "line", line), w1_io.at[2], w1_io.at[at + line], place.peer(line * PLANE))
    net.wait(("swap",), swap.at[1], place.sibling)
    mine_state = jnp.where(zero, h1.astype(F32), h2)
    mine_grad = jnp.where(zero, d0, d1.astype(F32))
    states_out[0] = jnp.where(zero, mine_state, swap[1, 0])
    states_out[1] = jnp.where(zero, swap[1, 0], mine_state)
    grads_out[0] = jnp.where(zero, mine_grad, swap[1, 1])
    grads_out[1] = jnp.where(zero, swap[1, 1], mine_grad)
    for line in range(3, place.lines):
        out_cross(1, line)
    out_level(1)
    for line in range(1, place.lines):
        net.wait(("w1", "line", line), w1_io.at[at + line], place.peer(line * PLANE))
        total = total + w1_io[at + line]
    w1_io[3] = total
    at += place.lines
    for q in range(1, PLANE):
        net.send(("w1", "plane", q), w1_io.at[3], w1_io.at[at + q], place.peer(q))
    net.settle(mark)
    for line in range(2, place.lines):
        out_level(line)
    for q in range(1, PLANE):
        net.wait(("w1", "plane", q), w1_io.at[at + q], place.peer(q))
        total = total + w1_io[at + q]
    w1_out[...] = total * scale
    for line in range(place.lines):
        first = place.level(line) + (1 - 2 * s) * parts
        net.wait(("out", "sib", line), full_out.at[pl.ds(first, PLANE)], place.sibling)
    net.drain()


def final_kernel(full_ref, w1_ref, st_ref, sg_ref, w2_out, b2_out, wi_out, bi_out, wh_out, bh_out,
                 gw1_out, gb1_out, st_out, sg_out, flat, out_sems):
    blocks = full_ref.shape[0]
    parts = blocks // 2
    width = b2_out.shape[0]
    rows = width * (width // blocks)

    def put(c):
        part = aligned(c, 8)
        return pltpu.make_async_copy(flat.at[part], w2_out.at[part], out_sems.at[c])

    gw1_out[...] = w1_ref[0:16]
    gb1_out[...] = w1_ref[16:17]
    st_out[...] = st_ref[...]
    sg_out[...] = sg_ref[...]
    low = lax.broadcasted_iota(jnp.int32, (1, 8, LANE), 1) < 4

    def place_rows(c):
        a = full_ref[c, :rows].astype(F32).reshape(rows // 8, 8, LANE)
        b = full_ref[c + parts, :rows].astype(F32).reshape(rows // 8, 8, LANE)
        even = jnp.where(low, a, pltpu.roll(b, 4, 1))
        odd = jnp.where(low, pltpu.roll(a, 4, 1), b)
        for p in range(rows // 8):
            flat[aligned(c, 8), (2 * p) * LANE : (2 * p + 1) * LANE] = even[p]
            flat[aligned(c, 8), (2 * p + 1) * LANE : (2 * p + 2) * LANE] = odd[p]
        put(c).start()

    loop(parts, place_rows)
    x = full_ref[:, rows:].astype(F32).reshape(-1, LANE)
    for q in range(3):
        cols = slice(q * LANE, (q + 1) * LANE)
        wi_out[:, cols] = x[q * LANE : (q + 1) * LANE]
        wh_out[:, cols] = x[(3 + q) * LANE : (4 + q) * LANE]
        bi_out[cols] = x[7 * LANE + q]
        bh_out[cols] = x[7 * LANE + 3 + q]
    b2_out[...] = x[6 * LANE : 7 * LANE]
    loop(parts, lambda c: put(c).wait())


def shards(
    node_input, edge_input, edge_source, edge_target, edge_valid, node_labeled,
    edge_w1, edge_b1, edge_w2, edge_b2, gru_wi, gru_bi, gru_wh, gru_bh, state_cot,
):
    micro, nodes, width = node_input.shape
    edges = edge_input.shape[2]
    parts = lax.axis_size("dp")
    blocks = 2 * parts
    per = width // blocks
    lines = parts // PLANE
    group, units = 2 * lines, PLANE * per
    half = SMALL_ROWS // 2
    plane_rows = half // lines
    own_rows = plane_rows // PLANE
    size = width * per + own_rows
    vm = pl.BlockSpec(memory_space=VMEM)
    hbm = pl.BlockSpec(memory_space=pl.ANY)
    sds = jax.ShapeDtypeStruct
    full, states, grads, gw1 = pl.pallas_call(
        main_kernel,
        out_shape=(
            VMEM((blocks, size, width), BF), VMEM((2, nodes, width), F32),
            VMEM((2, nodes, width), F32), VMEM((24, width), F32),
        ),
        in_specs=[vm] * 8 + [hbm] + [vm] * 6,
        out_specs=[vm] * 4,
        scratch_shapes=[
            VMEM((width, width * width), BF), VMEM((width * width, edges), BF),
            VMEM((edges // LANE, 8 * width, LANE), F32), VMEM((2 * width, edges), BF),
            VMEM((width, edges), F32), VMEM((2, width, edges), F32),
            VMEM((width, 2 * edges), BF), VMEM((2, width, edges), F32),
            VMEM((width, 2 * edges), BF),
            VMEM((width, edges), F32), VMEM((nodes, edges), BF), VMEM((nodes, edges), BF),
            VMEM((group, 16 * (edges // LANE + 1), LANE), BF),
            VMEM((2, group, nodes, width), BF), VMEM((2, group, width, nodes), BF),
            VMEM((2, group * nodes, units * width), BF), VMEM((group, units, edges), F32),
            VMEM((width, units * width), F32),
            VMEM((2, PLANE, per * width + 16, width), BF),
            VMEM((PLANE, width * per, width), F32),
            VMEM((SMALL_ROWS, width), F32), VMEM((half, width), F32),
            VMEM((half, width), BF), VMEM((lines, plane_rows, width), BF),
            VMEM((PLANE, own_rows, width), BF), VMEM((4 + lines + PLANE, 24, width), F32),
            VMEM((2, 2, nodes, width), F32),
            pltpu.SemaphoreType.DMA((width // ROUND,)),
            pltpu.SemaphoreType.DMA((SEMS,)), pltpu.SemaphoreType.DMA((SEMS,)),
        ],
        compiler_params=pltpu.CompilerParams(
            collective_id=0, has_side_effects=True, vmem_limit_bytes=57 * 2**20
        ),
    )(
        node_input, edge_input, edge_source, edge_target, edge_valid, node_labeled,
        edge_w1, edge_b1.reshape(1, -1), edge_w2, edge_b2.reshape(width, width),
        gru_wi, gru_bi, gru_wh, gru_bh, state_cot,
    )

    w2, b2, wi, bi, wh, bh, w1, b1, states, grads = pl.pallas_call(
        final_kernel,
        out_shape=(
            sds((width, width * width), F32), sds((width, width), F32),
            sds((width, 3 * width), F32), sds((3 * width,), F32),
            sds((width, 3 * width), F32), sds((3 * width,), F32),
            sds((16, width), F32), sds((1, width), F32),
            sds((2, nodes, width), F32), sds((2, nodes, width), F32),
        ),
        in_specs=[vm] * 4,
        out_specs=[hbm] + [vm] * 9,
        scratch_shapes=[
            VMEM((width, width * width), F32), pltpu.SemaphoreType.DMA((parts,)),
        ],
        compiler_params=pltpu.CompilerParams(vmem_limit_bytes=40 * 2**20),
    )(full, gw1, states, grads)
    return (
        states[None], grads[None], w1, b1.reshape(-1), w2, b2.reshape(-1),
        wi, bi, wh, bh,
    )


EDGE_BLOCK = 128


def passed_along(value, axis, steps):
    count = lax.axis_size(axis)
    leading, last = (max(0, -steps), min(count, count - steps))
    return lax.ppermute(value, axis, [(source, source + steps) for source in range(leading, last)])


def split_blocks(feats, source, target, valid, block):
    count = feats.shape[1] // block
    return (
        feats.reshape(feats.shape[0], count, block).transpose(1, 0, 2),
        source.reshape(count, block),
        target.reshape(count, block),
        valid.reshape(count, block),
    )


def block_front(feats_b, source_b, weights, state_low):
    width = state_low.shape[1]
    zpre = jnp.dot(feats_b.T, weights[0], preferred_element_type=jnp.float32) + weights[1].astype(
        jnp.float32
    )
    z_low = jax.nn.silu(zpre).astype(jnp.bfloat16)
    amat = (
        jnp.dot(z_low, weights[2], preferred_element_type=jnp.float32)
        + weights[3].astype(jnp.float32)
    ).astype(jnp.bfloat16)
    amat = amat.reshape(-1, width, width)
    node_ids = lax.iota(jnp.int32, state_low.shape[0])
    pick = (source_b[:, None] == node_ids[None, :]).astype(jnp.bfloat16)
    h_source = jnp.dot(pick, state_low, preferred_element_type=jnp.float32).astype(jnp.bfloat16)
    return (zpre, z_low, amat, h_source)


def target_table(target_b, valid_b, nodes):
    node_ids = lax.iota(jnp.int32, nodes)
    return ((target_b[:, None] == node_ids[None, :]) & (valid_b[:, None] > 0)).astype(jnp.bfloat16)


def forward_messages(state_low, blocks, weights):
    nodes, width = state_low.shape

    def add(total, pieces):
        feats_b, source_b, target_b, valid_b = pieces
        _, _, amat, h_source = block_front(feats_b, source_b, weights, state_low)
        message = jnp.einsum("eij,ej->ei", amat, h_source, preferred_element_type=jnp.float32)
        message = message * (valid_b > 0).astype(jnp.float32)[:, None]
        return (total + jax.ops.segment_sum(message, target_b, num_segments=nodes), None)

    summed, _ = lax.scan(add, jnp.zeros((nodes, width), jnp.float32), blocks)
    return summed


def gru_gates(gathered_low, state_low, weights):
    width = state_low.shape[1]
    gate_in = jnp.dot(gathered_low, weights[4], preferred_element_type=jnp.float32) + weights[
        5
    ].astype(jnp.float32)
    gate_state = jnp.dot(state_low, weights[6], preferred_element_type=jnp.float32) + weights[
        7
    ].astype(jnp.float32)
    reset = jax.nn.sigmoid(gate_in[:, :width] + gate_state[:, :width])
    update = jax.nn.sigmoid(gate_in[:, width : 2 * width] + gate_state[:, width : 2 * width])
    candidate = jnp.tanh(gate_in[:, 2 * width :] + reset * gate_state[:, 2 * width :])
    fresh = (1.0 - update) * candidate + update * state_low.astype(jnp.float32)
    return (fresh, gate_state, reset, update, candidate)


def backward_step(upstream, state_low, gathered_low, blocks, weights):
    nodes, width = state_low.shape
    fresh, gate_state, reset, update, candidate = gru_gates(gathered_low, state_low, weights)
    state = state_low.astype(jnp.float32)
    d_cand = upstream * (1.0 - update)
    d_update = upstream * (state - candidate)
    d_state = upstream * update
    d_npre = d_cand * (1.0 - candidate * candidate)
    d_upre = d_update * update * (1.0 - update)
    d_rpre = d_npre * gate_state[:, 2 * width :] * reset * (1.0 - reset)
    d_in = jnp.concatenate([d_rpre, d_upre, d_npre], axis=1).astype(jnp.bfloat16)
    d_hid = jnp.concatenate([d_rpre, d_upre, d_npre * reset], axis=1).astype(jnp.bfloat16)
    grad_wi = jnp.dot(gathered_low.T, d_in, preferred_element_type=jnp.float32)
    grad_bi = jnp.sum(d_in.astype(jnp.float32), axis=0)
    grad_wh = jnp.dot(state_low.T, d_hid, preferred_element_type=jnp.float32)
    grad_bh = jnp.sum(d_hid.astype(jnp.float32), axis=0)
    d_state = d_state + jnp.dot(d_hid, weights[6].T, preferred_element_type=jnp.float32)
    d_gathered = jnp.dot(d_in, weights[4].T, preferred_element_type=jnp.float32).astype(
        jnp.bfloat16
    )

    def back_block(carry, pieces):
        d_src, grad_w1, grad_b1, grad_w2, grad_b2 = carry
        feats_b, source_b, target_b, valid_b = pieces
        zpre, z_low, amat, h_source = block_front(feats_b, source_b, weights, state_low)
        put = target_table(target_b, valid_b, nodes)
        d_msg = jnp.dot(put, d_gathered, preferred_element_type=jnp.float32).astype(jnp.bfloat16)
        d_amat = d_msg.astype(jnp.float32)[:, :, None] * h_source.astype(jnp.float32)[:, None, :]
        d_amat = d_amat.reshape(d_amat.shape[0], width * width).astype(jnp.bfloat16)
        grad_w2 = grad_w2 + jnp.dot(z_low.T, d_amat, preferred_element_type=jnp.float32)
        grad_b2 = grad_b2 + jnp.sum(d_amat.astype(jnp.float32), axis=0)
        d_z = jnp.dot(d_amat, weights[2].T, preferred_element_type=jnp.float32)
        sig = jax.nn.sigmoid(zpre)
        d_zpre = (d_z * sig * (1.0 + zpre * (1.0 - sig))).astype(jnp.bfloat16)
        grad_w1 = grad_w1 + jnp.dot(feats_b, d_zpre, preferred_element_type=jnp.float32)
        grad_b1 = grad_b1 + jnp.sum(d_zpre.astype(jnp.float32), axis=0)
        d_source = jnp.einsum("eij,ei->ej", amat, d_msg, preferred_element_type=jnp.float32)
        d_src = d_src + jax.ops.segment_sum(d_source, source_b, num_segments=nodes)
        return ((d_src, grad_w1, grad_b1, grad_w2, grad_b2), None)

    start = (
        jnp.zeros((nodes, width), jnp.float32),
        jnp.zeros(weights[0].shape, jnp.float32),
        jnp.zeros(weights[1].shape, jnp.float32),
        jnp.zeros(weights[2].shape, jnp.float32),
        jnp.zeros(weights[3].shape, jnp.float32),
    )
    ends, _ = lax.scan(back_block, start, blocks)
    d_total = d_state + ends[0]
    return (d_total, (ends[1], ends[2], ends[3], ends[4], grad_wi, grad_bi, grad_wh, grad_bh))


def plain_shards(
    node_input,
    edge_input,
    edge_source,
    edge_target,
    edge_valid,
    node_labeled,
    edge_w1,
    edge_b1,
    edge_w2,
    edge_b2,
    gru_wi,
    gru_bi,
    gru_wh,
    gru_bh,
    state_cot,
):
    weights = (edge_w1, edge_b1, edge_w2, edge_b2, gru_wi, gru_bi, gru_wh, gru_bh)
    micro, nodes, width = node_input.shape
    block = min(EDGE_BLOCK, edge_input.shape[2])
    section_id = lax.axis_index("section")
    first = section_id == 0
    count_local = jnp.sum(node_labeled.astype(jnp.float32))

    def batch_blocks(index):
        feats = lax.dynamic_index_in_dim(edge_input, index, 0, keepdims=False)
        source = lax.dynamic_index_in_dim(edge_source, index, 0, keepdims=False)
        target = lax.dynamic_index_in_dim(edge_target, index, 0, keepdims=False)
        valid = lax.dynamic_index_in_dim(edge_valid, index, 0, keepdims=False)
        return split_blocks(feats, source, target, valid, block)

    received = jnp.zeros((nodes, width), jnp.bfloat16)
    saved = []
    states_out = jnp.zeros((micro, nodes, width), jnp.float32)
    for tick in range(micro + 1):
        batch = tick - section_id
        live = (batch >= 0) & (batch < micro)
        index = jnp.clip(batch, 0, micro - 1)
        state_low = jnp.where(first, node_input[min(tick, micro - 1)], received)
        blocks = batch_blocks(index)
        gathered_low = forward_messages(state_low, blocks, weights).astype(jnp.bfloat16)
        fresh = gru_gates(gathered_low, state_low, weights)[0]
        saved.append((state_low, gathered_low))
        sending = fresh.astype(jnp.bfloat16)
        value = jnp.where(first, sending.astype(jnp.float32), fresh)
        states_out = jnp.where(
            live, lax.dynamic_update_index_in_dim(states_out, value, index, 0), states_out
        )
        if tick < micro:
            received = passed_along(sending, "section", 1)
    grad_received = jnp.zeros((nodes, width), jnp.bfloat16)
    grads_out = jnp.zeros((micro, nodes, width), jnp.float32)
    totals = tuple((jnp.zeros(w.shape, jnp.float32) for w in weights))
    for tick in range(micro + 1):
        batch = micro - tick - section_id
        live = (batch >= 0) & (batch < micro)
        index = jnp.clip(batch, 0, micro - 1)
        state_low, gathered_low = saved[micro - tick]
        labels = lax.dynamic_index_in_dim(node_labeled, index, 0, keepdims=False).astype(
            jnp.float32
        )
        top = lax.dynamic_index_in_dim(state_cot, index, 0, keepdims=False) * labels[:, None]
        upstream = jnp.where(first, grad_received.astype(jnp.float32), top)
        d_total, terms = backward_step(
            upstream, state_low, gathered_low, batch_blocks(index), weights
        )
        totals = tuple((acc + jnp.where(live, term, 0.0) for acc, term in zip(totals, terms)))
        sending = d_total.astype(jnp.bfloat16)
        value = jnp.where(first, d_total, sending.astype(jnp.float32))
        grads_out = jnp.where(
            live, lax.dynamic_update_index_in_dim(grads_out, value, index, 0), grads_out
        )
        if tick < micro:
            grad_received = passed_along(sending, "section", -1)
    count_total = lax.psum(count_local, "dp")
    summed = lax.psum(
        (totals[0], totals[1], totals[2], totals[3], totals[4], totals[5], totals[6], totals[7]),
        ("section", "dp"),
    )
    scaled = [g / count_total for g in summed]
    return (
        states_out[None],
        grads_out[None],
        scaled[0],
        scaled[1],
        scaled[2],
        scaled[3],
        scaled[4],
        scaled[5],
        scaled[6],
        scaled[7],
    )


def solution(mesh):
    placed = (
        P(None, "dp", None), P(None, None, "dp"), P(None, "dp"), P(None, "dp"), P(None, "dp"),
        P(None, "dp"), P(), P(), P(), P(), P(), P(), P(), P(), P(None, "dp", None),
    )
    fits = LANE % (2 * mesh.shape["dp"]) == 0
    return jax.shard_map(
        shards if fits else plain_shards,
        mesh=mesh,
        in_specs=placed,
        out_specs=(P("section", None, "dp", None), P("section", None, "dp", None)) + (P(),) * 8,
        check_vma=False,
    )
```
